256 devices in a mesh: gx: 16 (over y_lo, x, core), gy: 8 (over z), ga: 2 (over y_hi).
Axes of the slice: x: 4, y: 4 (y_hi: 2, y_lo: 2; y = y_hi * 2 + y_lo), z: 8, core: 2. Of those that a mesh axis runs over, the one named last changes fastest.
Arguments:
- field: float32 [64, 512, 1024], P('ga', 'gx', 'gy'), may hold values from -25 to 25
- prev_field: float32 [64, 512, 1024], P('ga', 'gx', 'gy'), may hold values from -25 to 25
- diffusivity: float32 [64, 512, 1024], P('ga', 'gx', 'gy'), may hold values from 0.03 to 0.1
- velocity: float32 [3, 64, 512, 1024], P(None, 'ga', 'gx', 'gy'), may hold values from -0.13 to 0.13
- w_lift: bfloat16 [27, 128], replicated, may hold values from -1.25 to 1.25
- norm_gain: float32 [128], replicated, may hold values from 0.1 to 1.9
- w_conv: bfloat16 [16, 3456, 128], P('gx'), may hold values from -0.109375 to 0.109375
- w_out: bfloat16 [128], replicated, may hold values from -0.5 to 0.5
- tile_count: int32 [2, 16, 8], P('ga', 'gx', 'gy'), may hold values from 1 to 2, as said below
- patch_dest: int32 [2, 16, 8, 2], P('ga', 'gx', 'gy'), may hold values from 0 to 15, as said below
- anchor_x: int32 [2, 16, 8, 2], P('ga', 'gx', 'gy'), may hold values from 0 to 24
- anchor_y: int32 [2, 16, 8, 2], P('ga', 'gx', 'gy'), may hold values from 0 to 124
Outputs:
- new_field: float32 [64, 512, 1024], P('ga', 'gx', 'gy')
- learner_loss: float32 [2, 16, 8], P('ga', 'gx', 'gy')
- dir_lift: float32 [27, 128], replicated
- dir_gain: float32 [128], replicated
- dir_conv: float32 [16, 3456, 128], P('gx')
- dir_out: float32 [128], replicated
The draws below stay inside these ranges and needn't reach their ends.
Inputs may be any that keep to these rules, and one draw needn't show every extreme that they name: `tile_count`: in every line of tiles along x, at least two tiles yield 2 patches. `patch_dest`: among the valid slots of one line of tiles along x, at most 4 go to one learner, and in every line exactly 4 go to some learner; slots beyond a tile's count carry no patch.
All inputs are finite; a program needn't handle non-finite values.
Results may differ from the reference program's by a relative error of at most 0.004.
Values may be sent and summed in bfloat16 or wider, within the bound.
A program may use at most 128 MiB of HBM per device.

```python
import math
import jax
import jax.numpy as jnp
from jax import lax

CX = 32
CY = 128
CZ = 32
C = 128
PX = 8
PY = 4
MAXP = 2
STEPS = 2
PVOX = 1024
NX = 512
NY = 1024
NZ = 64
N_GX = 16
N_GY = 8
N_GA = 2


def amplitude_map(phase_key):
    phases = jax.random.uniform(phase_key, (2,), jnp.float32, 0.0, 2.0 * math.pi)
    places_x = jnp.mod(jnp.arange(NX), CX).astype(jnp.float32)
    places_y = jnp.mod(jnp.arange(NY), CY).astype(jnp.float32)
    wave_x = 0.8 * jnp.sin(2.0 * math.pi * places_x / CX + phases[0])
    wave_y = 0.8 * jnp.sin(2.0 * math.pi * places_y / CY + phases[1])
    return jnp.exp(wave_x[:, None] + wave_y[None, :])


def draw_field(key, part):
    key = jax.random.fold_in(key, 11)
    noise_key, phase_key = jax.random.split(key)
    amplitude = amplitude_map(phase_key)
    base = jnp.clip(jax.random.normal(noise_key, (NZ, NX, NY), jnp.float32), -5.0, 5.0)
    return base * amplitude[None]


def draw_prev_field(key, part):
    key = jax.random.fold_in(key, 23)
    noise_key, phase_key = jax.random.split(key)
    amplitude = amplitude_map(phase_key)
    base = jnp.clip(jax.random.normal(noise_key, (NZ, NX, NY), jnp.float32), -5.0, 5.0)
    return base * amplitude[None]


def patch_plan(key):

    def one_line(line_key):
        perm_key, hottest_key, count_key, spread_key = jax.random.split(line_key, 4)
        ranking = jax.random.permutation(perm_key, N_GX)
        hottest = jax.random.randint(hottest_key, (), 0, N_GX)
        counts = jax.random.randint(count_key, (N_GX,), 1, MAXP + 1)
        counts = counts.at[ranking[0]].set(MAXP).at[ranking[1]].set(MAXP)
        others = (hottest + 1 + jnp.arange(2 * MAXP * (N_GX - 1)) % (N_GX - 1)) % N_GX
        others = jax.random.permutation(spread_key, others)
        ordered = jnp.concatenate([jnp.full((2 * MAXP,), hottest), others[:N_GX * MAXP - 2 * MAXP]])
        targets = jnp.zeros((N_GX, MAXP), jnp.int32).at[ranking].set(ordered.reshape(N_GX, MAXP).astype(jnp.int32))
        return (counts.astype(jnp.int32), targets)
    line_keys = jax.random.split(key, N_GA * N_GY)
    counts, targets = jax.vmap(one_line)(line_keys)
    counts = jnp.transpose(counts.reshape(N_GA, N_GY, N_GX), (0, 2, 1))
    targets = jnp.transpose(targets.reshape(N_GA, N_GY, N_GX, MAXP), (0, 2, 1, 3))
    return (counts, targets)


def draw_tile_count(key, part):
    counts, targets = patch_plan(key)
    return counts


def draw_patch_dest(key, part):
    counts, targets = patch_plan(key)
    return targets


def touch_ends(entries, rng, least, top_value):
    index_at = [jax.random.randint(jax.random.fold_in(rng, axis), (), 0, length) for axis, length in enumerate(entries.shape)]
    longest = entries.shape.index(max(entries.shape))
    next_to = index_at[:longest] + [(index_at[longest] + 1) % entries.shape[longest]] + index_at[longest + 1:]
    return entries.at[tuple(index_at)].set(least).at[tuple(next_to)].set(top_value)


def levels(rng, dims, cuts, low, top_value):
    def one(position, shards_of):
        draws = jax.random.uniform(jax.random.fold_in(jax.random.fold_in(rng, 6), position), (shards_of,), jnp.float32, low / len(cuts), top_value / len(cuts))
        return jnp.repeat(jnp.exp(draws), dims[position] // shards_of).reshape((-1,) + (1,) * (len(dims) - position - 1))

    gain = one(*cuts[0])
    for cut in cuts[1:]:
        gain = gain * one(*cut)
    return gain


def normal_values(stream_key, dims, scale, most, cuts=(), kind=jnp.bfloat16):
    factor_of = levels(stream_key, dims, cuts, -0.22, 0.18) if cuts else 1.0
    array = jax.random.normal(stream_key, dims, jnp.float32) * scale * factor_of
    return jnp.minimum(jnp.maximum(array, -most), most).astype(kind)


def setup_inputs(seed: int = 0) -> dict:
    keys = jax.random.split(jax.random.key(seed), 13)
    field = draw_field(jax.random.fold_in(keys[12], 71), 0)
    prev_field = draw_prev_field(jax.random.fold_in(keys[12], 71), 0)
    diffusivity = jnp.clip(jnp.exp(math.log(0.1) - 1.2039728 * jax.random.uniform(keys[2], (NZ, NX, NY), jnp.float32) ** levels(keys[2], (NZ, NX, NY), ((0, 2), (1, 16), (2, 8)), -0.2, 0.2)), 0.03, 0.1)
    velocity = jnp.clip(jax.random.uniform(keys[3], (3, NZ, NX, NY), jnp.float32, -0.13, 0.13) * levels(keys[3], (3, NZ, NX, NY), ((1, 2), (2, 16), (3, 8)), -0.4, 0.0), -0.13, 0.13)
    w_lift = normal_values(keys[4], (27, C), 27 ** -0.5, 1.25)
    norm_gain = jnp.clip(1.0 + 0.18 * jax.random.normal(keys[5], (C,), jnp.float32), 0.1, 1.9)
    w_conv = normal_values(keys[6], (N_GX, 27 * C, C), (27 * C) ** -0.5, 0.109375, ((0, 16),))
    w_out = normal_values(keys[7], (C,), C ** -0.5, 0.5)
    tile_count = draw_tile_count(jax.random.fold_in(keys[12], 71), 0)
    patch_dest = draw_patch_dest(jax.random.fold_in(keys[12], 71), 0)
    anchor_x = touch_ends(jax.random.randint(keys[10], (N_GA, N_GX, N_GY, MAXP), 0, CX - PX + 1), jax.random.fold_in(keys[10], 1), 0, CX - PX).astype(jnp.int32)
    anchor_y = touch_ends(jax.random.randint(keys[11], (N_GA, N_GX, N_GY, MAXP), 0, CY - PY + 1), jax.random.fold_in(keys[11], 1), 0, CY - PY).astype(jnp.int32)
    return {"field": field, "prev_field": prev_field, "diffusivity": diffusivity, "velocity": velocity, "w_lift": w_lift, "norm_gain": norm_gain, "w_conv": w_conv, "w_out": w_out, "tile_count": tile_count, "patch_dest": patch_dest, "anchor_x": anchor_x, "anchor_y": anchor_y}


def neighbours(volume):
    extent_z, extent_x, extent_y = (volume.shape[0], volume.shape[1], volume.shape[2])
    padded = jnp.pad(volume, ((1, 1), (1, 1), (1, 1), (0, 0)))
    pieces = []
    for shift_z in range(3):
        for shift_x in range(3):
            for shift_y in range(3):
                pieces.append(padded[shift_z:shift_z + extent_z, shift_x:shift_x + extent_x, shift_y:shift_y + extent_y, :])
    return jnp.concatenate(pieces, axis=3).reshape(extent_z * extent_x * extent_y, -1)

def surrogate(params, inputs):
    w_lift, norm_gain, w_conv, w_out = params
    extent_z, extent_x, extent_y = inputs.shape
    lifted = jax.nn.gelu(jnp.dot(neighbours(inputs[..., None]), w_lift, preferred_element_type=jnp.float32)).astype(jnp.bfloat16)
    widened = lax.optimization_barrier(lifted).astype(jnp.float32)
    normed = (widened * lax.rsqrt(lax.optimization_barrier(jnp.mean(widened * widened, axis=1, keepdims=True)) + 1e-06) * norm_gain).astype(jnp.bfloat16)
    mixed = jax.nn.gelu(jnp.dot(neighbours(normed.reshape(extent_z, extent_x, extent_y, -1)), w_conv, preferred_element_type=jnp.float32))
    hidden = (widened + mixed).astype(jnp.bfloat16)
    return jnp.dot(hidden, w_out, preferred_element_type=jnp.float32)

def patch_terms(shared, member_conv, inputs, target, weight):

    def loss_of(shared, member_conv):
        params = (shared[0], shared[1], member_conv, shared[2])
        prediction = surrogate(params, inputs)
        misfit = prediction - target.reshape(-1).astype(jnp.float32)
        return weight * 0.5 * jnp.sum(misfit * misfit)
    patch_loss, pullback = jax.vjp(loss_of, shared, member_conv)
    shared_grad, conv_grad = pullback(jnp.ones((), jnp.float32))
    return (patch_loss, shared_grad, conv_grad)

def pad_field(state):
    sideways = jnp.pad(state, ((0, 0), (1, 1), (1, 1)), mode='wrap')
    return jnp.pad(sideways, ((1, 1), (0, 0), (0, 0)))

def advance(extended, diffusivity, velocity):
    centre = extended[1:-1, 1:-1, 1:-1]
    below = extended[:-2, 1:-1, 1:-1]
    above = extended[2:, 1:-1, 1:-1]
    behind = extended[1:-1, :-2, 1:-1]
    ahead = extended[1:-1, 2:, 1:-1]
    left_side = extended[1:-1, 1:-1, :-2]
    right_side = extended[1:-1, 1:-1, 2:]
    laplace = above + below + (ahead + behind) + (right_side + left_side) - 6.0 * centre
    transport = jnp.maximum(velocity[0], 0.0) * (centre - below) + jnp.minimum(velocity[0], 0.0) * (above - centre)
    transport = transport + (jnp.maximum(velocity[1], 0.0) * (centre - behind) + jnp.minimum(velocity[1], 0.0) * (ahead - centre))
    transport = transport + (jnp.maximum(velocity[2], 0.0) * (centre - left_side) + jnp.minimum(velocity[2], 0.0) * (right_side - centre))
    return centre + diffusivity * laplace - transport

def reference(field, prev_field, diffusivity, velocity, w_lift, norm_gain, w_conv, w_out, tile_count, patch_dest, anchor_x, anchor_y):
    state = field
    for repeat in range(STEPS):
        state = advance(pad_field(state), diffusivity, velocity)
    shared = (w_lift, norm_gain, w_out)
    per_tile = jax.vmap(patch_terms, in_axes=(None, 0, 0, 0, 0))

    def tile_step(running, flat_index):
        shared_run, conv_run = running
        layer = flat_index // (N_GX * N_GY)
        column = flat_index // N_GY % N_GX
        row_index = flat_index % N_GY
        starts_x = anchor_x[layer, column, row_index] + column * CX
        starts_y = anchor_y[layer, column, row_index] + row_index * CY
        members = patch_dest[layer, column, row_index]
        sources = []
        wanted = []
        for slot_index in range(MAXP):
            corner = (layer * CZ, starts_x[slot_index], starts_y[slot_index])
            sources.append(lax.dynamic_slice(prev_field, corner, (CZ, PX, PY)))
            wanted.append(lax.dynamic_slice(field, corner, (CZ, PX, PY)))
        inputs = jnp.stack(sources).astype(jnp.bfloat16)
        targets = jnp.stack(wanted).astype(jnp.bfloat16)
        weights = (jnp.arange(MAXP, dtype=jnp.int32) < tile_count[layer, column, row_index]).astype(jnp.float32)
        losses, shared_grad, conv_grad = per_tile(shared, w_conv[members], inputs, targets, weights)
        shared_run = jax.tree.map(lambda summed, gradient: summed + lax.optimization_barrier(jnp.sum(gradient.astype(jnp.float32), axis=0)), shared_run, shared_grad)
        conv_run = conv_run.at[members].add(conv_grad.astype(jnp.float32))
        return ((shared_run, conv_run), losses)
    initial = (jax.tree.map(lambda weight: jnp.zeros(weight.shape, jnp.float32), shared), jnp.zeros(w_conv.shape, jnp.float32))
    totals, losses = lax.scan(tile_step, initial, jnp.arange(N_GA * N_GX * N_GY, dtype=jnp.int32))
    shared_tot, conv_tot = totals
    param_count = w_lift.size + norm_gain.size + w_conv.size + w_out.size
    squares = jnp.sum(shared_tot[0] * shared_tot[0]) + jnp.sum(shared_tot[1] * shared_tot[1]) + jnp.sum(conv_tot * conv_tot) + jnp.sum(shared_tot[2] * shared_tot[2])
    scale = lax.rsqrt(squares / param_count + 1e-06)
    losses = losses.reshape(N_GA, N_GX, N_GY, MAXP)
    valid = jnp.arange(MAXP, dtype=jnp.int32) < tile_count[..., None]
    learners = jnp.arange(N_GX, dtype=jnp.int32)
    assigned = (patch_dest[..., None] == learners) & valid[..., None]
    loss_sum = lax.optimization_barrier(jnp.sum(jnp.where(assigned, losses[..., None], 0.0), axis=(1, 3)))
    loss_number = lax.optimization_barrier(jnp.sum(assigned.astype(jnp.int32), axis=(1, 3)))
    learner_loss = loss_sum / (PVOX * jnp.maximum(loss_number, 1).astype(jnp.float32))
    learner_loss = jnp.transpose(learner_loss, (0, 2, 1))
    return (state, learner_loss, shared_tot[0] * scale, shared_tot[1] * scale, conv_tot * scale, shared_tot[2] * scale)
```

```python
import functools

import jax
import jax.numpy as jnp
from jax import lax
from jax.experimental import pallas as pl
from jax.experimental.pallas import tpu as pltpu
from jax.sharding import PartitionSpec as P

STEPS = 2
PVOX = 1024
CAP = 4
ROOT = 0.7978845608028654
CUBE = 0.044715
MESH = pl.DeviceIdType.MESH
f32, bf16 = jnp.float32, jnp.bfloat16


def gelu_both(v):
    v2 = v * v
    t = jnp.tanh(ROOT * (v + CUBE * (v * v2)))
    half = 0.5 * (1.0 + t)
    slope = half + 0.5 * v * (1.0 - t * t) * (ROOT * (1.0 + 3.0 * CUBE * v2))
    return v * half, slope


def z_shifted(block, z_ids):
    up = jnp.where(z_ids == 31, 0.0, pltpu.roll(block, 127, 0))
    down = jnp.where(z_ids == 0, 0.0, pltpu.roll(block, 1, 0))
    return up, down


def train_kernel(
    meta, recs, w_lift, gain, w_conv, w_out, conv_out, small_out,
    wf, wb, vp, gp, nt, nu, lifted, slope1, pre2, dh,
):
    f32, bf16 = jnp.float32, jnp.bfloat16
    vp[...] = jnp.zeros_like(vp)
    gp[...] = jnp.zeros_like(gp)
    nt[...] = jnp.zeros_like(nt)
    nu[...] = jnp.zeros_like(nu)
    conv_out[...] = jnp.zeros_like(conv_out)
    small_out[...] = jnp.zeros_like(small_out)
    for q in range(3):
        for r in range(3):
            for p in range(3):
                blk = w_conv[pl.ds(((p * 3 + q) * 3 + r) * 128, 128), :]
                wf[q * 3 + r, pl.ds(p * 128, 128), :] = blk
                wb[q * 3 + r, pl.ds(p * 128, 128), :] = blk.astype(f32).T.astype(bf16)
    z_ids = lax.broadcasted_iota(jnp.int32, (128, 128), 0) % 32
    lane = lax.broadcasted_iota(jnp.int32, (8, 128), 1)
    sub = lax.broadcasted_iota(jnp.int32, (8, 128), 0)
    gain_row = gain[...]
    wo_row = w_out[...].astype(f32)

    def patch(i, carry):
        rec = recs[i].astype(f32)
        u = rec[0:8]
        target = rec[8:16]
        for p in range(3):
            dz = p - 1
            uz = u if dz == 0 else pltpu.roll(u, (-dz) % 128, 1)
            okz = (lane % 32 + dz >= 0) & (lane % 32 + dz < 32)
            for q in range(3):
                dx = q - 1
                ux = uz if dx == 0 else pltpu.roll(uz, (-dx) % 8, 0)
                okx = (sub + dx >= 0) & (sub + dx < 8)
                for r in range(3):
                    dy = r - 1
                    uy = ux if dy == 0 else pltpu.roll(ux, (-32 * dy) % 128, 1)
                    oky = (lane // 32 + dy >= 0) & (lane // 32 + dy < 4)
                    nu[:, p * 9 + q * 3 + r, :] = jnp.where(okz & okx & oky, uy, 0.0)

        def lift(x, c):
            pre = lax.dot_general(
                nu[x].astype(bf16), w_lift[...], (((0,), (0,)), ((), ())), preferred_element_type=f32
            )
            val, slope = gelu_both(pre)
            slope1[x] = slope
            low = val.astype(bf16)
            lifted[x] = low
            wide = low.astype(f32)
            inv = lax.rsqrt(jnp.mean(wide * wide, axis=1, keepdims=True) + 1e-06)
            normed = (wide * inv * gain_row).astype(bf16).astype(f32)
            up, down = z_shifted(normed, z_ids)
            for k, v in enumerate((down, normed, up)):
                vp[x + 1, 1:5, :, k * 128 : (k + 1) * 128] = v.astype(bf16).reshape(4, 32, 128)
            nt[x + 1] = normed.T.astype(bf16)
            return c

        lax.fori_loop(0, 8, lift, 0)
        acc = None
        for q in range(3):
            for r in range(3):
                lhs = vp[q : q + 8, r : r + 4].reshape(1024, 384)
                d = jnp.dot(lhs, wf[q * 3 + r], preferred_element_type=f32)
                acc = d if acc is None else acc + d
        pre2[...] = acc

        def out_step(x, c):
            loss, dwo = c
            mixed, slope = gelu_both(pre2[pl.ds(x * 128, 128), :])
            hid = (lifted[x].astype(f32) + mixed).astype(bf16).astype(f32)
            pred = jnp.sum(hid * wo_row, axis=1, keepdims=True)
            row = jnp.sum(jnp.where(sub == x, target, 0.0), axis=0, keepdims=True)
            wanted = jnp.broadcast_to(row, (128, 128)).T
            misfit = pred - wanted
            loss = loss + jnp.sum(misfit * misfit, axis=0, keepdims=True)
            dwo = dwo + jnp.sum(hid * misfit, axis=0, keepdims=True)
            d_hid = (misfit * wo_row).astype(bf16)
            dh[x] = d_hid
            g = (d_hid.astype(f32) * slope).astype(bf16).astype(f32)
            up, down = z_shifted(g, z_ids)
            for k, v in enumerate((up, g, down)):
                gp[x + 1, 1:5, :, k * 128 : (k + 1) * 128] = v.astype(bf16).reshape(4, 32, 128)
            return loss, dwo

        zero_row = jnp.zeros((1, 128), f32)
        loss, dwo = lax.fori_loop(0, 8, out_step, (zero_row, zero_row))
        lhs = jnp.concatenate(
            [jnp.concatenate([nt[q + x] for x in range(8)], axis=1) for q in range(3)], axis=0
        )
        for r in range(3):
            rhs = gp[1:9, 2 - r : 6 - r].reshape(1024, 384)
            d = jnp.dot(lhs, rhs, preferred_element_type=f32)
            for q in range(3):
                for p in range(3):
                    rows = pl.ds(((p * 3 + q) * 3 + r) * 128, 128)
                    piece = d[q * 128 : (q + 1) * 128, p * 128 : (p + 1) * 128]
                    conv_out[rows, :] += piece.astype(bf16).astype(f32)
        acc = None
        for q in range(3):
            for r in range(3):
                lhs = gp[2 - q : 10 - q, 2 - r : 6 - r].reshape(1024, 384)
                d = jnp.dot(lhs, wb[q * 3 + r], preferred_element_type=f32)
                acc = d if acc is None else acc + d
        pre2[...] = acc

        def back(x, c):
            dgain, dwl = c
            dn = pre2[pl.ds(x * 128, 128), :].astype(bf16).astype(f32)
            wide = lifted[x].astype(f32)
            inv = lax.rsqrt(jnp.mean(wide * wide, axis=1, keepdims=True) + 1e-06)
            unit = wide * inv
            dgain = dgain + jnp.sum(dn * unit, axis=0, keepdims=True)
            dt = dn * gain_row
            mean = jnp.sum(dt * wide, axis=1, keepdims=True) * (1.0 / 128.0)
            d_low = dh[x].astype(f32) + dt * inv - (inv * inv * inv * mean) * wide
            d_pre = d_low.astype(bf16).astype(f32) * slope1[x]
            dwl = dwl + jnp.dot(nu[x].astype(bf16), d_pre.astype(bf16), preferred_element_type=f32)
            return dgain, dwl

        dgain, dwl = lax.fori_loop(0, 8, back, (zero_row, jnp.zeros((32, 128), f32)))
        small_out[0:32, :] += dwl.astype(bf16).astype(f32)
        small_out[27:28, :] += dgain
        small_out[28:29, :] += dwo.astype(bf16).astype(f32)
        small_out[32:33, :] += jnp.where(lane[0:1] == meta[1 + i, 0], 0.5 * loss, 0.0)
        return carry

    lax.fori_loop(0, meta[0, 0], patch, 0)


def lanes_of(shape):
    return lax.broadcasted_iota(jnp.int32, shape, len(shape) - 1)


def group_partners(n_gy, n_ga):
    gy, ga = lax.axis_index("gy"), lax.axis_index("ga")
    for far in range(1, n_gy * n_ga):
        there = (gy + far % n_gy) % n_gy
        across = (ga + far // n_gy) % n_ga
        yield far, {"gy": there, "ga": across}


def line_partners(n_gx):
    gx = lax.axis_index("gx")
    for far in range(1, n_gx):
        yield far, {"gx": (gx + far) % n_gx}


def meet(n_gx, n_gy, n_ga):
    barrier = pltpu.get_barrier_semaphore()
    for _, device in line_partners(n_gx):
        pl.semaphore_signal(barrier, inc=1, device_id=device, device_id_type=MESH)
    for _, device in group_partners(n_gy, n_ga):
        pl.semaphore_signal(barrier, inc=1, device_id=device, device_id_type=MESH)
    return barrier, n_gx - 1 + n_gy * n_ga - 1


def remote(src, dst, send_sem, recv_sem, device):
    return pltpu.make_async_remote_copy(
        src_ref=src, dst_ref=dst, send_sem=send_sem, recv_sem=recv_sem,
        device_id=device, device_id_type=MESH,
    )


def route_kernel(
    n_gx, n_gy, n_ga,
    count, dest, start_x, start_y, field, prev_field, diffusivity, velocity,
    new_field, batch, meta,
    state, later, prev, diff, speed, load_sem,
    mine, line, sent, group,
    z_in, x_out, x_in, y_out, y_in,
    line_send, line_recv, group_send, group_recv, halo_send, halo_recv,
):
    gx, gy, ga = lax.axis_index("gx"), lax.axis_index("gy"), lax.axis_index("ga")
    barrier, expected = meet(n_gx, n_gy, n_ga)
    size_z, size_x, size_y = prev.shape
    loads = [
        pltpu.make_async_copy(field, state.at[pl.ds(1, size_z)], load_sem.at[0]),
        pltpu.make_async_copy(prev_field, prev, load_sem.at[1]),
        pltpu.make_async_copy(diffusivity, diff, load_sem.at[2]),
        pltpu.make_async_copy(velocity, speed, load_sem.at[3]),
    ]
    for load in loads:
        load.start()
    lane8 = lanes_of((8, 128))
    xi = lax.broadcasted_iota(jnp.int32, (size_x, 128), 0)
    li = lanes_of((size_x, 128))
    row_y = lax.broadcasted_iota(jnp.int32, (128, 128), 0)
    col = lanes_of((128, 128))
    z_mask = (
        lax.broadcasted_iota(jnp.int32, (size_z, 8, 128), 0) == lanes_of((size_z, 8, 128)) % size_z
    )
    zero_tile = jnp.zeros((size_x, 128), f32)

    def pack_faces(step, cells, high, low):
        x_out[step, 0] = cells[1 : size_z + 1, 0, :]
        x_out[step, 1] = cells[1 : size_z + 1, size_x - 1, :]
        y_out[step, 0] = low
        y_out[step, 1] = high

    def halo_copies(step, cells):
        base = step * 5
        z_src = cells.at[size_z - (size_z - 1) * ga]
        there = {"ga": 1 - ga}
        z_out_copy = remote(
            z_src, z_in.at[step], halo_send.at[base], halo_recv.at[base], there
        )
        copies = [z_out_copy]
        for side in range(2):
            near = (gx + (n_gx - 1 if side == 0 else 1)) % n_gx
            copies.append(remote(
                x_out.at[step, side], x_in.at[step, 1 - side],
                halo_send.at[base + 1 + side], halo_recv.at[base + 1 + side], {"gx": near},
            ))
        for side in range(2):
            near = (gy + (n_gy - 1 if side == 0 else 1)) % n_gy
            copies.append(remote(
                y_out.at[step, side], y_in.at[step, 1 - side],
                halo_send.at[base + 3 + side], halo_recv.at[base + 3 + side], {"gy": near},
            ))
        return copies

    def place(z, cells, high, low):
        high = jnp.where(li == z, pltpu.roll(cells, z + 1, 1), high)
        low = jnp.where(li == z, pltpu.roll(cells, z, 1), low)
        return high, low

    def advance(step, cells, store, pack):
        z_face = z_in[step]
        cells[0] = jnp.where(ga == 1, z_face, 0.0)
        cells[size_z + 1] = jnp.where(ga == 0, z_face, 0.0)

        def layer(z, faces):
            centre = cells[z + 1]
            below = cells[z]
            above = cells[z + 2]
            behind = jnp.where(xi == 0, x_in[step, 0, pl.ds(z, 1), :], pltpu.roll(centre, 1, 0))
            ahead = jnp.where(
                xi == size_x - 1, x_in[step, 1, pl.ds(z, 1), :], pltpu.roll(centre, size_x - 1, 0)
            )
            left = jnp.where(
                li == 0, pltpu.roll(y_in[step, 0], 128 - z, 1), pltpu.roll(centre, 1, 1)
            )
            right = jnp.where(
                li == 127, pltpu.roll(y_in[step, 1], 127 - z, 1), pltpu.roll(centre, 127, 1)
            )
            laplace = above + below + (ahead + behind) + (right + left) - 6.0 * centre
            moved = jnp.zeros_like(centre)
            for d, (low, high) in enumerate(((below, above), (behind, ahead), (left, right))):
                v = speed[d, z]
                moved = moved + (
                    jnp.maximum(v, 0.0) * (centre - low) + jnp.minimum(v, 0.0) * (high - centre)
                )
            result = centre + diff[z] * laplace - moved
            store(z, result)
            return place(z, result, *faces) if pack else faces

        return lax.fori_loop(0, size_z, layer, (zero_tile, zero_tile))

    loads[0].wait()
    high, low = lax.fori_loop(
        0, size_z, lambda z, faces: place(z, state[z + 1], *faces), (zero_tile, zero_tile)
    )
    pack_faces(0, state, high, low)
    loads[1].wait()
    for k in range(2):
        chosen = (row_y == start_y[k] + col // size_z).astype(bf16)
        parts = []
        for source in (0, 1):
            if source == 0:
                window = prev[:, pl.ds(start_x[k], 8), :]
            else:
                window = state[1 : size_z + 1, pl.ds(start_x[k], 8), :]
            spread = jnp.dot(
                window.reshape(size_z * 8, 128).astype(bf16), chosen, preferred_element_type=f32
            ).reshape(size_z, 8, 128)
            parts.append(jnp.sum(jnp.where(z_mask, spread, 0.0), axis=0))
        mine[pl.ds(16 * k, 16), :] = jnp.concatenate(parts, axis=0).astype(bf16)
    goals = [jnp.where(k < count[0], dest[k], -1).astype(f32) for k in range(2)]
    mine[32:48, :] = jnp.concatenate(
        [jnp.full((8, 128), goals[0]), jnp.full((8, 128), goals[1])], axis=0
    ).astype(bf16)
    line[gx] = mine[...]

    pl.semaphore_wait(barrier, expected)
    first = []
    for far, device in line_partners(n_gx):
        copy = remote(mine, line.at[gx], line_send.at[far], line_recv.at[far], device)
        copy.start()
        first.append(copy)
    halos = halo_copies(0, state)
    for copy in halos:
        copy.start()

    for copy in first:
        copy.wait_recv()
    empty = jnp.zeros((16, 128), f32)
    myself = gx.astype(f32)

    def from_line(source, carry):
        rank, picked = carry
        for k in range(2):
            goal = line[source, 32:48, :].astype(f32)[8 * k : 8 * k + 8]
            record = line[source, pl.ds(16 * k, 16), :].astype(f32)
            hit = goal == myself
            picked = tuple(
                jnp.where(jnp.concatenate([hit & (rank == c)] * 2, axis=0), record, old)
                for c, old in enumerate(picked)
            )
            rank = rank + hit.astype(f32)
        return rank, picked

    rank, picked = lax.fori_loop(
        0, n_gx, from_line, (jnp.zeros((8, 128), f32), (empty,) * CAP)
    )
    for c in range(CAP):
        sent[pl.ds(16 * c, 16), :] = picked[c].astype(bf16)
    sent[16 * CAP : 16 * CAP + 16, :] = jnp.concatenate([rank, rank], axis=0).astype(bf16)
    line_id = ga * n_gy + gy
    group[line_id] = sent[...]
    second = []
    for far, device in group_partners(n_gy, n_ga):
        copy = remote(sent, group.at[line_id], group_send.at[far], group_recv.at[far], device)
        copy.start()
        second.append(copy)

    loads[2].wait()
    loads[3].wait()
    for copy in halos:
        copy.wait_recv()

    def keep(z, value):
        later[z + 1] = value

    high, low = advance(0, state, keep, True)
    pack_faces(1, later, high, low)
    more = halo_copies(1, later)
    for copy in more:
        copy.start()

    for copy in second:
        copy.wait_recv()
    share = n_gy * n_ga
    place_f = line_id.astype(f32)

    def from_group(source, carry):
        base, picked, lines = carry
        number = group[source, 16 * CAP : 16 * CAP + 16, :].astype(f32)[0:8]
        for c in range(CAP):
            record = group[source, pl.ds(16 * c, 16), :].astype(f32)
            spot = jnp.where(number > c, base + c, -1.0)
            hits = [spot == place_f + share * i for i in range(CAP)]
            picked = tuple(
                jnp.where(jnp.concatenate([hit] * 2, axis=0), record, old)
                for hit, old in zip(hits, picked)
            )
            lines = tuple(jnp.where(hit, source, old) for hit, old in zip(hits, lines))
        return base + number, picked, lines

    none = jnp.zeros((8, 128), jnp.int32)
    total, picked, lines = lax.fori_loop(
        0, share, from_group, (jnp.zeros((8, 128), f32), (empty,) * CAP, (none,) * CAP)
    )
    number = none
    for i in range(CAP):
        batch[i] = picked[i].astype(bf16)
        number = number + (place_f + share * i < total).astype(jnp.int32)
    meta[0:1, :] = number[0:1]
    for i in range(CAP):
        meta[1 + i : 2 + i, :] = lines[i][0:1]
    meta[5:8, :] = rank[0:3].astype(jnp.int32)

    for copy in more:
        copy.wait_recv()

    def emit(z, value):
        new_field[z] = value

    advance(1, later, emit, False)
    for copy in first + second + halos + more:
        copy.wait_send()


def route_call(count, dest, start_x, start_y, field, prev_field, diffusivity, velocity):
    n_gx, n_gy, n_ga = (lax.axis_size(name) for name in ("gx", "gy", "ga"))
    size_z, size_x, size_y = field.shape
    smem = pl.BlockSpec(memory_space=pltpu.SMEM)
    vmem = pl.BlockSpec(memory_space=pltpu.VMEM)
    hbm = pl.BlockSpec(memory_space=pl.ANY)
    share = n_gy * n_ga
    dma = pltpu.SemaphoreType.DMA
    return pl.pallas_call(
        functools.partial(route_kernel, n_gx, n_gy, n_ga),
        out_shape=(
            jax.ShapeDtypeStruct(field.shape, f32),
            jax.ShapeDtypeStruct((CAP, 16, 128), bf16),
            jax.ShapeDtypeStruct((8, 128), jnp.int32),
        ),
        in_specs=[smem] * 4 + [hbm] * 4,
        out_specs=(vmem,) * 3,
        scratch_shapes=[
            pltpu.VMEM((size_z + 2, size_x, size_y), f32),
            pltpu.VMEM((size_z + 2, size_x, size_y), f32),
            pltpu.VMEM((size_z, size_x, size_y), f32),
            pltpu.VMEM((size_z, size_x, size_y), f32),
            pltpu.VMEM((3, size_z, size_x, size_y), f32),
            dma((4,)),
            pltpu.VMEM((48, 128), bf16),
            pltpu.VMEM((n_gx, 48, 128), bf16),
            pltpu.VMEM((16 * CAP + 16, 128), bf16),
            pltpu.VMEM((share, 16 * CAP + 16, 128), bf16),
            pltpu.VMEM((STEPS, size_x, 128), f32),
            pltpu.VMEM((STEPS, 2, size_z, 128), f32),
            pltpu.VMEM((STEPS, 2, size_z, 128), f32),
            pltpu.VMEM((STEPS, 2, size_x, 128), f32),
            pltpu.VMEM((STEPS, 2, size_x, 128), f32),
            dma((n_gx,)),
            dma((n_gx,)),
            dma((share,)),
            dma((share,)),
            dma((STEPS * 5,)),
            dma((STEPS * 5,)),
        ],
        compiler_params=pltpu.CompilerParams(
            collective_id=0, has_side_effects=True, vmem_limit_bytes=32 * 1024 * 1024
        ),
    )(count, dest, start_x, start_y, field, prev_field, diffusivity, velocity)


def train_call(meta, recs, w_lift, gain, w_conv, w_out):
    vm = pl.BlockSpec(memory_space=pltpu.VMEM)
    return pl.pallas_call(
        train_kernel,
        out_shape=(jax.ShapeDtypeStruct((3456, 128), f32), jax.ShapeDtypeStruct((40, 128), f32)),
        in_specs=[pl.BlockSpec(memory_space=pltpu.SMEM)] + [vm] * 5,
        out_specs=(vm, vm),
        scratch_shapes=[
            pltpu.VMEM((9, 384, 128), bf16),
            pltpu.VMEM((9, 384, 128), bf16),
            pltpu.VMEM((10, 6, 32, 384), bf16),
            pltpu.VMEM((10, 6, 32, 384), bf16),
            pltpu.VMEM((10, 128, 128), bf16),
            pltpu.VMEM((8, 32, 128), f32),
            pltpu.VMEM((8, 128, 128), bf16),
            pltpu.VMEM((8, 128, 128), f32),
            pltpu.VMEM((1024, 128), f32),
            pltpu.VMEM((8, 128, 128), bf16),
        ],
        compiler_params=pltpu.CompilerParams(vmem_limit_bytes=40 * 1024 * 1024),
    )(meta, recs, w_lift, gain, w_conv, w_out)


def reduce_kernel(
    n_gx, n_gy, n_ga, rows, padded, entries,
    conv, small, meta,
    total_out, lift_out, gain_out, out_out, scale_out, loss_out,
    ring, other, gathered, pieces, from_line, tile_b, from_group, tile_c, from_all,
    ring_send, ring_recv, pair_send, pair_recv, gather_send, gather_recv,
    a_send, a_recv, b_send, b_recv, c_send, c_recv,
):
    gx, gy, ga = lax.axis_index("gx"), lax.axis_index("gy"), lax.axis_index("ga")
    line_id = ga * n_gy + gy
    barrier, expected = meet(n_gx, n_gy, n_ga)
    steps = n_gy - 1
    cut = (rows // 16) * 8
    subs = ((0, cut), (cut, rows - cut))
    cut16 = (padded // 32) * 16
    subs16 = ((0, cut16), (cut16, padded - cut16))
    signs = (1, -1)
    sub8 = lax.broadcasted_iota(jnp.int32, (8, 128), 0)
    lane8 = lanes_of((8, 128))
    share = n_gy * n_ga
    per = 32 // n_gx

    for k in range(n_gx):
        pieces[k] = jnp.concatenate(
            [small[per * k : per * k + per, :], jnp.zeros((8 - per, 128), f32)], axis=0
        )
    from_line[gx] = pieces[gx]

    def chunk_at(index, side, low, size):
        chunk = (index + 2 * n_gy) % n_gy
        start = pl.multiple_of(chunk * (2 * rows) + side * rows + low, 8)
        return pl.ds(start, size)

    def ring_copy(step, side, part):
        low, size = subs[part]
        if step == 0:
            src = conv.at[chunk_at(gy - signs[side], side, low, size)]
        else:
            src = ring.at[step - 1, side, pl.ds(low, size)]
        return remote(
            src, ring.at[step, side, pl.ds(low, size)],
            ring_send.at[step, side, part], ring_recv.at[step, side, part],
            {"gy": (gy + signs[side] + n_gy) % n_gy},
        )

    waits = []
    order = [(0, 0), (1, 0), (0, 1), (1, 1)]
    pl.semaphore_wait(barrier, expected)
    flying = {}
    for key in order:
        flying[key] = ring_copy(0, *key)
        flying[key].start()
    line_copies = []
    for far, device in line_partners(n_gx):
        copy = remote(
            pieces.at[device["gx"]], from_line.at[gx], a_send.at[far], a_recv.at[far], device
        )
        copy.start()
        line_copies.append(copy)

    for step in range(steps):
        for key in order:
            side, part = key
            low, size = subs[part]
            flying[key].wait_recv()
            waits.append(flying[key])
            mine = chunk_at(gy - signs[side] * (step + 2), side, low, size)
            ring[step, side, pl.ds(low, size), :] += conv[mine, :]
            if step + 1 < steps:
                flying[key] = ring_copy(step + 1, *key)
                flying[key].start()

    across = {"ga": 1 - ga}
    pair = remote(ring.at[steps - 1, 1 - ga], other, pair_send.at[0], pair_recv.at[0], across)
    pair.start()
    for copy in line_copies:
        copy.wait_recv()
    piece = lax.fori_loop(0, n_gx, lambda k, acc: acc + from_line[k], jnp.zeros((8, 128), f32))
    pair.wait_recv()
    total = ring[steps - 1, ga] + other[...]
    squares = jnp.sum(total * total, axis=0, keepdims=True)
    filled = [total] if padded == rows else [total, jnp.zeros((padded - rows, 128), f32)]
    gathered[gy, ga] = jnp.concatenate(filled, axis=0).astype(bf16)
    swap = remote(
        gathered.at[gy, ga], gathered.at[gy, ga], pair_send.at[1], pair_recv.at[1], across
    )
    swap.start()
    toward = 1 - 2 * ga

    def gather_copy(step, stream, part):
        low, size = subs16[part]
        sign = toward if stream == 0 else -toward
        half = ga if stream == 0 else 1 - ga
        chunk = (gy - sign * step + n_gy * 2) % n_gy
        where = gathered.at[chunk, half, pl.ds(low, size)]
        return remote(
            where, where,
            gather_send.at[step, stream, part], gather_recv.at[step, stream, part],
            {"gy": (gy + sign + n_gy) % n_gy},
        )

    for part in range(2):
        flying[0, part] = gather_copy(0, 0, part)
        flying[0, part].start()
    tile_b[...] = jnp.where(
        sub8 < per, piece, jnp.where(sub8 == per, squares, jnp.where(sub8 == per + 1, small[32:33, :], 0.0))
    )
    from_group[line_id] = tile_b[...]
    group_copies = []
    for far, device in group_partners(n_gy, n_ga):
        copy = remote(tile_b, from_group.at[line_id], b_send.at[far], b_recv.at[far], device)
        copy.start()
        group_copies.append(copy)
    swap.wait_recv()
    for part in range(2):
        flying[1, part] = gather_copy(0, 1, part)
        flying[1, part].start()

    def second_stage():
        for copy in group_copies:
            copy.wait_recv()
        summed = lax.fori_loop(
            0, share, lambda k, acc: acc + from_group[k], jnp.zeros((8, 128), f32)
        )
        tile_c[...] = summed
        from_all[gx] = summed
        copies = []
        for far, device in line_partners(n_gx):
            copy = remote(tile_c, from_all.at[gx], c_send.at[far], c_recv.at[far], device)
            copy.start()
            copies.append(copy)
        return summed, copies

    for step in range(steps):
        for stream in range(2):
            for part in range(2):
                copy = flying[stream, part]
                copy.wait_recv()
                waits.append(copy)
                if step + 1 < steps:
                    flying[stream, part] = gather_copy(step + 1, stream, part)
                    flying[stream, part].start()
        if step == min(1, steps - 1):
            summed, last_copies = second_stage()

    for copy in last_copies:
        copy.wait_recv()
    shared = jnp.concatenate([from_all[k, 0:per, :] for k in range(n_gx)], axis=0)
    conv_squares = lax.fori_loop(
        0, n_gx, lambda k, acc: acc + from_all[k], jnp.zeros((8, 128), f32)
    )[per : per + 1]
    all_squares = jnp.sum(
        conv_squares + jnp.sum(shared * shared, axis=0, keepdims=True), axis=1, keepdims=True
    )
    scale = lax.rsqrt(all_squares / entries + 1e-06)
    lift_out[...] = shared[0:27] * scale
    gain_out[...] = shared[27:28] * scale
    out_out[...] = shared[28:29] * scale
    scale_out[...] = jnp.broadcast_to(scale, (1, 128))
    number = jnp.maximum(meta[5:6, :], 1).astype(f32)
    own = jnp.sum(
        jnp.where(lane8[0:1] == line_id, summed[per + 1 : per + 2], 0.0), axis=1, keepdims=True
    )
    loss_out[...] = own / (PVOX * number)
    for chunk in range(n_gy):
        total_out[chunk] = gathered[chunk]
    for copy in waits + line_copies + group_copies + last_copies + [pair, swap]:
        copy.wait_send()


def reduce_call(conv, small, meta, entries):
    n_gx, n_gy, n_ga = (lax.axis_size(name) for name in ("gx", "gy", "ga"))
    share = n_gy * n_ga
    rows = conv.shape[0] // share
    padded = -(-rows // 16) * 16
    steps = n_gy - 1
    vmem = pl.BlockSpec(memory_space=pltpu.VMEM)
    dma = pltpu.SemaphoreType.DMA
    tile = functools.partial(jax.ShapeDtypeStruct, dtype=f32)
    return pl.pallas_call(
        functools.partial(reduce_kernel, n_gx, n_gy, n_ga, rows, padded, entries),
        out_shape=(
            jax.ShapeDtypeStruct((n_gy, n_ga, padded, 128), bf16),
            tile((27, 128)), tile((1, 128)), tile((1, 128)), tile((1, 128)), tile((1, 128)),
        ),
        in_specs=[vmem] * 3,
        out_specs=(vmem,) * 6,
        scratch_shapes=[
            pltpu.VMEM((steps, 2, rows, 128), f32),
            pltpu.VMEM((rows, 128), f32),
            pltpu.VMEM((n_gy, n_ga, padded, 128), bf16),
            pltpu.VMEM((n_gx, 8, 128), f32),
            pltpu.VMEM((n_gx, 8, 128), f32),
            pltpu.VMEM((8, 128), f32),
            pltpu.VMEM((share, 8, 128), f32),
            pltpu.VMEM((8, 128), f32),
            pltpu.VMEM((n_gx, 8, 128), f32),
            dma((steps, 2, 2)), dma((steps, 2, 2)),
            dma((2,)), dma((2,)),
            dma((steps, 2, 2)), dma((steps, 2, 2)),
            dma((n_gx,)), dma((n_gx,)),
            dma((share,)), dma((share,)),
            dma((n_gx,)), dma((n_gx,)),
        ],
        compiler_params=pltpu.CompilerParams(
            collective_id=1, has_side_effects=True, vmem_limit_bytes=32 * 1024 * 1024
        ),
    )(conv, small, meta)


def body(
    field, prev_field, diffusivity, velocity, w_lift, norm_gain, w_conv, w_out,
    tile_count, patch_dest, anchor_x, anchor_y,
):
    new_field, batch, meta = route_call(
        tile_count.reshape(1), patch_dest.reshape(2), anchor_x.reshape(2), anchor_y.reshape(2),
        field, prev_field, diffusivity, velocity,
    )
    lift_rows = jnp.pad(w_lift, ((0, 32 - w_lift.shape[0]), (0, 0)))
    conv, small = train_call(
        meta, batch, lift_rows, norm_gain[None], w_conv[0], w_out[None]
    )
    entries = w_lift.size + norm_gain.size + w_out.size + lax.axis_size("gx") * w_conv[0].size
    total, lift, gain, out, scale, loss = reduce_call(conv, small, meta, entries)
    rows = conv.shape[0] // (total.shape[0] * total.shape[1])
    dir_conv = total[:, :, :rows].astype(f32) * scale[0, 0]
    return (
        new_field, loss[:, :1].reshape(1, 1, 1), lift, gain.reshape(-1),
        dir_conv.reshape(w_conv.shape), out.reshape(-1),
    )


def solution(mesh):
    tiles = P("ga", "gx", "gy")
    slots = P("ga", "gx", "gy", None)
    in_specs = (
        tiles, tiles, tiles, P(None, "ga", "gx", "gy"), P(), P(), P("gx", None, None), P(),
        tiles, slots, slots, slots,
    )
    out_specs = (tiles, tiles, P(), P(), P("gx", None, None), P())
    return jax.shard_map(body, mesh=mesh, in_specs=in_specs, out_specs=out_specs, check_vma=False)
```

```python
import functools

import jax
import jax.numpy as jnp
from jax import lax
from jax.experimental import pallas as pl
from jax.experimental.pallas import tpu as pltpu
from jax.sharding import PartitionSpec as P

STEPS = 2
PVOX = 1024
CAP = 4
ROOT = 0.7978845608028654
CUBE = 0.044715
MESH = pl.DeviceIdType.MESH
f32, bf16 = jnp.float32, jnp.bfloat16


def gelu_both(v):
    v2 = v * v
    t = jnp.tanh(ROOT * (v + CUBE * (v * v2)))
    half = 0.5 * (1.0 + t)
    slope = half + 0.5 * v * (1.0 - t * t) * (ROOT * (1.0 + 3.0 * CUBE * v2))
    return v * half, slope


def z_shifted(block, z_ids):
    up = jnp.where(z_ids == 31, 0.0, pltpu.roll(block, 127, 0))
    down = jnp.where(z_ids == 0, 0.0, pltpu.roll(block, 1, 0))
    return up, down


def steps_of(count, step, carry):
    for x in range(count):
        carry = step(x, carry)
    return carry


def train_kernel(
    meta, recs, w_lift, gain, w_conv, w_out, cells, conv_out, small_out, cells_out,
    wf, wb, vp, gp, nt, nu, lifted, slope1, pre2, dh, pass_sem,
):
    passed = pltpu.make_async_copy(cells, cells_out, pass_sem)
    passed.start()
    f32, bf16 = jnp.float32, jnp.bfloat16
    vp[...] = jnp.zeros_like(vp)
    gp[...] = jnp.zeros_like(gp)
    nt[...] = jnp.zeros_like(nt)
    nu[...] = jnp.zeros_like(nu)
    conv_out[...] = jnp.zeros_like(conv_out)
    small_out[...] = jnp.zeros_like(small_out)
    for q in range(3):
        for r in range(3):
            for p in range(3):
                blk = w_conv[pl.ds(((p * 3 + q) * 3 + r) * 128, 128), :]
                wf[q * 3 + r, pl.ds(p * 128, 128), :] = blk
                wb[q * 3 + r, pl.ds(p * 128, 128), :] = blk.astype(f32).T.astype(bf16)
    z_ids = lax.broadcasted_iota(jnp.int32, (128, 128), 0) % 32
    lane = lax.broadcasted_iota(jnp.int32, (8, 128), 1)
    sub = lax.broadcasted_iota(jnp.int32, (8, 128), 0)
    gain_row = gain[...]
    wo_row = w_out[...].astype(f32)

    def patch(i, carry):
        rec = recs[i].astype(f32)
        u = rec[0:8]
        target = rec[8:16]
        for p in range(3):
            dz = p - 1
            uz = u if dz == 0 else pltpu.roll(u, (-dz) % 128, 1)
            okz = (lane % 32 + dz >= 0) & (lane % 32 + dz < 32)
            for q in range(3):
                dx = q - 1
                ux = uz if dx == 0 else pltpu.roll(uz, (-dx) % 8, 0)
                okx = (sub + dx >= 0) & (sub + dx < 8)
                for r in range(3):
                    dy = r - 1
                    uy = ux if dy == 0 else pltpu.roll(ux, (-32 * dy) % 128, 1)
                    oky = (lane // 32 + dy >= 0) & (lane // 32 + dy < 4)
                    nu[:, p * 9 + q * 3 + r, :] = jnp.where(okz & okx & oky, uy, 0.0)

        def lift(x, c):
            pre = lax.dot_general(
                nu[x].astype(bf16), w_lift[...], (((0,), (0,)), ((), ())), preferred_element_type=f32
            )
            val, slope = gelu_both(pre)
            slope1[x] = slope
            low = val.astype(bf16)
            lifted[x] = low
            wide = low.astype(f32)
            inv = lax.rsqrt(jnp.mean(wide * wide, axis=1, keepdims=True) + 1e-06)
            normed = (wide * inv * gain_row).astype(bf16).astype(f32)
            up, down = z_shifted(normed, z_ids)
            for k, v in enumerate((down, normed, up)):
                vp[x + 1, 1:5, :, k * 128 : (k + 1) * 128] = v.astype(bf16).reshape(4, 32, 128)
            nt[x + 1] = normed.T.astype(bf16)
            return c

        steps_of(8, lift, 0)
        acc = None
        for q in range(3):
            for r in range(3):
                lhs = vp[q : q + 8, r : r + 4].reshape(1024, 384)
                d = jnp.dot(lhs, wf[q * 3 + r], preferred_element_type=f32)
                acc = d if acc is None else acc + d
        pre2[...] = acc

        def out_step(x, c):
            loss, dwo = c
            mixed, slope = gelu_both(pre2[pl.ds(x * 128, 128), :])
            hid = (lifted[x].astype(f32) + mixed).astype(bf16).astype(f32)
            pred = jnp.sum(hid * wo_row, axis=1, keepdims=True)
            row = jnp.sum(jnp.where(sub == x, target, 0.0), axis=0, keepdims=True)
            wanted = jnp.broadcast_to(row, (128, 128)).T
            misfit = pred - wanted
            loss = loss + jnp.sum(misfit * misfit, axis=0, keepdims=True)
            dwo = dwo + jnp.sum(hid * misfit, axis=0, keepdims=True)
            d_hid = (misfit * wo_row).astype(bf16)
            dh[x] = d_hid
            g = (d_hid.astype(f32) * slope).astype(bf16).astype(f32)
            up, down = z_shifted(g, z_ids)
            for k, v in enumerate((up, g, down)):
                gp[x + 1, 1:5, :, k * 128 : (k + 1) * 128] = v.astype(bf16).reshape(4, 32, 128)
            return loss, dwo

        zero_row = jnp.zeros((1, 128), f32)
        loss, dwo = steps_of(8, out_step, (zero_row, zero_row))
        lhs = jnp.concatenate(
            [jnp.concatenate([nt[q + x] for x in range(8)], axis=1) for q in range(3)], axis=0
        )
        for r in range(3):
            rhs = gp[1:9, 2 - r : 6 - r].reshape(1024, 384)
            d = jnp.dot(lhs, rhs, preferred_element_type=f32)
            for q in range(3):
                for p in range(3):
                    rows = pl.ds(((p * 3 + q) * 3 + r) * 128, 128)
                    piece = d[q * 128 : (q + 1) * 128, p * 128 : (p + 1) * 128]
                    conv_out[rows, :] += piece.astype(bf16).astype(f32)
        acc = None
        for q in range(3):
            for r in range(3):
                lhs = gp[2 - q : 10 - q, 2 - r : 6 - r].reshape(1024, 384)
                d = jnp.dot(lhs, wb[q * 3 + r], preferred_element_type=f32)
                acc = d if acc is None else acc + d
        pre2[...] = acc

        def back(x, c):
            dgain, dwl = c
            dn = pre2[pl.ds(x * 128, 128), :].astype(bf16).astype(f32)
            wide = lifted[x].astype(f32)
            inv = lax.rsqrt(jnp.mean(wide * wide, axis=1, keepdims=True) + 1e-06)
            unit = wide * inv
            dgain = dgain + jnp.sum(dn * unit, axis=0, keepdims=True)
            dt = dn * gain_row
            mean = jnp.sum(dt * wide, axis=1, keepdims=True) * (1.0 / 128.0)
            d_low = dh[x].astype(f32) + dt * inv - (inv * inv * inv * mean) * wide
            d_pre = d_low.astype(bf16).astype(f32) * slope1[x]
            dwl = dwl + jnp.dot(nu[x].astype(bf16), d_pre.astype(bf16), preferred_element_type=f32)
            return dgain, dwl

        dgain, dwl = steps_of(8, back, (zero_row, jnp.zeros((32, 128), f32)))
        small_out[0:32, :] += dwl.astype(bf16).astype(f32)
        small_out[27:28, :] += dgain
        small_out[28:29, :] += dwo.astype(bf16).astype(f32)
        small_out[32:33, :] += jnp.where(lane[0:1] == meta[1 + i, 0], 0.5 * loss, 0.0)
        return carry

    lax.fori_loop(0, meta[0, 0], patch, 0)
    passed.wait()


def lanes_of(shape):
    return lax.broadcasted_iota(jnp.int32, shape, len(shape) - 1)


def group_partners(n_gy, n_ga):
    gy, ga = lax.axis_index("gy"), lax.axis_index("ga")
    for far in range(1, n_gy * n_ga):
        there = (gy + far % n_gy) % n_gy
        across = (ga + far // n_gy) % n_ga
        yield far, {"gy": there, "ga": across}


def line_partners(n_gx):
    gx = lax.axis_index("gx")
    for far in range(1, n_gx):
        yield far, {"gx": (gx + far) % n_gx}


def block_partners(n_ga):
    gy, ga = lax.axis_index("gy"), lax.axis_index("ga")
    for far in range(1, 2 * n_ga):
        there = gy + (far % 2) * (1 - 2 * (gy % 2))
        yield far, {"gy": there, "ga": (ga + far // 2) % n_ga}


def meet(devices):
    barrier = pltpu.get_barrier_semaphore()
    for device in devices:
        pl.semaphore_signal(barrier, inc=1, device_id=device, device_id_type=MESH)
    return barrier, len(devices)


def several(count, step, carry, at_once=4):
    def run(block, carry):
        for i in range(at_once):
            carry = step(block * at_once + i, carry)
        return carry

    return lax.fori_loop(0, count // at_once, run, carry)


def remote(src, dst, send_sem, recv_sem, device):
    return pltpu.make_async_remote_copy(
        src_ref=src, dst_ref=dst, send_sem=send_sem, recv_sem=recv_sem,
        device_id=device, device_id_type=MESH,
    )


def route_kernel(
    n_gx, n_gy, n_ga,
    count, dest, start_x, start_y, field, prev_field, diffusivity, velocity,
    new_field, batch, meta,
    state, later, prev, diff, speed, load_sem,
    mine, line, sent, group,
    z_in, x_out, x_in, y_out, y_in,
    line_send, line_recv, group_send, group_recv, halo_send, halo_recv,
):
    gx, gy, ga = lax.axis_index("gx"), lax.axis_index("gy"), lax.axis_index("ga")
    barrier, expected = meet(
        [device for _, device in line_partners(n_gx)]
        + [device for _, device in block_partners(n_ga)]
        + [{"gy": (gy + 1) % n_gy}, {"gy": (gy + n_gy - 1) % n_gy}]
    )
    size_z, size_x, size_y = prev.shape
    loads = [
        pltpu.make_async_copy(field, state.at[pl.ds(1, size_z)], load_sem.at[0]),
        pltpu.make_async_copy(prev_field, prev, load_sem.at[1]),
        pltpu.make_async_copy(diffusivity, diff, load_sem.at[2]),
        pltpu.make_async_copy(velocity, speed, load_sem.at[3]),
    ]
    for load in loads:
        load.start()
    lane8 = lanes_of((8, 128))
    xi = lax.broadcasted_iota(jnp.int32, (size_x, 128), 0)
    li = lanes_of((size_x, 128))
    row_y = lax.broadcasted_iota(jnp.int32, (128, 128), 0)
    col = lanes_of((128, 128))
    z_mask = (
        lax.broadcasted_iota(jnp.int32, (size_z, 8, 128), 0) == lanes_of((size_z, 8, 128)) % size_z
    )
    zero_tile = jnp.zeros((size_x, 128), f32)

    def pack_faces(step, cells, high, low):
        x_out[step, 0] = cells[1 : size_z + 1, 0, :]
        x_out[step, 1] = cells[1 : size_z + 1, size_x - 1, :]
        y_out[step, 0] = low
        y_out[step, 1] = high

    def halo_copies(step, cells):
        base = step * 5
        z_src = cells.at[size_z - (size_z - 1) * ga]
        there = {"ga": 1 - ga}
        z_out_copy = remote(
            z_src, z_in.at[step], halo_send.at[base], halo_recv.at[base], there
        )
        copies = [z_out_copy]
        for side in range(2):
            near = (gx + (n_gx - 1 if side == 0 else 1)) % n_gx
            copies.append(remote(
                x_out.at[step, side], x_in.at[step, 1 - side],
                halo_send.at[base + 1 + side], halo_recv.at[base + 1 + side], {"gx": near},
            ))
        for side in range(2):
            near = (gy + (n_gy - 1 if side == 0 else 1)) % n_gy
            copies.append(remote(
                y_out.at[step, side], y_in.at[step, 1 - side],
                halo_send.at[base + 3 + side], halo_recv.at[base + 3 + side], {"gy": near},
            ))
        return copies

    def place(z, cells, high, low):
        high = jnp.where(li == z, pltpu.roll(cells, z + 1, 1), high)
        low = jnp.where(li == z, pltpu.roll(cells, z, 1), low)
        return high, low

    def advance(step, cells, store, pack):
        z_face = z_in[step]
        cells[0] = jnp.where(ga == 1, z_face, 0.0)
        cells[size_z + 1] = jnp.where(ga == 0, z_face, 0.0)

        def layer(z, faces):
            centre = cells[z + 1]
            below = cells[z]
            above = cells[z + 2]
            behind = jnp.where(xi == 0, x_in[step, 0, pl.ds(z, 1), :], pltpu.roll(centre, 1, 0))
            ahead = jnp.where(
                xi == size_x - 1, x_in[step, 1, pl.ds(z, 1), :], pltpu.roll(centre, size_x - 1, 0)
            )
            left = jnp.where(
                li == 0, pltpu.roll(y_in[step, 0], 128 - z, 1), pltpu.roll(centre, 1, 1)
            )
            right = jnp.where(
                li == 127, pltpu.roll(y_in[step, 1], 127 - z, 1), pltpu.roll(centre, 127, 1)
            )
            laplace = above + below + (ahead + behind) + (right + left) - 6.0 * centre
            moved = jnp.zeros_like(centre)
            for d, (low, high) in enumerate(((below, above), (behind, ahead), (left, right))):
                v = speed[d, z]
                moved = moved + (
                    jnp.maximum(v, 0.0) * (centre - low) + jnp.minimum(v, 0.0) * (high - centre)
                )
            result = centre + diff[z] * laplace - moved
            store(z, result)
            return place(z, result, *faces) if pack else faces

        return several(size_z, layer, (zero_tile, zero_tile))

    loads[0].wait()
    high, low = several(
        size_z, lambda z, faces: place(z, state[z + 1], *faces), (zero_tile, zero_tile)
    )
    pack_faces(0, state, high, low)
    loads[1].wait()
    for k in range(2):
        chosen = (row_y == start_y[k] + col // size_z).astype(bf16)
        parts = []
        for source in (0, 1):
            if source == 0:
                window = prev[:, pl.ds(start_x[k], 8), :]
            else:
                window = state[1 : size_z + 1, pl.ds(start_x[k], 8), :]
            spread = jnp.dot(
                window.reshape(size_z * 8, 128).astype(bf16), chosen, preferred_element_type=f32
            ).reshape(size_z, 8, 128)
            parts.append(jnp.sum(jnp.where(z_mask, spread, 0.0), axis=0))
        mine[pl.ds(16 * k, 16), :] = jnp.concatenate(parts, axis=0).astype(bf16)
    goals = [jnp.where(k < count[0], dest[k], -1).astype(f32) for k in range(2)]
    mine[32:48, :] = jnp.concatenate(
        [jnp.full((8, 128), goals[0]), jnp.full((8, 128), goals[1])], axis=0
    ).astype(bf16)
    line[gx] = mine[...]

    pl.semaphore_wait(barrier, expected)
    first = []
    for far, device in line_partners(n_gx):
        copy = remote(mine, line.at[gx], line_send.at[far], line_recv.at[far], device)
        copy.start()
        first.append(copy)
    halos = halo_copies(0, state)
    for copy in halos:
        copy.start()

    loads[2].wait()
    loads[3].wait()
    for copy in halos:
        copy.wait_recv()

    def keep(z, value):
        later[z + 1] = value

    high, low = advance(0, state, keep, True)
    pack_faces(1, later, high, low)
    more = halo_copies(1, later)
    for copy in more:
        copy.start()

    for copy in first:
        copy.wait_recv()
    empty = jnp.zeros((16, 128), f32)
    myself = gx.astype(f32)

    def from_line(source, carry):
        rank, picked = carry
        for k in range(2):
            goal = line[source, 32:48, :].astype(f32)[8 * k : 8 * k + 8]
            record = line[source, pl.ds(16 * k, 16), :].astype(f32)
            hit = goal == myself
            picked = tuple(
                jnp.where(jnp.concatenate([hit & (rank == c)] * 2, axis=0), record, old)
                for c, old in enumerate(picked)
            )
            rank = rank + hit.astype(f32)
        return rank, picked

    rank, picked = lax.fori_loop(
        0, n_gx, from_line, (jnp.zeros((8, 128), f32), (empty,) * CAP)
    )
    for c in range(CAP):
        sent[pl.ds(16 * c, 16), :] = picked[c].astype(bf16)
    sent[16 * CAP : 16 * CAP + 16, :] = jnp.concatenate([rank, rank], axis=0).astype(bf16)
    place_id = ga * 2 + gy % 2
    group[place_id] = sent[...]
    second = []
    for far, device in block_partners(n_ga):
        copy = remote(sent, group.at[place_id], group_send.at[far], group_recv.at[far], device)
        copy.start()
        second.append(copy)

    for copy in more:
        copy.wait_recv()

    def emit(z, value):
        new_field[z] = value

    advance(1, later, emit, False)
    for copy in second:
        copy.wait_recv()
    share = 2 * n_ga
    place_f = place_id.astype(f32)
    first_line = gy - gy % 2

    def from_group(source, carry):
        base, picked, lines = carry
        number = group[source, 16 * CAP : 16 * CAP + 16, :].astype(f32)[0:8]
        for c in range(CAP):
            record = group[source, pl.ds(16 * c, 16), :].astype(f32)
            spot = jnp.where(number > c, base + c, -1.0)
            hits = [spot == place_f + share * i for i in range(CAP)]
            picked = tuple(
                jnp.where(jnp.concatenate([hit] * 2, axis=0), record, old)
                for hit, old in zip(hits, picked)
            )
            origin = (source // 2) * n_gy + first_line + source % 2
            lines = tuple(jnp.where(hit, origin, old) for hit, old in zip(hits, lines))
        return base + number, picked, lines

    none = jnp.zeros((8, 128), jnp.int32)
    total, picked, lines = lax.fori_loop(
        0, share, from_group, (jnp.zeros((8, 128), f32), (empty,) * CAP, (none,) * CAP)
    )
    number = none
    for i in range(CAP):
        batch[i] = picked[i].astype(bf16)
        number = number + (place_f + share * i < total).astype(jnp.int32)
    meta[0:1, :] = number[0:1]
    for i in range(CAP):
        meta[1 + i : 2 + i, :] = lines[i][0:1]
    meta[5:8, :] = rank[0:3].astype(jnp.int32)

    for copy in first + second + halos + more:
        copy.wait_send()


def route_call(count, dest, start_x, start_y, field, prev_field, diffusivity, velocity):
    n_gx, n_gy, n_ga = (lax.axis_size(name) for name in ("gx", "gy", "ga"))
    size_z, size_x, size_y = field.shape
    smem = pl.BlockSpec(memory_space=pltpu.SMEM)
    vmem = pl.BlockSpec(memory_space=pltpu.VMEM)
    hbm = pl.BlockSpec(memory_space=pltpu.HBM)
    share = 2 * n_ga
    dma = pltpu.SemaphoreType.DMA
    return pl.pallas_call(
        functools.partial(route_kernel, n_gx, n_gy, n_ga),
        out_shape=(
            jax.ShapeDtypeStruct(field.shape, f32),
            jax.ShapeDtypeStruct((CAP, 16, 128), bf16),
            jax.ShapeDtypeStruct((8, 128), jnp.int32),
        ),
        in_specs=[smem] * 4 + [hbm] * 4,
        out_specs=(vmem,) * 3,
        scratch_shapes=[
            pltpu.VMEM((size_z + 2, size_x, size_y), f32),
            pltpu.VMEM((size_z + 2, size_x, size_y), f32),
            pltpu.VMEM((size_z, size_x, size_y), f32),
            pltpu.VMEM((size_z, size_x, size_y), f32),
            pltpu.VMEM((3, size_z, size_x, size_y), f32),
            dma((4,)),
            pltpu.VMEM((48, 128), bf16),
            pltpu.VMEM((n_gx, 48, 128), bf16),
            pltpu.VMEM((16 * CAP + 16, 128), bf16),
            pltpu.VMEM((share, 16 * CAP + 16, 128), bf16),
            pltpu.VMEM((STEPS, size_x, 128), f32),
            pltpu.VMEM((STEPS, 2, size_z, 128), f32),
            pltpu.VMEM((STEPS, 2, size_z, 128), f32),
            pltpu.VMEM((STEPS, 2, size_x, 128), f32),
            pltpu.VMEM((STEPS, 2, size_x, 128), f32),
            dma((n_gx,)),
            dma((n_gx,)),
            dma((share,)),
            dma((share,)),
            dma((STEPS * 5,)),
            dma((STEPS * 5,)),
        ],
        compiler_params=pltpu.CompilerParams(
            collective_id=0, has_side_effects=True, vmem_limit_bytes=56 * 1024 * 1024
        ),
    )(count, dest, start_x, start_y, field, prev_field, diffusivity, velocity)


def train_call(meta, recs, w_lift, gain, w_conv, w_out, cells):
    vm = pl.BlockSpec(memory_space=pltpu.VMEM)
    hbm = pl.BlockSpec(memory_space=pltpu.HBM)
    return pl.pallas_call(
        train_kernel,
        out_shape=(
            jax.ShapeDtypeStruct((3456, 128), f32),
            jax.ShapeDtypeStruct((40, 128), f32),
            jax.ShapeDtypeStruct(cells.shape, f32),
        ),
        in_specs=[pl.BlockSpec(memory_space=pltpu.SMEM)] + [vm] * 6,
        out_specs=(vm, vm, hbm),
        scratch_shapes=[
            pltpu.VMEM((9, 384, 128), bf16),
            pltpu.VMEM((9, 384, 128), bf16),
            pltpu.VMEM((10, 6, 32, 384), bf16),
            pltpu.VMEM((10, 6, 32, 384), bf16),
            pltpu.VMEM((10, 128, 128), bf16),
            pltpu.VMEM((8, 32, 128), f32),
            pltpu.VMEM((8, 128, 128), bf16),
            pltpu.VMEM((8, 128, 128), f32),
            pltpu.VMEM((1024, 128), f32),
            pltpu.VMEM((8, 128, 128), bf16),
            pltpu.SemaphoreType.DMA,
        ],
        compiler_params=pltpu.CompilerParams(vmem_limit_bytes=32 * 1024 * 1024),
    )(meta, recs, w_lift, gain, w_conv, w_out, cells)


def row_cuts(rows):
    tiles = rows // 16
    ends = [16 * (tiles * i // 4 + (1 if 0 < i < 4 and tiles * i % 4 else 0)) for i in range(5)]
    return [(low, high - low) for low, high in zip(ends, ends[1:])]


def reduce_kernel(
    n_gx, n_gy, n_ga, rows, entries,
    conv, small, meta,
    total_out, tail_out,
    ring, own, other, gathered, pieces, from_line, tile_b, from_group, tile_c, from_all,
    ring_send, ring_recv, pair_send, pair_recv, gather_send, gather_recv,
    a_send, a_recv, b_send, b_recv, c_send, c_recv,
):
    gx, gy, ga = lax.axis_index("gx"), lax.axis_index("gy"), lax.axis_index("ga")
    line_id = ga * n_gy + gy
    barrier, expected = meet(
        [device for _, device in line_partners(n_gx)]
        + [device for _, device in group_partners(n_gy, n_ga)]
    )
    subs = row_cuts(rows)
    far_side = n_gy // 2
    signs = (1, -1)
    keys = [(0, 0), (1, 2), (0, 1), (1, 3), (0, 2), (1, 0), (0, 3), (1, 1)]
    depth = {(side, part): far_side if part // 2 == side else n_gy - 1 - far_side for side, part in keys}
    sub8 = lax.broadcasted_iota(jnp.int32, (8, 128), 0)
    lane8 = lanes_of((8, 128))
    share = n_gy * n_ga
    per = 32 // n_gx

    for k in range(n_gx):
        pieces[k] = jnp.concatenate(
            [small[per * k : per * k + per, :], jnp.zeros((8 - per, 128), f32)], axis=0
        )
    from_line[gx] = pieces[gx]

    def wrap(index):
        return (index + 2 * n_gy) % n_gy

    def rows_of(index, part):
        low, size = subs[part]
        return pl.ds(pl.multiple_of(wrap(index) * rows + low, 8), size)

    def next_to(side):
        return {"gy": wrap(gy + signs[side])}

    def ring_copy(step, side, part):
        low, size = subs[part]
        if step == 0:
            src = conv.at[rows_of(gy + signs[side] * depth[side, part], part)]
        else:
            src = ring.at[step - 1, side, pl.ds(low, size)]
        return remote(
            src, ring.at[step, side, pl.ds(low, size)],
            ring_send.at[step, side, part], ring_recv.at[step, side, part], next_to(side),
        )

    started = []

    def begin(copy):
        copy.start()
        started.append(copy)
        return copy

    pl.semaphore_wait(barrier, expected)
    flying = {key: begin(ring_copy(0, *key)) for key in keys}
    line_copies = [
        begin(remote(
            pieces.at[device["gx"]], from_line.at[gx], a_send.at[far], a_recv.at[far], device
        ))
        for far, device in line_partners(n_gx)
    ]

    pairs = {}
    for step in range(far_side):
        for key in keys:
            side, part = key
            low, size = subs[part]
            if step >= depth[key]:
                continue
            flying[key].wait_recv()
            if step + 1 < depth[key]:
                there = rows_of(gy + signs[side] * (depth[key] - 1 - step), part)
                ring[step, side, pl.ds(low, size), :] += conv[there, :]
                flying[key] = begin(ring_copy(step + 1, *key))
            elif step == far_side - 1:
                here = pl.ds(low, size)
                near = depth[1 - side, part] - 1
                own[here, :] = (
                    ring[step, side, here, :] + ring[near, 1 - side, here, :]
                ) + conv[rows_of(gy, part), :]
                pairs[part] = begin(remote(
                    own.at[here], other.at[here], pair_send.at[part], pair_recv.at[part],
                    {"ga": 1 - ga},
                ))

    for copy in line_copies:
        copy.wait_recv()
    piece = lax.fori_loop(0, n_gx, lambda k, acc: acc + from_line[k], jnp.zeros((8, 128), f32))

    def gather_copy(step, side, part):
        low, size = subs[part]
        where = gathered.at[wrap(gy - signs[side] * step), pl.ds(low, size)]
        return remote(
            where, where,
            gather_send.at[step, side, part], gather_recv.at[step, side, part], next_to(side),
        )

    squares = jnp.zeros((1, 128), f32)
    for part in (0, 2, 1, 3):
        low, size = subs[part]
        here = pl.ds(low, size)
        pairs[part].wait_recv()
        total = own[here, :] + other[here, :]
        gathered[gy, here, :] = total.astype(bf16)
        for side in (part // 2, 1 - part // 2):
            flying[side, part] = begin(gather_copy(0, side, part))
        squares = squares + jnp.sum(total * total, axis=0, keepdims=True)
    squares = jnp.where(ga == 0, squares, 0.0)
    tile_b[...] = jnp.where(
        sub8 < per,
        piece,
        jnp.where(sub8 == per, squares, jnp.where(sub8 == per + 1, small[32:33, :], 0.0)),
    )
    from_group[line_id] = tile_b[...]
    group_copies = [
        begin(remote(tile_b, from_group.at[line_id], b_send.at[far], b_recv.at[far], device))
        for far, device in group_partners(n_gy, n_ga)
    ]

    for step in range(far_side):
        for key in keys:
            if step >= depth[key]:
                continue
            flying[key].wait_recv()
            if step + 1 < depth[key]:
                flying[key] = begin(gather_copy(step + 1, *key))
        if step == 1:
            for copy in group_copies:
                copy.wait_recv()
            summed = lax.fori_loop(
                0, share, lambda k, acc: acc + from_group[k], jnp.zeros((8, 128), f32)
            )
            tile_c[...] = summed
            from_all[gx] = summed
            last_copies = [
                begin(remote(tile_c, from_all.at[gx], c_send.at[far], c_recv.at[far], device))
                for far, device in line_partners(n_gx)
            ]

    total_out[...] = gathered[...]
    for copy in last_copies:
        copy.wait_recv()
    shared = jnp.concatenate([from_all[k, 0:per, :] for k in range(n_gx)], axis=0)
    conv_squares = lax.fori_loop(
        0, n_gx, lambda k, acc: acc + from_all[k], jnp.zeros((8, 128), f32)
    )[per : per + 1]
    all_squares = jnp.sum(
        conv_squares + jnp.sum(shared * shared, axis=0, keepdims=True), axis=1, keepdims=True
    )
    scale = lax.rsqrt(all_squares / entries + 1e-06)
    tail_out[0:32, :] = shared * scale
    number = jnp.maximum(meta[5:6, :], 1).astype(f32)
    own_loss = jnp.sum(
        jnp.where(lane8[0:1] == line_id, summed[per + 1 : per + 2], 0.0), axis=1, keepdims=True
    )
    loss = own_loss / (PVOX * number)
    tail_out[32:40, :] = jnp.where(sub8 == 0, jnp.broadcast_to(scale, (8, 128)), loss)
    for copy in started:
        copy.wait_send()


def reduce_call(conv, small, meta, entries):
    n_gx, n_gy, n_ga = (lax.axis_size(name) for name in ("gx", "gy", "ga"))
    share = n_gy * n_ga
    rows = conv.shape[0] // n_gy
    far_side = n_gy // 2
    vmem = pl.BlockSpec(memory_space=pltpu.VMEM)
    dma = pltpu.SemaphoreType.DMA
    return pl.pallas_call(
        functools.partial(reduce_kernel, n_gx, n_gy, n_ga, rows, entries),
        out_shape=(
            jax.ShapeDtypeStruct((n_gy, rows, 128), bf16), jax.ShapeDtypeStruct((40, 128), f32)
        ),
        in_specs=[vmem] * 3,
        out_specs=(vmem,) * 2,
        scratch_shapes=[
            pltpu.VMEM((far_side, 2, rows, 128), f32),
            pltpu.VMEM((rows, 128), f32),
            pltpu.VMEM((rows, 128), f32),
            pltpu.VMEM((n_gy, rows, 128), bf16),
            pltpu.VMEM((n_gx, 8, 128), f32),
            pltpu.VMEM((n_gx, 8, 128), f32),
            pltpu.VMEM((8, 128), f32),
            pltpu.VMEM((share, 8, 128), f32),
            pltpu.VMEM((8, 128), f32),
            pltpu.VMEM((n_gx, 8, 128), f32),
            dma((far_side, 2, 4)), dma((far_side, 2, 4)),
            dma((4,)), dma((4,)),
            dma((far_side, 2, 4)), dma((far_side, 2, 4)),
            dma((n_gx,)), dma((n_gx,)),
            dma((share,)), dma((share,)),
            dma((n_gx,)), dma((n_gx,)),
        ],
        compiler_params=pltpu.CompilerParams(
            collective_id=1, has_side_effects=True, vmem_limit_bytes=32 * 1024 * 1024
        ),
    )(conv, small, meta)


def finish_kernel(total, tail, conv_out, lift_out, gain_out, out_out, loss_out):
    scale = tail[32:33, :]
    for chunk in range(total.shape[0]):
        size = total.shape[1]
        conv_out[pl.ds(chunk * size, size), :] = total[chunk].astype(f32) * scale
    lift_out[...] = tail[0:27, :]
    gain_out[...] = tail[27:28, :]
    out_out[...] = tail[28:29, :]
    loss_out[...] = tail[33:34, :]


def finish_call(total, tail):
    vmem = pl.BlockSpec(memory_space=pltpu.VMEM)
    tile = functools.partial(jax.ShapeDtypeStruct, dtype=f32)
    return pl.pallas_call(
        finish_kernel,
        out_shape=(
            tile((total.shape[0] * total.shape[1], 128)),
            tile((27, 128)), tile((1, 128)), tile((1, 128)), tile((1, 128)),
        ),
        in_specs=[vmem] * 2,
        out_specs=(vmem,) * 5,
        compiler_params=pltpu.CompilerParams(vmem_limit_bytes=16 * 1024 * 1024),
    )(total, tail)


def body(
    field, prev_field, diffusivity, velocity, w_lift, norm_gain, w_conv, w_out,
    tile_count, patch_dest, anchor_x, anchor_y,
):
    stepped, batch, meta = route_call(
        tile_count.reshape(1), patch_dest.reshape(2), anchor_x.reshape(2), anchor_y.reshape(2),
        field, prev_field, diffusivity, velocity,
    )
    lift_rows = jnp.pad(w_lift, ((0, 32 - w_lift.shape[0]), (0, 0)))
    conv, small, new_field = train_call(
        meta, batch, lift_rows, norm_gain[None], w_conv[0], w_out[None], stepped
    )
    entries = w_lift.size + norm_gain.size + w_out.size + lax.axis_size("gx") * w_conv[0].size
    total, tail = reduce_call(conv, small, meta, entries)
    dir_conv, lift, gain, out, loss = finish_call(total, tail)
    return (
        new_field, loss[:, :1].reshape(1, 1, 1), lift, gain.reshape(-1),
        dir_conv.reshape(w_conv.shape), out.reshape(-1),
    )


def solution(mesh):
    tiles = P("ga", "gx", "gy")
    slots = P("ga", "gx", "gy", None)
    in_specs = (
        tiles, tiles, tiles, P(None, "ga", "gx", "gy"), P(), P(), P("gx", None, None), P(),
        tiles, slots, slots, slots,
    )
    out_specs = (tiles, tiles, P(), P(), P("gx", None, None), P())
    return jax.shard_map(body, mesh=mesh, in_specs=in_specs, out_specs=out_specs, check_vma=False)
```

```python
import functools

import jax
import jax.numpy as jnp
from jax import lax
from jax.experimental import pallas as pl
from jax.experimental.pallas import tpu as pltpu
from jax.sharding import PartitionSpec as P

STEPS = 2
PVOX = 1024
CAP = 4
META = 16 * CAP
ROOT = 0.7978845608028654
CUBE = 0.044715
MESH = pl.DeviceIdType.MESH
f32, bf16 = jnp.float32, jnp.bfloat16


def gelu_both(v):
    v2 = v * v
    t = jnp.tanh(ROOT * (v + CUBE * (v * v2)))
    half = 0.5 * (1.0 + t)
    slope = half + 0.5 * v * (1.0 - t * t) * (ROOT * (1.0 + 3.0 * CUBE * v2))
    return v * half, slope


def z_shifted(block, z_ids):
    up = jnp.where(z_ids == 31, 0.0, pltpu.roll(block, 127, 0))
    down = jnp.where(z_ids == 0, 0.0, pltpu.roll(block, 1, 0))
    return up, down


def steps_of(count, step, carry):
    for x in range(count):
        carry = step(x, carry)
    return carry


def move_y(block, by):
    if by == 0:
        return block
    gap = jnp.zeros((1,) + block.shape[1:], block.dtype)
    parts = [block[1:], gap] if by > 0 else [gap, block[:-1]]
    return jnp.concatenate(parts, axis=0)


def conv_rows(source, weights, x, sign):
    acc = None
    for q in range(3):
        x_in = x + sign * (q - 1)
        if x_in < 0 or x_in > 7:
            continue
        lhs = source[x_in + 1, 1:5].reshape(128, 384)
        d = jnp.dot(lhs, weights[q], preferred_element_type=f32).reshape(4, 32, 384)
        for r in range(3):
            piece = move_y(d[:, :, r * 128 : (r + 1) * 128], sign * (r - 1))
            acc = piece if acc is None else acc + piece
    return acc.reshape(128, 128)


def train_kernel(
    routed, w_lift, gain, w_conv, w_out, conv_out, small_out,
    wf, wb, vp, gp, nt, nu, lifted, slope1, pre2, dh, lift_rows,
):
    f32, bf16 = jnp.float32, jnp.bfloat16
    vp[...] = jnp.zeros_like(vp)
    gp[...] = jnp.zeros_like(gp)
    nt[...] = jnp.zeros_like(nt)
    nu[...] = jnp.zeros_like(nu)
    conv_out[...] = jnp.zeros_like(conv_out)
    small_out[...] = jnp.zeros_like(small_out)
    for q in range(3):
        for r in range(3):
            for p in range(3):
                blk = w_conv[pl.ds(((p * 3 + q) * 3 + r) * 128, 128), :]
                wf[q, pl.ds(p * 128, 128), pl.ds(r * 128, 128)] = blk
                wb[q, pl.ds(p * 128, 128), pl.ds(r * 128, 128)] = blk.astype(f32).T.astype(bf16)
    z_ids = lax.broadcasted_iota(jnp.int32, (128, 128), 0) % 32
    lane = lax.broadcasted_iota(jnp.int32, (8, 128), 1)
    sub = lax.broadcasted_iota(jnp.int32, (8, 128), 0)
    gain_row = gain[...]
    lift_rows[...] = jnp.zeros_like(lift_rows)
    lift_rows[0:27, :] = w_lift[...].astype(f32)
    lift_weights = lift_rows[...].astype(bf16)
    wo_row = w_out[...].astype(f32)

    def patch(i, carry):
        u = routed[pl.ds(16 * i, 8), :]
        target = routed[pl.ds(16 * i + 8, 8), :]
        for p in range(3):
            dz = p - 1
            uz = u if dz == 0 else pltpu.roll(u, (-dz) % 128, 1)
            okz = (lane % 32 + dz >= 0) & (lane % 32 + dz < 32)
            for q in range(3):
                dx = q - 1
                ux = uz if dx == 0 else pltpu.roll(uz, (-dx) % 8, 0)
                okx = (sub + dx >= 0) & (sub + dx < 8)
                for r in range(3):
                    dy = r - 1
                    uy = ux if dy == 0 else pltpu.roll(ux, (-32 * dy) % 128, 1)
                    oky = (lane // 32 + dy >= 0) & (lane // 32 + dy < 4)
                    nu[:, p * 9 + q * 3 + r, :] = jnp.where(okz & okx & oky, uy, 0.0)

        def lift(x, c):
            pre = lax.dot_general(
                nu[x].astype(bf16), lift_weights, (((0,), (0,)), ((), ())), preferred_element_type=f32
            )
            val, slope = gelu_both(pre)
            slope1[x] = slope
            low = val.astype(bf16)
            lifted[x] = low
            wide = low.astype(f32)
            inv = lax.rsqrt(jnp.mean(wide * wide, axis=1, keepdims=True) + 1e-06)
            normed = (wide * inv * gain_row).astype(bf16).astype(f32)
            up, down = z_shifted(normed, z_ids)
            for k, v in enumerate((down, normed, up)):
                vp[x + 1, 1:5, :, k * 128 : (k + 1) * 128] = v.astype(bf16).reshape(4, 32, 128)
            nt[x + 1] = normed.T.astype(bf16)
            return c

        steps_of(8, lift, 0)
        for x in range(8):
            pre2[pl.ds(x * 128, 128), :] = conv_rows(vp, wf, x, 1)

        def out_step(x, c):
            loss, dwo = c
            mixed, slope = gelu_both(pre2[pl.ds(x * 128, 128), :])
            hid = (lifted[x].astype(f32) + mixed).astype(bf16).astype(f32)
            pred = jnp.sum(hid * wo_row, axis=1, keepdims=True)
            row = jnp.sum(jnp.where(sub == x, target, 0.0), axis=0, keepdims=True)
            wanted = jnp.broadcast_to(row, (128, 128)).T
            misfit = pred - wanted
            loss = loss + jnp.sum(misfit * misfit, axis=0, keepdims=True)
            dwo = dwo + jnp.sum(hid * misfit, axis=0, keepdims=True)
            d_hid = (misfit * wo_row).astype(bf16)
            dh[x] = d_hid
            g = (d_hid.astype(f32) * slope).astype(bf16).astype(f32)
            up, down = z_shifted(g, z_ids)
            for k, v in enumerate((up, g, down)):
                gp[x + 1, 1:5, :, k * 128 : (k + 1) * 128] = v.astype(bf16).reshape(4, 32, 128)
            return loss, dwo

        zero_row = jnp.zeros((1, 128), f32)
        loss, dwo = steps_of(8, out_step, (zero_row, zero_row))
        lhs = jnp.concatenate(
            [jnp.concatenate([nt[q + x] for x in range(8)], axis=1) for q in range(3)], axis=0
        )
        for r in range(3):
            rhs = gp[1:9, 2 - r : 6 - r].reshape(1024, 384)
            d = jnp.dot(lhs, rhs, preferred_element_type=f32)
            for q in range(3):
                for p in range(3):
                    rows = pl.ds(((p * 3 + q) * 3 + r) * 128, 128)
                    piece = d[q * 128 : (q + 1) * 128, p * 128 : (p + 1) * 128]
                    conv_out[rows, :] += piece.astype(bf16).astype(f32)
        for x in range(8):
            pre2[pl.ds(x * 128, 128), :] = conv_rows(gp, wb, x, -1)

        def back(x, c):
            dgain, dwl = c
            dn = pre2[pl.ds(x * 128, 128), :].astype(bf16).astype(f32)
            wide = lifted[x].astype(f32)
            inv = lax.rsqrt(jnp.mean(wide * wide, axis=1, keepdims=True) + 1e-06)
            unit = wide * inv
            dgain = dgain + jnp.sum(dn * unit, axis=0, keepdims=True)
            dt = dn * gain_row
            mean = jnp.sum(dt * wide, axis=1, keepdims=True) * (1.0 / 128.0)
            d_low = dh[x].astype(f32) + dt * inv - (inv * inv * inv * mean) * wide
            d_pre = d_low.astype(bf16).astype(f32) * slope1[x]
            dwl = dwl + jnp.dot(nu[x].astype(bf16), d_pre.astype(bf16), preferred_element_type=f32)
            return dgain, dwl

        dgain, dwl = steps_of(8, back, (zero_row, jnp.zeros((32, 128), f32)))
        small_out[0:32, :] += dwl.astype(bf16).astype(f32)
        small_out[27:28, :] += dgain
        small_out[28:29, :] += dwo.astype(bf16).astype(f32)
        line = routed[pl.ds(META + 1 + i, 1), :]
        small_out[32:33, :] += jnp.where(lane[0:1].astype(f32) == line, 0.5 * loss, 0.0)
        return carry

    number = jnp.max(routed[META : META + 1, :]).astype(jnp.int32)
    lax.fori_loop(0, number, patch, 0)


def lanes_of(shape):
    return lax.broadcasted_iota(jnp.int32, shape, len(shape) - 1)


def group_partners(n_gy, n_ga):
    gy, ga = lax.axis_index("gy"), lax.axis_index("ga")
    for far in range(1, n_gy * n_ga):
        there = (gy + far % n_gy) % n_gy
        across = (ga + far // n_gy) % n_ga
        yield far, {"gy": there, "ga": across}


def line_partners(n_gx):
    gx = lax.axis_index("gx")
    for far in range(1, n_gx):
        yield far, {"gx": (gx + far) % n_gx}


def block_partners(n_ga):
    gy, ga = lax.axis_index("gy"), lax.axis_index("ga")
    for far in range(1, 2 * n_ga):
        there = gy + (far % 2) * (1 - 2 * (gy % 2))
        yield far, {"gy": there, "ga": (ga + far // 2) % n_ga}


def meet(devices):
    barrier = pltpu.get_barrier_semaphore()
    for device in devices:
        pl.semaphore_signal(barrier, inc=1, device_id=device, device_id_type=MESH)
    return barrier, len(devices)


def several(count, step, carry, at_once=4):
    def run(block, carry):
        for i in range(at_once):
            carry = step(block * at_once + i, carry)
        return carry

    return lax.fori_loop(0, count // at_once, run, carry)


def remote(src, dst, send_sem, recv_sem, device):
    return pltpu.make_async_remote_copy(
        src_ref=src, dst_ref=dst, send_sem=send_sem, recv_sem=recv_sem,
        device_id=device, device_id_type=MESH,
    )


def route_kernel(
    n_gx, n_gy, n_ga,
    count, dest, start_x, start_y, field, prev_field, diffusivity, velocity,
    new_field, routed,
    state, later, prev, diff, speed, load_sem,
    mine, line, sent, group,
    z_in, x_out, x_in, y_out, y_in,
    line_send, line_recv, group_send, group_recv, halo_send, halo_recv,
):
    gx, gy, ga = lax.axis_index("gx"), lax.axis_index("gy"), lax.axis_index("ga")
    barrier, expected = meet(
        [device for _, device in line_partners(n_gx)]
        + [device for _, device in block_partners(n_ga)]
        + [{"gy": (gy + 1) % n_gy}, {"gy": (gy + n_gy - 1) % n_gy}]
    )
    size_z, size_x, size_y = prev.shape
    loads = [
        pltpu.make_async_copy(field, state.at[pl.ds(1, size_z)], load_sem.at[0]),
        pltpu.make_async_copy(prev_field, prev, load_sem.at[1]),
        pltpu.make_async_copy(diffusivity, diff, load_sem.at[2]),
        pltpu.make_async_copy(velocity, speed, load_sem.at[3]),
    ]
    for load in loads:
        load.start()
    sub8 = lax.broadcasted_iota(jnp.int32, (8, 128), 0)
    xi = lax.broadcasted_iota(jnp.int32, (size_x, 128), 0)
    li = lanes_of((size_x, 128))
    row_y = lax.broadcasted_iota(jnp.int32, (128, 128), 0)
    col = lanes_of((128, 128))
    z_mask = (
        lax.broadcasted_iota(jnp.int32, (size_z, 8, 128), 0) == lanes_of((size_z, 8, 128)) % size_z
    )
    zero_tile = jnp.zeros((size_x, 128), f32)

    def pack_faces(step, cells, high, low):
        x_out[step, 0] = cells[1 : size_z + 1, 0, :]
        x_out[step, 1] = cells[1 : size_z + 1, size_x - 1, :]
        y_out[step, 0] = low
        y_out[step, 1] = high

    def halo_copies(step, cells):
        base = step * 5
        z_src = cells.at[size_z - (size_z - 1) * ga]
        there = {"ga": 1 - ga}
        z_out_copy = remote(
            z_src, z_in.at[step], halo_send.at[base], halo_recv.at[base], there
        )
        copies = [z_out_copy]
        for side in range(2):
            near = (gx + (n_gx - 1 if side == 0 else 1)) % n_gx
            copies.append(remote(
                x_out.at[step, side], x_in.at[step, 1 - side],
                halo_send.at[base + 1 + side], halo_recv.at[base + 1 + side], {"gx": near},
            ))
        for side in range(2):
            near = (gy + (n_gy - 1 if side == 0 else 1)) % n_gy
            copies.append(remote(
                y_out.at[step, side], y_in.at[step, 1 - side],
                halo_send.at[base + 3 + side], halo_recv.at[base + 3 + side], {"gy": near},
            ))
        return copies

    def place(z, cells, high, low):
        high = jnp.where(li == z, pltpu.roll(cells, z + 1, 1), high)
        low = jnp.where(li == z, pltpu.roll(cells, z, 1), low)
        return high, low

    def advance(step, cells, store, pack):
        z_face = z_in[step]
        cells[0] = jnp.where(ga == 1, z_face, 0.0)
        cells[size_z + 1] = jnp.where(ga == 0, z_face, 0.0)

        def layer(z, faces):
            centre = cells[z + 1]
            below = cells[z]
            above = cells[z + 2]
            behind = jnp.where(xi == 0, x_in[step, 0, pl.ds(z, 1), :], pltpu.roll(centre, 1, 0))
            ahead = jnp.where(
                xi == size_x - 1, x_in[step, 1, pl.ds(z, 1), :], pltpu.roll(centre, size_x - 1, 0)
            )
            left = jnp.where(
                li == 0, pltpu.roll(y_in[step, 0], 128 - z, 1), pltpu.roll(centre, 1, 1)
            )
            right = jnp.where(
                li == 127, pltpu.roll(y_in[step, 1], 127 - z, 1), pltpu.roll(centre, 127, 1)
            )
            laplace = above + below + (ahead + behind) + (right + left) - 6.0 * centre
            moved = jnp.zeros_like(centre)
            for d, (low, high) in enumerate(((below, above), (behind, ahead), (left, right))):
                v = speed[d, z]
                moved = moved + (
                    jnp.maximum(v, 0.0) * (centre - low) + jnp.minimum(v, 0.0) * (high - centre)
                )
            result = centre + diff[z] * laplace - moved
            store(z, result)
            return place(z, result, *faces) if pack else faces

        return several(size_z, layer, (zero_tile, zero_tile))

    loads[0].wait()
    high, low = several(
        size_z, lambda z, faces: place(z, state[z + 1], *faces), (zero_tile, zero_tile)
    )
    pack_faces(0, state, high, low)
    loads[1].wait()
    for k in range(2):
        chosen = (row_y == start_y[k] + col // size_z).astype(bf16)
        parts = []
        for source in (0, 1):
            if source == 0:
                window = prev[:, pl.ds(start_x[k], 8), :]
            else:
                window = state[1 : size_z + 1, pl.ds(start_x[k], 8), :]
            spread = jnp.dot(
                window.reshape(size_z * 8, 128).astype(bf16), chosen, preferred_element_type=f32
            ).reshape(size_z, 8, 128)
            parts.append(jnp.sum(jnp.where(z_mask, spread, 0.0), axis=0))
        mine[pl.ds(16 * k, 16), :] = jnp.concatenate(parts, axis=0).astype(bf16)
    goals = [jnp.where(k < count[0], dest[k], -1).astype(f32) for k in range(2)]
    mine[32:48, :] = jnp.concatenate(
        [jnp.full((8, 128), goals[0]), jnp.full((8, 128), goals[1])], axis=0
    ).astype(bf16)
    line[gx] = mine[...]

    pl.semaphore_wait(barrier, expected)
    first = []
    for far, device in line_partners(n_gx):
        copy = remote(mine, line.at[gx], line_send.at[far], line_recv.at[far], device)
        copy.start()
        first.append(copy)
    halos = halo_copies(0, state)
    for copy in halos:
        copy.start()

    loads[2].wait()
    loads[3].wait()
    for copy in halos:
        copy.wait_recv()

    def keep(z, value):
        later[z + 1] = value

    high, low = advance(0, state, keep, True)
    pack_faces(1, later, high, low)
    more = halo_copies(1, later)
    for copy in more:
        copy.start()

    for copy in first:
        copy.wait_recv()
    empty = jnp.zeros((16, 128), f32)
    myself = gx.astype(f32)

    def from_line(source, carry):
        rank, picked = carry
        for k in range(2):
            goal = line[source, 32:48, :].astype(f32)[8 * k : 8 * k + 8]
            record = line[source, pl.ds(16 * k, 16), :].astype(f32)
            hit = goal == myself
            picked = tuple(
                jnp.where(jnp.concatenate([hit & (rank == c)] * 2, axis=0), record, old)
                for c, old in enumerate(picked)
            )
            rank = rank + hit.astype(f32)
        return rank, picked

    rank, picked = lax.fori_loop(
        0, n_gx, from_line, (jnp.zeros((8, 128), f32), (empty,) * CAP)
    )
    for c in range(CAP):
        sent[pl.ds(16 * c, 16), :] = picked[c].astype(bf16)
    sent[16 * CAP : 16 * CAP + 16, :] = jnp.concatenate([rank, rank], axis=0).astype(bf16)
    place_id = ga * 2 + gy % 2
    group[place_id] = sent[...]
    second = []
    for far, device in block_partners(n_ga):
        copy = remote(sent, group.at[place_id], group_send.at[far], group_recv.at[far], device)
        copy.start()
        second.append(copy)

    for copy in more:
        copy.wait_recv()

    def emit(z, value):
        new_field[z] = value

    advance(1, later, emit, False)
    for copy in second:
        copy.wait_recv()
    share = 2 * n_ga
    place_f = place_id.astype(f32)
    first_line = gy - gy % 2

    def from_group(source, carry):
        base, picked, lines = carry
        number = group[source, 16 * CAP : 16 * CAP + 16, :].astype(f32)[0:8]
        for c in range(CAP):
            record = group[source, pl.ds(16 * c, 16), :].astype(f32)
            spot = jnp.where(number > c, base + c, -1.0)
            hits = [spot == place_f + share * i for i in range(CAP)]
            picked = tuple(
                jnp.where(jnp.concatenate([hit] * 2, axis=0), record, old)
                for hit, old in zip(hits, picked)
            )
            origin = (source // 2) * n_gy + first_line + source % 2
            lines = tuple(jnp.where(hit, origin.astype(f32), old) for hit, old in zip(hits, lines))
        return base + number, picked, lines

    none = jnp.zeros((8, 128), f32)
    total, picked, lines = lax.fori_loop(
        0, share, from_group, (none, (empty,) * CAP, (none,) * CAP)
    )
    number = none
    for i in range(CAP):
        routed[pl.ds(16 * i, 16), :] = picked[i]
        number = number + (place_f + share * i < total).astype(f32)
    rows = jnp.where(sub8 == 0, number, rank)
    for i in range(CAP):
        rows = jnp.where(sub8 == 1 + i, lines[i], rows)
    routed[META : META + 8, :] = rows

    for copy in first + second + halos + more:
        copy.wait_send()


def route_call(count, dest, start_x, start_y, field, prev_field, diffusivity, velocity):
    n_gx, n_gy, n_ga = (lax.axis_size(name) for name in ("gx", "gy", "ga"))
    size_z, size_x, size_y = field.shape
    smem = pl.BlockSpec(memory_space=pltpu.SMEM)
    vmem = pl.BlockSpec(memory_space=pltpu.VMEM)
    hbm = pl.BlockSpec(memory_space=pltpu.HBM)
    share = 2 * n_ga
    dma = pltpu.SemaphoreType.DMA
    return pl.pallas_call(
        functools.partial(route_kernel, n_gx, n_gy, n_ga),
        out_shape=(
            jax.ShapeDtypeStruct(field.shape, f32),
            jax.ShapeDtypeStruct((META + 8, 128), f32),
        ),
        in_specs=[smem] * 4 + [hbm] * 4,
        out_specs=(vmem,) * 2,
        scratch_shapes=[
            pltpu.VMEM((size_z + 2, size_x, size_y), f32),
            pltpu.VMEM((size_z + 2, size_x, size_y), f32),
            pltpu.VMEM((size_z, size_x, size_y), f32),
            pltpu.VMEM((size_z, size_x, size_y), f32),
            pltpu.VMEM((3, size_z, size_x, size_y), f32),
            dma((4,)),
            pltpu.VMEM((48, 128), bf16),
            pltpu.VMEM((n_gx, 48, 128), bf16),
            pltpu.VMEM((16 * CAP + 16, 128), bf16),
            pltpu.VMEM((share, 16 * CAP + 16, 128), bf16),
            pltpu.VMEM((STEPS, size_x, 128), f32),
            pltpu.VMEM((STEPS, 2, size_z, 128), f32),
            pltpu.VMEM((STEPS, 2, size_z, 128), f32),
            pltpu.VMEM((STEPS, 2, size_x, 128), f32),
            pltpu.VMEM((STEPS, 2, size_x, 128), f32),
            dma((n_gx,)),
            dma((n_gx,)),
            dma((share,)),
            dma((share,)),
            dma((STEPS * 5,)),
            dma((STEPS * 5,)),
        ],
        compiler_params=pltpu.CompilerParams(
            collective_id=0, has_side_effects=True, vmem_limit_bytes=56 * 1024 * 1024
        ),
    )(count, dest, start_x, start_y, field, prev_field, diffusivity, velocity)


def train_call(routed, w_lift, gain, w_conv, w_out):
    vmem = pl.BlockSpec(memory_space=pltpu.VMEM)
    return pl.pallas_call(
        train_kernel,
        out_shape=(jax.ShapeDtypeStruct((3456, 128), f32), jax.ShapeDtypeStruct((40, 128), f32)),
        in_specs=[vmem] * 5,
        out_specs=(vmem, vmem),
        scratch_shapes=[
            pltpu.VMEM((3, 384, 384), bf16),
            pltpu.VMEM((3, 384, 384), bf16),
            pltpu.VMEM((10, 6, 32, 384), bf16),
            pltpu.VMEM((10, 6, 32, 384), bf16),
            pltpu.VMEM((10, 128, 128), bf16),
            pltpu.VMEM((8, 32, 128), f32),
            pltpu.VMEM((8, 128, 128), bf16),
            pltpu.VMEM((8, 128, 128), f32),
            pltpu.VMEM((1024, 128), f32),
            pltpu.VMEM((8, 128, 128), bf16),
            pltpu.VMEM((32, 128), f32),
        ],
        compiler_params=pltpu.CompilerParams(vmem_limit_bytes=32 * 1024 * 1024),
    )(routed, w_lift, gain, w_conv, w_out)


def row_cuts(rows):
    tiles = rows // 16
    ends = [16 * (tiles * i // 4 + (1 if 0 < i < 4 and tiles * i % 4 else 0)) for i in range(5)]
    return [(low, high - low) for low, high in zip(ends, ends[1:])]


def reduce_kernel(
    n_gx, n_gy, n_ga, rows, entries,
    conv, small, routed,
    total_out, tail_out,
    leaf_out, leaf_in, ring, own, other, gathered, pieces, from_line, tile_b, from_group, tile_c, from_all,
    ring_send, ring_recv, pair_send, pair_recv, gather_send, gather_recv,
    a_send, a_recv, b_send, b_recv, c_send, c_recv,
):
    gx, gy, ga = lax.axis_index("gx"), lax.axis_index("gy"), lax.axis_index("ga")
    line_id = ga * n_gy + gy
    barrier, expected = meet(
        [device for _, device in line_partners(n_gx)]
        + [device for _, device in group_partners(n_gy, n_ga)]
    )
    subs = row_cuts(rows)
    far_side = n_gy // 2
    signs = (1, -1)
    keys = [(0, 0), (1, 2), (0, 1), (1, 3), (0, 2), (1, 0), (0, 3), (1, 1)]
    depth = {(side, part): far_side if part // 2 == side else n_gy - 1 - far_side for side, part in keys}
    sub8 = lax.broadcasted_iota(jnp.int32, (8, 128), 0)
    lane8 = lanes_of((8, 128))
    share = n_gy * n_ga
    per = 32 // n_gx

    for k in range(n_gx):
        pieces[k] = jnp.concatenate(
            [small[per * k : per * k + per, :], jnp.zeros((8 - per, 128), f32)], axis=0
        )
    from_line[gx] = pieces[gx]

    def wrap(index):
        return (index + 2 * n_gy) % n_gy

    def rows_of(index, part):
        low, size = subs[part]
        return pl.ds(pl.multiple_of(wrap(index) * rows + low, 8), size)

    def next_to(side):
        return {"gy": wrap(gy + signs[side])}

    def ring_copy(step, side, part):
        low, size = subs[part]
        if step == 0:
            return remote(
                leaf_out.at[side, pl.ds(low, size)], leaf_in.at[side, pl.ds(low, size)],
                ring_send.at[0, side, part], ring_recv.at[0, side, part], next_to(side),
            )
        return remote(
            ring.at[step - 1, side, pl.ds(low, size)], ring.at[step, side, pl.ds(low, size)],
            ring_send.at[step, side, part], ring_recv.at[step, side, part], next_to(side),
        )

    for side, part in keys:
        low, size = subs[part]
        first = rows_of(gy + signs[side] * depth[side, part], part)
        leaf_out[side, pl.ds(low, size), :] = conv[first, :].astype(bf16)
    started = []

    def begin(copy):
        copy.start()
        started.append(copy)
        return copy

    pl.semaphore_wait(barrier, expected)
    flying = {key: begin(ring_copy(0, *key)) for key in keys}
    line_copies = [
        begin(remote(
            pieces.at[device["gx"]], from_line.at[gx], a_send.at[far], a_recv.at[far], device
        ))
        for far, device in line_partners(n_gx)
    ]

    pairs = {}
    for step in range(far_side):
        for key in keys:
            side, part = key
            low, size = subs[part]
            if step >= depth[key]:
                continue
            flying[key].wait_recv()
            if step + 1 < depth[key]:
                there = rows_of(gy + signs[side] * (depth[key] - 1 - step), part)
                here = pl.ds(low, size)
                came = leaf_in[side, here, :].astype(f32) if step == 0 else ring[step, side, here, :]
                ring[step, side, here, :] = came + conv[there, :]
                flying[key] = begin(ring_copy(step + 1, *key))
            elif step == far_side - 1:
                here = pl.ds(low, size)
                near = depth[1 - side, part] - 1
                own[here, :] = (
                    ring[step, side, here, :] + ring[near, 1 - side, here, :]
                ) + conv[rows_of(gy, part), :]
                pairs[part] = begin(remote(
                    own.at[here], other.at[here], pair_send.at[part], pair_recv.at[part],
                    {"ga": 1 - ga},
                ))

    for copy in line_copies:
        copy.wait_recv()
    piece = lax.fori_loop(0, n_gx, lambda k, acc: acc + from_line[k], jnp.zeros((8, 128), f32))

    def gather_copy(step, side, part):
        low, size = subs[part]
        where = gathered.at[wrap(gy - signs[side] * step), pl.ds(low, size)]
        return remote(
            where, where,
            gather_send.at[step, side, part], gather_recv.at[step, side, part], next_to(side),
        )

    squares = jnp.zeros((1, 128), f32)
    for part in (0, 2, 1, 3):
        low, size = subs[part]
        here = pl.ds(low, size)
        pairs[part].wait_recv()
        total = own[here, :] + other[here, :]
        gathered[gy, here, :] = total.astype(bf16)
        for side in (part // 2, 1 - part // 2):
            flying[side, part] = begin(gather_copy(0, side, part))
        squares = squares + jnp.sum(total * total, axis=0, keepdims=True)
    squares = jnp.where(ga == 0, squares, 0.0)
    tile_b[...] = jnp.where(
        sub8 < per,
        piece,
        jnp.where(sub8 == per, squares, jnp.where(sub8 == per + 1, small[32:33, :], 0.0)),
    )
    from_group[line_id] = tile_b[...]
    group_copies = [
        begin(remote(tile_b, from_group.at[line_id], b_send.at[far], b_recv.at[far], device))
        for far, device in group_partners(n_gy, n_ga)
    ]

    for step in range(far_side):
        for key in keys:
            if step >= depth[key]:
                continue
            flying[key].wait_recv()
            if step + 1 < depth[key]:
                flying[key] = begin(gather_copy(step + 1, *key))
        if step == 1:
            for copy in group_copies:
                copy.wait_recv()
            summed = lax.fori_loop(
                0, share, lambda k, acc: acc + from_group[k], jnp.zeros((8, 128), f32)
            )
            tile_c[...] = summed
            from_all[gx] = summed
            last_copies = [
                begin(remote(tile_c, from_all.at[gx], c_send.at[far], c_recv.at[far], device))
                for far, device in line_partners(n_gx)
            ]

    total_out[...] = gathered[...]
    for copy in last_copies:
        copy.wait_recv()
    shared = jnp.concatenate([from_all[k, 0:per, :] for k in range(n_gx)], axis=0)
    conv_squares = lax.fori_loop(
        0, n_gx, lambda k, acc: acc + from_all[k], jnp.zeros((8, 128), f32)
    )[per : per + 1]
    all_squares = jnp.sum(
        conv_squares + jnp.sum(shared * shared, axis=0, keepdims=True), axis=1, keepdims=True
    )
    scale = lax.rsqrt(all_squares / entries + 1e-06)
    tail_out[0:32, :] = shared * scale
    number = jnp.maximum(routed[META + 5 : META + 6, :], 1.0)
    own_loss = jnp.sum(
        jnp.where(lane8[0:1] == line_id, summed[per + 1 : per + 2], 0.0), axis=1, keepdims=True
    )
    loss = own_loss / (PVOX * number)
    tail_out[32:40, :] = jnp.where(sub8 == 0, jnp.broadcast_to(scale, (8, 128)), loss)
    for copy in started:
        copy.wait_send()


def reduce_call(conv, small, routed, entries):
    n_gx, n_gy, n_ga = (lax.axis_size(name) for name in ("gx", "gy", "ga"))
    share = n_gy * n_ga
    rows = conv.shape[0] // n_gy
    far_side = n_gy // 2
    vmem = pl.BlockSpec(memory_space=pltpu.VMEM)
    dma = pltpu.SemaphoreType.DMA
    return pl.pallas_call(
        functools.partial(reduce_kernel, n_gx, n_gy, n_ga, rows, entries),
        out_shape=(
            jax.ShapeDtypeStruct((n_gy, rows, 128), bf16), jax.ShapeDtypeStruct((40, 128), f32)
        ),
        in_specs=[vmem] * 3,
        out_specs=(vmem,) * 2,
        scratch_shapes=[
            pltpu.VMEM((2, rows, 128), bf16),
            pltpu.VMEM((2, rows, 128), bf16),
            pltpu.VMEM((far_side, 2, rows, 128), f32),
            pltpu.VMEM((rows, 128), f32),
            pltpu.VMEM((rows, 128), f32),
            pltpu.VMEM((n_gy, rows, 128), bf16),
            pltpu.VMEM((n_gx, 8, 128), f32),
            pltpu.VMEM((n_gx, 8, 128), f32),
            pltpu.VMEM((8, 128), f32),
            pltpu.VMEM((share, 8, 128), f32),
            pltpu.VMEM((8, 128), f32),
            pltpu.VMEM((n_gx, 8, 128), f32),
            dma((far_side, 2, 4)), dma((far_side, 2, 4)),
            dma((4,)), dma((4,)),
            dma((far_side, 2, 4)), dma((far_side, 2, 4)),
            dma((n_gx,)), dma((n_gx,)),
            dma((share,)), dma((share,)),
            dma((n_gx,)), dma((n_gx,)),
        ],
        compiler_params=pltpu.CompilerParams(
            collective_id=1, has_side_effects=True, vmem_limit_bytes=32 * 1024 * 1024
        ),
    )(conv, small, routed)


def finish_kernel(total, tail, conv_out, lift_out, gain_out, out_out, loss_out):
    scale = tail[32:33, :]
    for chunk in range(total.shape[0]):
        size = total.shape[1]
        conv_out[pl.ds(chunk * size, size), :] = total[chunk].astype(f32) * scale
    lift_out[...] = tail[0:27, :]
    gain_out[...] = tail[27:28, :]
    out_out[...] = tail[28:29, :]
    loss_out[...] = tail[33:34, :]


def finish_call(total, tail):
    vmem = pl.BlockSpec(memory_space=pltpu.VMEM)
    tile = functools.partial(jax.ShapeDtypeStruct, dtype=f32)
    return pl.pallas_call(
        finish_kernel,
        out_shape=(
            tile((total.shape[0] * total.shape[1], 128)),
            tile((27, 128)), tile((1, 128)), tile((1, 128)), tile((1, 128)),
        ),
        in_specs=[vmem] * 2,
        out_specs=(vmem,) * 5,
        compiler_params=pltpu.CompilerParams(vmem_limit_bytes=16 * 1024 * 1024),
    )(total, tail)


def body(
    field, prev_field, diffusivity, velocity, w_lift, norm_gain, w_conv, w_out,
    tile_count, patch_dest, anchor_x, anchor_y,
):
    new_field, routed = route_call(
        tile_count.reshape(1), patch_dest.reshape(2), anchor_x.reshape(2), anchor_y.reshape(2),
        field, prev_field, diffusivity, velocity,
    )
    conv, small = train_call(routed, w_lift, norm_gain[None], w_conv[0], w_out[None])
    entries = w_lift.size + norm_gain.size + w_out.size + lax.axis_size("gx") * w_conv[0].size
    total, tail = reduce_call(conv, small, routed, entries)
    dir_conv, lift, gain, out, loss = finish_call(total, tail)
    return (
        new_field, loss[:, :1].reshape(1, 1, 1), lift, gain.reshape(-1),
        dir_conv.reshape(w_conv.shape), out.reshape(-1),
    )


def solution(mesh):
    tiles = P("ga", "gx", "gy")
    slots = P("ga", "gx", "gy", None)
    in_specs = (
        tiles, tiles, tiles, P(None, "ga", "gx", "gy"), P(), P(), P("gx", None, None), P(),
        tiles, slots, slots, slots,
    )
    out_specs = (tiles, tiles, P(), P(), P("gx", None, None), P())
    return jax.shard_map(body, mesh=mesh, in_specs=in_specs, out_specs=out_specs, check_vma=False)
```

```python
import functools

import jax
import jax.numpy as jnp
from jax import lax
from jax.experimental import pallas as pl
from jax.experimental.pallas import tpu as pltpu
from jax.sharding import PartitionSpec as P

STEPS = 2
PVOX = 1024
CAP = 4
PAIR = 2
ROOT = 0.7978845608028654
CUBE = 0.044715
MESH = pl.DeviceIdType.MESH
f32, bf16 = jnp.float32, jnp.bfloat16


def gelu_both(v):
    v2 = v * v
    t = jnp.tanh(ROOT * (v + CUBE * (v * v2)))
    half = 0.5 * (1.0 + t)
    slope = half + 0.5 * v * (1.0 - t * t) * (ROOT * (1.0 + 3.0 * CUBE * v2))
    return v * half, slope


def z_shifted(block, z_ids):
    up = jnp.where(z_ids == 31, 0.0, pltpu.roll(block, 127, 0))
    down = jnp.where(z_ids == 0, 0.0, pltpu.roll(block, 1, 0))
    return up, down


def move_y(block, by):
    if by == 0:
        return block
    gap = jnp.zeros_like(block[:, :1])
    parts = [block[:, 1:], gap] if by > 0 else [gap, block[:, :-1]]
    return jnp.concatenate(parts, axis=1)


def conv_rows(source, weights, x, sign):
    acc = None
    number = source.shape[1]
    for q in range(3):
        x_in = x + sign * (q - 1)
        if x_in < 0 or x_in > 7:
            continue
        lhs = source[x_in + 1, :, 1:5].reshape(number * 128, 384)
        d = jnp.dot(lhs, weights[q], preferred_element_type=f32).reshape(number, 4, 32, 384)
        for r in range(3):
            piece = move_y(d[:, :, :, r * 128 : (r + 1) * 128], sign * (r - 1))
            acc = piece if acc is None else acc + piece
    return acc.reshape(number, 128, 128)


def lanes_of(shape):
    return lax.broadcasted_iota(jnp.int32, shape, len(shape) - 1)


def group_partners(n_gy, n_ga):
    gy, ga = lax.axis_index("gy"), lax.axis_index("ga")
    for far in range(1, n_gy * n_ga):
        there = (gy + far % n_gy) % n_gy
        across = (ga + far // n_gy) % n_ga
        yield far, {"gy": there, "ga": across}


def line_partners(n_gx):
    gx = lax.axis_index("gx")
    for far in range(1, n_gx):
        yield far, {"gx": (gx + far) % n_gx}


def meet(devices):
    barrier = pltpu.get_barrier_semaphore()
    for device in devices:
        pl.semaphore_signal(barrier, inc=1, device_id=device, device_id_type=MESH)
    return barrier, len(devices)


def several(count, step, carry, at_once=4):
    def run(block, carry):
        for i in range(at_once):
            carry = step(block * at_once + i, carry)
        return carry

    return lax.fori_loop(0, count // at_once, run, carry)


def remote(src, dst, send_sem, recv_sem, device):
    return pltpu.make_async_remote_copy(
        src_ref=src, dst_ref=dst, send_sem=send_sem, recv_sem=recv_sem,
        device_id=device, device_id_type=MESH,
    )


def row_cuts(rows):
    tiles = rows // 16
    ends = [16 * (tiles * i // 4 + (1 if 0 < i < 4 and tiles * i % 4 else 0)) for i in range(5)]
    return [(low, high - low) for low, high in zip(ends, ends[1:])]


def whole_kernel(
    n_gx, n_gy, n_ga, rows, entries,
    count, dest, start_x, start_y, field, prev_field, diffusivity, velocity,
    w_lift, gain, w_conv, w_out,
    new_field, total_out, tail_out, *scratch,
):
    (
        state, later, prev, diff, speed, weights,
        mine, line, z_in, x_out, x_in, y_out, y_in, records,
        wf, wb, lift_rows, vp, gp, nt, nu, lifted, slope1, pre2, dh,
        conv, small, leaf_out, leaf_in, ring, own, other, gathered,
        pieces, from_line_sums, tile_b, from_group, tile_c, from_all,
        load_sem, line_send, line_recv, halo_send, halo_recv,
        ring_send, ring_recv, pair_send, pair_recv, gather_send, gather_recv,
        a_send, a_recv, b_send, b_recv, c_send, c_recv,
    ) = scratch
    gx, gy, ga = lax.axis_index("gx"), lax.axis_index("gy"), lax.axis_index("ga")
    line_id = ga * n_gy + gy
    barrier, expected = meet(
        [device for _, device in line_partners(n_gx)]
        + [device for _, device in group_partners(n_gy, n_ga)]
    )
    size_z, size_x, size_y = prev.shape
    loads = [
        pltpu.make_async_copy(field, state.at[pl.ds(1, size_z)], load_sem.at[0]),
        pltpu.make_async_copy(prev_field, prev, load_sem.at[1]),
        pltpu.make_async_copy(diffusivity, diff, load_sem.at[2]),
        pltpu.make_async_copy(velocity, speed, load_sem.at[3]),
        pltpu.make_async_copy(w_conv, weights, load_sem.at[4]),
    ]
    for load in loads:
        load.start()
    sub8 = lax.broadcasted_iota(jnp.int32, (8, 128), 0)
    lane8 = lanes_of((8, 128))
    xi = lax.broadcasted_iota(jnp.int32, (size_x, 128), 0)
    li = lanes_of((size_x, 128))
    row_y = lax.broadcasted_iota(jnp.int32, (128, 128), 0)
    col = lanes_of((128, 128))
    z_mask = (
        lax.broadcasted_iota(jnp.int32, (size_z, 8, 128), 0) == lanes_of((size_z, 8, 128)) % size_z
    )
    zero_tile = jnp.zeros((size_x, 128), f32)
    for held in (vp, gp, nt, nu, lifted, slope1, dh, conv, small, lift_rows):
        held[...] = jnp.zeros_like(held)
    lift_rows[0:27, :] = w_lift[...].astype(f32)
    lift_weights = lift_rows[...].astype(bf16)
    gain_row = gain[...]
    wo_row = w_out[...].astype(f32)

    def pack_faces(step, cells, high, low):
        x_out[step, 0] = cells[1 : size_z + 1, 0, :]
        x_out[step, 1] = cells[1 : size_z + 1, size_x - 1, :]
        y_out[step, 0] = low
        y_out[step, 1] = high

    def halo_copies(step, cells):
        base = step * 5
        z_src = cells.at[size_z - (size_z - 1) * ga]
        there = {"ga": 1 - ga}
        z_out_copy = remote(
            z_src, z_in.at[step], halo_send.at[base], halo_recv.at[base], there
        )
        copies = [z_out_copy]
        for side in range(2):
            near = (gx + (n_gx - 1 if side == 0 else 1)) % n_gx
            copies.append(remote(
                x_out.at[step, side], x_in.at[step, 1 - side],
                halo_send.at[base + 1 + side], halo_recv.at[base + 1 + side], {"gx": near},
            ))
        for side in range(2):
            near = (gy + (n_gy - 1 if side == 0 else 1)) % n_gy
            copies.append(remote(
                y_out.at[step, side], y_in.at[step, 1 - side],
                halo_send.at[base + 3 + side], halo_recv.at[base + 3 + side], {"gy": near},
            ))
        return copies

    def place(z, cells, high, low):
        high = jnp.where(li == z, pltpu.roll(cells, z + 1, 1), high)
        low = jnp.where(li == z, pltpu.roll(cells, z, 1), low)
        return high, low

    def advance(step, cells, store, pack):
        z_face = z_in[step]
        cells[0] = jnp.where(ga == 1, z_face, 0.0)
        cells[size_z + 1] = jnp.where(ga == 0, z_face, 0.0)

        def layer(z, faces):
            centre = cells[z + 1]
            below = cells[z]
            above = cells[z + 2]
            behind = jnp.where(xi == 0, x_in[step, 0, pl.ds(z, 1), :], pltpu.roll(centre, 1, 0))
            ahead = jnp.where(
                xi == size_x - 1, x_in[step, 1, pl.ds(z, 1), :], pltpu.roll(centre, size_x - 1, 0)
            )
            left = jnp.where(
                li == 0, pltpu.roll(y_in[step, 0], 128 - z, 1), pltpu.roll(centre, 1, 1)
            )
            right = jnp.where(
                li == 127, pltpu.roll(y_in[step, 1], 127 - z, 1), pltpu.roll(centre, 127, 1)
            )
            laplace = above + below + (ahead + behind) + (right + left) - 6.0 * centre
            moved = jnp.zeros_like(centre)
            for d, (low, high) in enumerate(((below, above), (behind, ahead), (left, right))):
                v = speed[d, z]
                moved = moved + (
                    jnp.maximum(v, 0.0) * (centre - low) + jnp.minimum(v, 0.0) * (high - centre)
                )
            result = centre + diff[z] * laplace - moved
            store(z, result)
            return place(z, result, *faces) if pack else faces

        return several(size_z, layer, (zero_tile, zero_tile))

    loads[0].wait()
    high, low = several(
        size_z, lambda z, faces: place(z, state[z + 1], *faces), (zero_tile, zero_tile)
    )
    pack_faces(0, state, high, low)
    loads[1].wait()
    for k in range(2):
        chosen = (row_y == start_y[k] + col // size_z).astype(bf16)
        parts = []
        for source in (0, 1):
            if source == 0:
                window = prev[:, pl.ds(start_x[k], 8), :]
            else:
                window = state[1 : size_z + 1, pl.ds(start_x[k], 8), :]
            spread = jnp.dot(
                window.reshape(size_z * 8, 128).astype(bf16), chosen, preferred_element_type=f32
            ).reshape(size_z, 8, 128)
            parts.append(jnp.sum(jnp.where(z_mask, spread, 0.0), axis=0))
        mine[pl.ds(16 * k, 16), :] = jnp.concatenate(parts, axis=0).astype(bf16)
    goals = [jnp.where(k < count[0], dest[k], -1).astype(f32) for k in range(2)]
    mine[32:48, :] = jnp.concatenate(
        [jnp.full((8, 128), goals[0]), jnp.full((8, 128), goals[1])], axis=0
    ).astype(bf16)
    line[gx] = mine[...]

    pl.semaphore_wait(barrier, expected)
    first = []
    for far, device in line_partners(n_gx):
        copy = remote(mine, line.at[gx], line_send.at[far], line_recv.at[far], device)
        copy.start()
        first.append(copy)
    halos = halo_copies(0, state)
    for copy in halos:
        copy.start()

    loads[4].wait()
    for q in range(3):
        for r in range(3):
            for p in range(3):
                blk = weights[pl.ds(((p * 3 + q) * 3 + r) * 128, 128), :]
                wf[q, pl.ds(p * 128, 128), pl.ds(r * 128, 128)] = blk
                wb[q, pl.ds(p * 128, 128), pl.ds(r * 128, 128)] = blk.astype(f32).T.astype(bf16)

    loads[2].wait()
    loads[3].wait()
    for copy in halos:
        copy.wait_recv()

    def keep(z, value):
        later[z + 1] = value

    high, low = advance(0, state, keep, True)
    pack_faces(1, later, high, low)
    more = halo_copies(1, later)
    for copy in more:
        copy.start()

    for copy in first:
        copy.wait_recv()
    empty = jnp.zeros((16, 128), f32)
    myself = gx.astype(f32)

    def from_line(source, carry):
        rank, picked = carry
        for k in range(2):
            goal = line[source, 32:48, :].astype(f32)[8 * k : 8 * k + 8]
            record = line[source, pl.ds(16 * k, 16), :].astype(f32)
            hit = goal == myself
            picked = tuple(
                jnp.where(jnp.concatenate([hit & (rank == c)] * 2, axis=0), record, old)
                for c, old in enumerate(picked)
            )
            rank = rank + hit.astype(f32)
        return rank, picked

    rank, picked = lax.fori_loop(
        0, n_gx, from_line, (jnp.zeros((8, 128), f32), (empty,) * CAP)
    )
    for c in range(CAP):
        records[pl.ds(16 * c, 16), :] = picked[c]

    z_ids = lax.broadcasted_iota(jnp.int32, (128, 128), 0) % 32

    def first_part(i):
        for slot in range(PAIR):
            u = records[pl.ds(16 * (PAIR * i + slot), 8), :]
            for p in range(3):
                dz = p - 1
                uz = u if dz == 0 else pltpu.roll(u, (-dz) % 128, 1)
                okz = (lane8 % 32 + dz >= 0) & (lane8 % 32 + dz < 32)
                for q in range(3):
                    dx = q - 1
                    ux = uz if dx == 0 else pltpu.roll(uz, (-dx) % 8, 0)
                    okx = (sub8 + dx >= 0) & (sub8 + dx < 8)
                    for r in range(3):
                        dy = r - 1
                        uy = ux if dy == 0 else pltpu.roll(ux, (-32 * dy) % 128, 1)
                        oky = (lane8 // 32 + dy >= 0) & (lane8 // 32 + dy < 4)
                        nu[slot, :, p * 9 + q * 3 + r, :] = jnp.where(okz & okx & oky, uy, 0.0)
            for x in range(8):
                pre = lax.dot_general(
                    nu[slot, x].astype(bf16), lift_weights, (((0,), (0,)), ((), ())), preferred_element_type=f32
                )
                val, slope = gelu_both(pre)
                slope1[slot, x] = slope
                low = val.astype(bf16)
                lifted[slot, x] = low
                wide = low.astype(f32)
                inv = lax.rsqrt(jnp.mean(wide * wide, axis=1, keepdims=True) + 1e-06)
                normed = (wide * inv * gain_row).astype(bf16).astype(f32)
                up, down = z_shifted(normed, z_ids)
                for k, v in enumerate((down, normed, up)):
                    vp[x + 1, slot, 1:5, :, k * 128 : (k + 1) * 128] = v.astype(bf16).reshape(4, 32, 128)
                nt[slot, x + 1] = normed.T.astype(bf16)
        for x in range(8):
            pre2[x] = conv_rows(vp, wf, x, 1)
        for slot in range(PAIR):
            target = records[pl.ds(16 * (PAIR * i + slot) + 8, 8), :]
            loss = dwo = jnp.zeros((1, 128), f32)
            for x in range(8):
                mixed, slope = gelu_both(pre2[x, slot])
                hid = (lifted[slot, x].astype(f32) + mixed).astype(bf16).astype(f32)
                pred = jnp.sum(hid * wo_row, axis=1, keepdims=True)
                row = jnp.sum(jnp.where(sub8 == x, target, 0.0), axis=0, keepdims=True)
                wanted = jnp.broadcast_to(row, (128, 128)).T
                misfit = pred - wanted
                loss = loss + jnp.sum(misfit * misfit, axis=0, keepdims=True)
                dwo = dwo + jnp.sum(hid * misfit, axis=0, keepdims=True)
                d_hid = (misfit * wo_row).astype(bf16)
                dh[slot, x] = d_hid
                g = (d_hid.astype(f32) * slope).astype(bf16).astype(f32)
                up, down = z_shifted(g, z_ids)
                for k, v in enumerate((up, g, down)):
                    gp[x + 1, slot, 1:5, :, k * 128 : (k + 1) * 128] = v.astype(bf16).reshape(4, 32, 128)
            lhs = jnp.concatenate(
                [jnp.concatenate([nt[slot, q + x] for x in range(8)], axis=1) for q in range(3)], axis=0
            )
            for r in range(3):
                rhs = gp[1:9, slot, 2 - r : 6 - r].reshape(1024, 384)
                d = jnp.dot(lhs, rhs, preferred_element_type=f32)
                for q in range(3):
                    for p in range(3):
                        rows = pl.ds(((p * 3 + q) * 3 + r) * 128, 128)
                        piece = d[q * 128 : (q + 1) * 128, p * 128 : (p + 1) * 128]
                        conv[rows, :] += piece.astype(bf16).astype(f32)
            small[28:29, :] += dwo.astype(bf16).astype(f32)
            small[32:33, :] += 0.5 * loss

    def second_part():
        for x in range(8):
            pre2[x] = conv_rows(gp, wb, x, -1)
        for slot in range(PAIR):
            dgain, dwl = jnp.zeros((1, 128), f32), jnp.zeros((32, 128), f32)
            for x in range(8):
                dn = pre2[x, slot].astype(bf16).astype(f32)
                wide = lifted[slot, x].astype(f32)
                inv = lax.rsqrt(jnp.mean(wide * wide, axis=1, keepdims=True) + 1e-06)
                unit = wide * inv
                dgain = dgain + jnp.sum(dn * unit, axis=0, keepdims=True)
                dt = dn * gain_row
                mean = jnp.sum(dt * wide, axis=1, keepdims=True) * (1.0 / 128.0)
                d_low = dh[slot, x].astype(f32) + dt * inv - (inv * inv * inv * mean) * wide
                d_pre = d_low.astype(bf16).astype(f32) * slope1[slot, x]
                dwl = dwl + jnp.dot(nu[slot, x].astype(bf16), d_pre.astype(bf16), preferred_element_type=f32)
            small[0:32, :] += dwl.astype(bf16).astype(f32)
            small[27:28, :] += dgain

    def one_pair(i, carry):
        pl.when(i > 0)(second_part)
        first_part(i)
        return carry

    lax.fori_loop(0, CAP // PAIR, one_pair, 0)

    subs = row_cuts(rows)
    far_side = n_gy // 2
    signs = (1, -1)
    keys = [(0, 0), (1, 2), (0, 1), (1, 3), (0, 2), (1, 0), (0, 3), (1, 1)]
    depth = {(side, part): far_side if part // 2 == side else n_gy - 1 - far_side for side, part in keys}
    share = n_gy * n_ga
    per = 32 // n_gx

    def wrap(index):
        return (index + 2 * n_gy) % n_gy

    def rows_of(index, part):
        low, size = subs[part]
        return pl.ds(pl.multiple_of(wrap(index) * rows + low, 8), size)

    def next_to(side):
        return {"gy": wrap(gy + signs[side])}

    def ring_copy(step, side, part):
        low, size = subs[part]
        if step == 0:
            return remote(
                leaf_out.at[side, pl.ds(low, size)], leaf_in.at[side, pl.ds(low, size)],
                ring_send.at[0, side, part], ring_recv.at[0, side, part], next_to(side),
            )
        return remote(
            ring.at[step - 1, side, pl.ds(low, size)], ring.at[step, side, pl.ds(low, size)],
            ring_send.at[step, side, part], ring_recv.at[step, side, part], next_to(side),
        )

    for side, part in keys:
        low, size = subs[part]
        leaf = rows_of(gy + signs[side] * depth[side, part], part)
        leaf_out[side, pl.ds(low, size), :] = conv[leaf, :].astype(bf16)
    started = []

    def begin(copy):
        copy.start()
        started.append(copy)
        return copy

    flying = {key: begin(ring_copy(0, *key)) for key in keys}
    second_part()

    for k in range(n_gx):
        pieces[k] = jnp.concatenate(
            [small[per * k : per * k + per, :], jnp.zeros((8 - per, 128), f32)], axis=0
        )
    from_line_sums[gx] = pieces[gx]

    line_copies = [
        begin(remote(
            pieces.at[device["gx"]], from_line_sums.at[gx], a_send.at[far], a_recv.at[far], device
        ))
        for far, device in line_partners(n_gx)
    ]

    pairs = {}
    for step in range(far_side):
        for key in keys:
            side, part = key
            low, size = subs[part]
            if step >= depth[key]:
                continue
            flying[key].wait_recv()
            if step + 1 < depth[key]:
                there = rows_of(gy + signs[side] * (depth[key] - 1 - step), part)
                here = pl.ds(low, size)
                came = leaf_in[side, here, :].astype(f32) if step == 0 else ring[step, side, here, :]
                ring[step, side, here, :] = came + conv[there, :]
                flying[key] = begin(ring_copy(step + 1, *key))
            elif step == far_side - 1:
                here = pl.ds(low, size)
                near = depth[1 - side, part] - 1
                own[here, :] = (
                    ring[step, side, here, :] + ring[near, 1 - side, here, :]
                ) + conv[rows_of(gy, part), :]
                pairs[part] = begin(remote(
                    own.at[here], other.at[here], pair_send.at[part], pair_recv.at[part],
                    {"ga": 1 - ga},
                ))

    for copy in line_copies:
        copy.wait_recv()
    piece = lax.fori_loop(0, n_gx, lambda k, acc: acc + from_line_sums[k], jnp.zeros((8, 128), f32))

    def gather_copy(step, side, part):
        low, size = subs[part]
        where = gathered.at[wrap(gy - signs[side] * step), pl.ds(low, size)]
        return remote(
            where, where,
            gather_send.at[step, side, part], gather_recv.at[step, side, part], next_to(side),
        )

    squares = jnp.zeros((1, 128), f32)
    for part in (0, 2, 1, 3):
        low, size = subs[part]
        here = pl.ds(low, size)
        pairs[part].wait_recv()
        total = own[here, :] + other[here, :]
        gathered[gy, here, :] = total.astype(bf16)
        for side in (part // 2, 1 - part // 2):
            flying[side, part] = begin(gather_copy(0, side, part))
        squares = squares + jnp.sum(total * total, axis=0, keepdims=True)
    squares = jnp.where(ga == 0, squares, 0.0)
    tile_b[...] = jnp.where(sub8 < per, piece, jnp.where(sub8 == per, squares, 0.0))
    from_group[line_id] = tile_b[...]
    group_copies = [
        begin(remote(tile_b, from_group.at[line_id], b_send.at[far], b_recv.at[far], device))
        for far, device in group_partners(n_gy, n_ga)
    ]

    for copy in more:
        copy.wait_recv()

    def emit(z, value):
        new_field[z] = value

    advance(1, later, emit, False)
    for step in range(far_side):
        for key in keys:
            if step >= depth[key]:
                continue
            flying[key].wait_recv()
            if step + 1 < depth[key]:
                flying[key] = begin(gather_copy(step + 1, *key))
        if step == 1:
            for copy in group_copies:
                copy.wait_recv()
            summed = lax.fori_loop(
                0, share, lambda k, acc: acc + from_group[k], jnp.zeros((8, 128), f32)
            )
            tile_c[...] = summed
            from_all[gx] = summed
            last_copies = [
                begin(remote(tile_c, from_all.at[gx], c_send.at[far], c_recv.at[far], device))
                for far, device in line_partners(n_gx)
            ]

    total_out[...] = gathered[...]
    for copy in last_copies:
        copy.wait_recv()
    shared = jnp.concatenate([from_all[k, 0:per, :] for k in range(n_gx)], axis=0)
    conv_squares = lax.fori_loop(
        0, n_gx, lambda k, acc: acc + from_all[k], jnp.zeros((8, 128), f32)
    )[per : per + 1]
    all_squares = jnp.sum(
        conv_squares + jnp.sum(shared * shared, axis=0, keepdims=True), axis=1, keepdims=True
    )
    scale = lax.rsqrt(all_squares / entries + 1e-06)
    tail_out[0:32, :] = shared * scale
    loss = small[32:33, :] / (PVOX * jnp.maximum(rank[0:1], 1.0))
    tail_out[32:40, :] = jnp.where(sub8 == 0, jnp.broadcast_to(scale, (8, 128)), loss)
    for copy in started + first + halos + more:
        copy.wait_send()


def whole_call(
    count, dest, start_x, start_y, field, prev_field, diffusivity, velocity,
    w_lift, gain, w_conv, w_out, entries,
):
    n_gx, n_gy, n_ga = (lax.axis_size(name) for name in ("gx", "gy", "ga"))
    size_z, size_x, size_y = field.shape
    share = n_gy * n_ga
    rows = w_conv.shape[0] // n_gy
    far_side = n_gy // 2
    smem = pl.BlockSpec(memory_space=pltpu.SMEM)
    vmem = pl.BlockSpec(memory_space=pltpu.VMEM)
    hbm = pl.BlockSpec(memory_space=pl.ANY)
    dma = pltpu.SemaphoreType.DMA
    held = pltpu.VMEM
    return pl.pallas_call(
        functools.partial(whole_kernel, n_gx, n_gy, n_ga, rows, entries),
        out_shape=(
            jax.ShapeDtypeStruct(field.shape, f32),
            jax.ShapeDtypeStruct((n_gy, rows, 128), bf16),
            jax.ShapeDtypeStruct((40, 128), f32),
        ),
        in_specs=[smem] * 4 + [hbm] * 4 + [vmem, vmem, hbm, vmem],
        out_specs=(vmem,) * 3,
        scratch_shapes=[
            held((size_z + 2, size_x, size_y), f32),
            held((size_z + 2, size_x, size_y), f32),
            held((size_z, size_x, size_y), f32),
            held((size_z, size_x, size_y), f32),
            held((3, size_z, size_x, size_y), f32),
            held(w_conv.shape, bf16),
            held((48, 128), bf16),
            held((n_gx, 48, 128), bf16),
            held((STEPS, size_x, 128), f32),
            held((STEPS, 2, size_z, 128), f32),
            held((STEPS, 2, size_z, 128), f32),
            held((STEPS, 2, size_x, 128), f32),
            held((STEPS, 2, size_x, 128), f32),
            held((16 * CAP, 128), f32),
            held((3, 384, 384), bf16),
            held((3, 384, 384), bf16),
            held((32, 128), f32),
            held((10, PAIR, 6, 32, 384), bf16),
            held((10, PAIR, 6, 32, 384), bf16),
            held((PAIR, 10, 128, 128), bf16),
            held((PAIR, 8, 32, 128), f32),
            held((PAIR, 8, 128, 128), bf16),
            held((PAIR, 8, 128, 128), f32),
            held((8, PAIR, 128, 128), f32),
            held((PAIR, 8, 128, 128), bf16),
            held(w_conv.shape, f32),
            held((40, 128), f32),
            held((2, rows, 128), bf16),
            held((2, rows, 128), bf16),
            held((far_side, 2, rows, 128), f32),
            held((rows, 128), f32),
            held((rows, 128), f32),
            held((n_gy, rows, 128), bf16),
            held((n_gx, 8, 128), f32),
            held((n_gx, 8, 128), f32),
            held((8, 128), f32),
            held((share, 8, 128), f32),
            held((8, 128), f32),
            held((n_gx, 8, 128), f32),
            dma((5,)),
            dma((n_gx,)), dma((n_gx,)),
            dma((STEPS * 5,)), dma((STEPS * 5,)),
            dma((far_side, 2, 4)), dma((far_side, 2, 4)),
            dma((4,)), dma((4,)),
            dma((far_side, 2, 4)), dma((far_side, 2, 4)),
            dma((n_gx,)), dma((n_gx,)),
            dma((share,)), dma((share,)),
            dma((n_gx,)), dma((n_gx,)),
        ],
        compiler_params=pltpu.CompilerParams(
            collective_id=0, has_side_effects=True, vmem_limit_bytes=56 * 1024 * 1024
        ),
    )(
        count, dest, start_x, start_y, field, prev_field, diffusivity, velocity,
        w_lift, gain, w_conv, w_out,
    )


def finish_kernel(total, tail, cells, conv_out, lift_out, gain_out, out_out, loss_out, cells_out):
    cells_out[...] = cells[...]
    scale = tail[32:33, :]
    for chunk in range(total.shape[0]):
        size = total.shape[1]
        conv_out[pl.ds(chunk * size, size), :] = total[chunk].astype(f32) * scale
    lift_out[...] = tail[0:27, :]
    gain_out[...] = tail[27:28, :]
    out_out[...] = tail[28:29, :]
    loss_out[...] = tail[33:34, :]


def finish_call(total, tail, cells):
    vmem = pl.BlockSpec(memory_space=pltpu.VMEM)
    tile = functools.partial(jax.ShapeDtypeStruct, dtype=f32)
    return pl.pallas_call(
        finish_kernel,
        out_shape=(
            tile((total.shape[0] * total.shape[1], 128)),
            tile((27, 128)), tile((1, 128)), tile((1, 128)), tile((1, 128)),
            tile(cells.shape),
        ),
        in_specs=[vmem] * 3,
        out_specs=(vmem,) * 6,
        compiler_params=pltpu.CompilerParams(vmem_limit_bytes=56 * 1024 * 1024),
    )(total, tail, cells)


def body(
    field, prev_field, diffusivity, velocity, w_lift, norm_gain, w_conv, w_out,
    tile_count, patch_dest, anchor_x, anchor_y,
):
    entries = w_lift.size + norm_gain.size + w_out.size + lax.axis_size("gx") * w_conv[0].size
    stepped, total, tail = whole_call(
        tile_count.reshape(1), patch_dest.reshape(2), anchor_x.reshape(2), anchor_y.reshape(2),
        field, prev_field, diffusivity, velocity,
        w_lift, norm_gain[None], w_conv[0], w_out[None], entries,
    )
    dir_conv, lift, gain, out, loss, new_field = finish_call(total, tail, stepped)
    return (
        new_field, loss[:, :1].reshape(1, 1, 1), lift, gain.reshape(-1),
        dir_conv.reshape(w_conv.shape), out.reshape(-1),
    )


def solution(mesh):
    tiles = P("ga", "gx", "gy")
    slots = P("ga", "gx", "gy", None)
    in_specs = (
        tiles, tiles, tiles, P(None, "ga", "gx", "gy"), P(), P(), P("gx", None, None), P(),
        tiles, slots, slots, slots,
    )
    out_specs = (tiles, tiles, P(), P(), P("gx", None, None), P())
    return jax.shard_map(body, mesh=mesh, in_specs=in_specs, out_specs=out_specs, check_vma=False)
```

```python
import functools

import jax
import jax.numpy as jnp
from jax import lax
from jax.experimental import pallas as pl
from jax.experimental.pallas import tpu as pltpu
from jax.sharding import PartitionSpec as P

STEPS = 2
PVOX = 1024
CAP = 4
PAIR = 2
BEFORE = 5
ROOT = 0.7978845608028654
CUBE = 0.044715
MESH = pl.DeviceIdType.MESH
f32, bf16 = jnp.float32, jnp.bfloat16


def gelu_both(v):
    v2 = v * v
    t = jnp.tanh(ROOT * (v + CUBE * (v * v2)))
    half = 0.5 * (1.0 + t)
    slope = half + 0.5 * v * (1.0 - t * t) * (ROOT * (1.0 + 3.0 * CUBE * v2))
    return v * half, slope


def z_shifted(block, z_ids):
    up = jnp.where(z_ids == 31, 0.0, pltpu.roll(block, 127, 0))
    down = jnp.where(z_ids == 0, 0.0, pltpu.roll(block, 1, 0))
    return up, down


def move_y(block, by):
    if by == 0:
        return block
    gap = jnp.zeros_like(block[:, :1])
    parts = [block[:, 1:], gap] if by > 0 else [gap, block[:, :-1]]
    return jnp.concatenate(parts, axis=1)


def conv_rows(source, weights, x, sign):
    acc = None
    number = PAIR
    for q in range(3):
        x_in = x + sign * (q - 1)
        if x_in < 0 or x_in > 7:
            continue
        lhs = source[x_in + 1, :, 1:5].reshape(number * 128, 384)
        d = jnp.dot(lhs, weights[q], preferred_element_type=f32).reshape(number, 4, 32, 384)
        for r in range(3):
            piece = move_y(d[:, :, :, r * 128 : (r + 1) * 128], sign * (r - 1))
            acc = piece if acc is None else acc + piece
    return acc.reshape(number, 128, 128)


def lanes_of(shape):
    return lax.broadcasted_iota(jnp.int32, shape, len(shape) - 1)


def group_partners(n_gy, n_ga):
    gy, ga = lax.axis_index("gy"), lax.axis_index("ga")
    for far in range(1, n_gy * n_ga):
        there = (gy + far % n_gy) % n_gy
        across = (ga + far // n_gy) % n_ga
        yield far, {"gy": there, "ga": across}


def line_partners(n_gx):
    gx = lax.axis_index("gx")
    for far in range(1, n_gx):
        yield far, {"gx": (gx + far) % n_gx}


def meet(devices):
    barrier = pltpu.get_barrier_semaphore()
    for device in devices:
        pl.semaphore_signal(barrier, inc=1, device_id=device, device_id_type=MESH)
    return barrier, len(devices)


def several(count, step, carry, at_once=4):
    def run(block, carry):
        for i in range(at_once):
            carry = step(block * at_once + i, carry)
        return carry

    return lax.fori_loop(0, count // at_once, run, carry)


def remote(src, dst, send_sem, recv_sem, device):
    return pltpu.make_async_remote_copy(
        src_ref=src, dst_ref=dst, send_sem=send_sem, recv_sem=recv_sem,
        device_id=device, device_id_type=MESH,
    )


def row_cuts(rows):
    tiles = rows // 16
    ends = [16 * (tiles * i // 4 + (1 if 0 < i < 4 and tiles * i % 4 else 0)) for i in range(5)]
    return [(low, high - low) for low, high in zip(ends, ends[1:])]


def whole_kernel(
    n_gx, n_gy, n_ga, rows, entries,
    count_in, dest_in, start_x_in, start_y_in, field, prev_field, diffusivity, velocity,
    w_lift, gain, w_conv, w_out,
    new_field, total_out, tail_out, *scratch,
):
    (
        state, later, prev, diff, speed, weights,
        mine, line, z_in, x_out, x_in, y_out, y_in, records,
        wf, wb, lift_rows, vp, gp, nt, nu, lifted, slope1, pre2, dh,
        conv, small, leaf_out, leaf_in, ring, own, other, gathered,
        pieces, from_line_sums, tile_b, from_group, tile_c, from_all,
        load_sem, line_send, line_recv, halo_send, halo_recv,
        ring_send, ring_recv, pair_send, pair_recv, gather_send, gather_recv,
        a_send, a_recv, b_send, b_recv, c_send, c_recv,
        count, dest, start_x, start_y,
    ) = scratch
    gx, gy, ga = lax.axis_index("gx"), lax.axis_index("gy"), lax.axis_index("ga")
    line_id = ga * n_gy + gy
    size_z, size_x, size_y = prev.shape
    loads = [
        pltpu.make_async_copy(field, state.at[pl.ds(1, size_z)], load_sem.at[0]),
        pltpu.make_async_copy(prev_field, prev, load_sem.at[1]),
        pltpu.make_async_copy(diffusivity, diff, load_sem.at[2]),
        pltpu.make_async_copy(velocity, speed, load_sem.at[3]),
        pltpu.make_async_copy(w_conv, weights, load_sem.at[4]),
    ]
    loads += [
        pltpu.make_async_copy(source, held, load_sem.at[5 + i])
        for i, (source, held) in enumerate(
            ((count_in, count), (dest_in, dest), (start_x_in, start_x), (start_y_in, start_y))
        )
    ]
    for load in loads:
        load.start()
    barrier, expected = meet(
        [device for _, device in line_partners(n_gx)]
        + [device for _, device in group_partners(n_gy, n_ga)]
    )
    sub8 = lax.broadcasted_iota(jnp.int32, (8, 128), 0)
    lane8 = lanes_of((8, 128))
    xi = lax.broadcasted_iota(jnp.int32, (size_x, 128), 0)
    li = lanes_of((size_x, 128))
    row_y = lax.broadcasted_iota(jnp.int32, (128, 128), 0)
    col = lanes_of((128, 128))
    z_mask = (
        lax.broadcasted_iota(jnp.int32, (size_z, 8, 128), 0) == lanes_of((size_z, 8, 128)) % size_z
    )
    zero_tile = jnp.zeros((size_x, 128), f32)

    def pack_faces(step, cells, high, low):
        x_out[step, 0] = cells[1 : size_z + 1, 0, :]
        x_out[step, 1] = cells[1 : size_z + 1, size_x - 1, :]
        y_out[step, 0] = low
        y_out[step, 1] = high

    def halo_copies(step, cells):
        base = step * 5
        z_src = cells.at[size_z - (size_z - 1) * ga]
        there = {"ga": 1 - ga}
        z_out_copy = remote(
            z_src, z_in.at[step], halo_send.at[base], halo_recv.at[base], there
        )
        copies = [z_out_copy]
        for side in range(2):
            near = (gx + (n_gx - 1 if side == 0 else 1)) % n_gx
            copies.append(remote(
                x_out.at[step, side], x_in.at[step, 1 - side],
                halo_send.at[base + 1 + side], halo_recv.at[base + 1 + side], {"gx": near},
            ))
        for side in range(2):
            near = (gy + (n_gy - 1 if side == 0 else 1)) % n_gy
            copies.append(remote(
                y_out.at[step, side], y_in.at[step, 1 - side],
                halo_send.at[base + 3 + side], halo_recv.at[base + 3 + side], {"gy": near},
            ))
        return copies

    def place(z, cells, high, low):
        high = jnp.where(li == z, pltpu.roll(cells, z + 1, 1), high)
        low = jnp.where(li == z, pltpu.roll(cells, z, 1), low)
        return high, low

    def advance(step, cells, store, pack):
        z_face = z_in[step]
        cells[0] = jnp.where(ga == 1, z_face, 0.0)
        cells[size_z + 1] = jnp.where(ga == 0, z_face, 0.0)

        def layer(z, faces):
            centre = cells[z + 1]
            below = cells[z]
            above = cells[z + 2]
            behind = jnp.where(xi == 0, x_in[step, 0, pl.ds(z, 1), :], pltpu.roll(centre, 1, 0))
            ahead = jnp.where(
                xi == size_x - 1, x_in[step, 1, pl.ds(z, 1), :], pltpu.roll(centre, size_x - 1, 0)
            )
            left = jnp.where(
                li == 0, pltpu.roll(y_in[step, 0], 128 - z, 1), pltpu.roll(centre, 1, 1)
            )
            right = jnp.where(
                li == 127, pltpu.roll(y_in[step, 1], 127 - z, 1), pltpu.roll(centre, 127, 1)
            )
            laplace = above + below + (ahead + behind) + (right + left) - 6.0 * centre
            moved = jnp.zeros_like(centre)
            for d, (low, high) in enumerate(((below, above), (behind, ahead), (left, right))):
                v = speed[d, z]
                moved = moved + (
                    jnp.maximum(v, 0.0) * (centre - low) + jnp.minimum(v, 0.0) * (high - centre)
                )
            result = centre + diff[z] * laplace - moved
            store(z, result)
            return place(z, result, *faces) if pack else faces

        return several(size_z, layer, (zero_tile, zero_tile))

    loads[0].wait()
    high, low = several(
        size_z, lambda z, faces: place(z, state[z + 1], *faces), (zero_tile, zero_tile)
    )
    pack_faces(0, state, high, low)
    loads[1].wait()
    for load in loads[5:]:
        load.wait()
    for k in range(2):
        chosen = (row_y == start_y[k] + col // size_z).astype(bf16)
        parts = []
        for source in (0, 1):
            if source == 0:
                window = prev[:, pl.ds(start_x[k], 8), :]
            else:
                window = state[1 : size_z + 1, pl.ds(start_x[k], 8), :]
            spread = jnp.dot(
                window.reshape(size_z * 8, 128).astype(bf16), chosen, preferred_element_type=f32
            ).reshape(size_z, 8, 128)
            parts.append(jnp.sum(jnp.where(z_mask, spread, 0.0), axis=0))
        mine[pl.ds(16 * k, 16), :] = jnp.concatenate(parts, axis=0).astype(bf16)
    goals = [jnp.where(k < count[0], dest[k], -1).astype(f32) for k in range(2)]
    mine[32:48, :] = jnp.concatenate(
        [jnp.full((8, 128), goals[0]), jnp.full((8, 128), goals[1])], axis=0
    ).astype(bf16)
    line[gx] = mine[...]

    pl.semaphore_wait(barrier, expected)
    first = []
    for far, device in line_partners(n_gx):
        copy = remote(mine, line.at[gx], line_send.at[far], line_recv.at[far], device)
        copy.start()
        first.append(copy)
    halos = halo_copies(0, state)
    for copy in halos:
        copy.start()

    for held in (nu, conv, small, lift_rows):
        held[...] = jnp.zeros_like(held)
    for edge in (0, 5):
        gp[:, :, :, edge] = jnp.zeros_like(gp[:, :, :, edge])
    for edge in (0, 9):
        nt[:, edge] = jnp.zeros_like(nt[:, edge])
    lift_rows[0:27, :] = w_lift[...].astype(f32)
    lift_weights = lift_rows[...].astype(bf16)
    gain_row = gain[...]
    wo_row = w_out[...].astype(f32)

    loads[4].wait()
    for q in range(3):
        for r in range(3):
            for p in range(3):
                blk = weights[pl.ds(((p * 3 + q) * 3 + r) * 128, 128), :]
                wf[q, pl.ds(p * 128, 128), pl.ds(r * 128, 128)] = blk
                wb[q, pl.ds(p * 128, 128), pl.ds(r * 128, 128)] = blk.astype(f32).T.astype(bf16)

    loads[2].wait()
    loads[3].wait()
    for copy in halos:
        copy.wait_recv()

    def keep(z, value):
        later[z + 1] = value

    high, low = advance(0, state, keep, True)
    pack_faces(1, later, high, low)
    more = halo_copies(1, later)
    for copy in more:
        copy.start()

    for copy in first:
        copy.wait_recv()
    empty = jnp.zeros((16, 128), f32)
    myself = gx.astype(f32)

    def from_line(source, carry):
        rank, picked = carry
        for k in range(2):
            goal = line[source, 32:48, :].astype(f32)[8 * k : 8 * k + 8]
            record = line[source, pl.ds(16 * k, 16), :].astype(f32)
            hit = goal == myself
            picked = tuple(
                jnp.where(jnp.concatenate([hit & (rank == c)] * 2, axis=0), record, old)
                for c, old in enumerate(picked)
            )
            rank = rank + hit.astype(f32)
        return rank, picked

    rank, picked = lax.fori_loop(
        0, n_gx, from_line, (jnp.zeros((8, 128), f32), (empty,) * CAP)
    )
    for c in range(CAP):
        records[pl.ds(16 * c, 16), :] = picked[c]

    z_ids = lax.broadcasted_iota(jnp.int32, (128, 128), 0) % 32

    def first_part(i):
        for slot in range(PAIR):
            u = records[pl.ds(16 * (PAIR * i + slot), 8), :]
            for p in range(3):
                dz = p - 1
                uz = u if dz == 0 else pltpu.roll(u, (-dz) % 128, 1)
                okz = (lane8 % 32 + dz >= 0) & (lane8 % 32 + dz < 32)
                for q in range(3):
                    dx = q - 1
                    ux = uz if dx == 0 else pltpu.roll(uz, (-dx) % 8, 0)
                    okx = (sub8 + dx >= 0) & (sub8 + dx < 8)
                    for r in range(3):
                        dy = r - 1
                        uy = ux if dy == 0 else pltpu.roll(ux, (-32 * dy) % 128, 1)
                        oky = (lane8 // 32 + dy >= 0) & (lane8 // 32 + dy < 4)
                        nu[i, slot, :, p * 9 + q * 3 + r, :] = jnp.where(okz & okx & oky, uy, 0.0)
            for x in range(8):
                pre = lax.dot_general(
                    nu[i, slot, x].astype(bf16), lift_weights, (((0,), (0,)), ((), ())), preferred_element_type=f32
                )
                val, slope = gelu_both(pre)
                slope1[i, slot, x] = slope
                low = val.astype(bf16)
                lifted[i, slot, x] = low
                wide = low.astype(f32)
                inv = lax.rsqrt(jnp.mean(wide * wide, axis=1, keepdims=True) + 1e-06)
                normed = (wide * inv * gain_row).astype(bf16).astype(f32)
                up, down = z_shifted(normed, z_ids)
                for k, v in enumerate((down, normed, up)):
                    vp[x + 1, slot, 1:5, :, k * 128 : (k + 1) * 128] = v.astype(bf16).reshape(4, 32, 128)
                nt[slot, x + 1] = normed.T.astype(bf16)
        for x in range(8):
            pre2[x] = conv_rows(vp, wf, x, 1)
        for slot in range(PAIR):
            target = records[pl.ds(16 * (PAIR * i + slot) + 8, 8), :]
            loss = dwo = jnp.zeros((1, 128), f32)
            for x in range(8):
                mixed, slope = gelu_both(pre2[x, slot])
                hid = (lifted[i, slot, x].astype(f32) + mixed).astype(bf16).astype(f32)
                pred = jnp.sum(hid * wo_row, axis=1, keepdims=True)
                row = jnp.sum(jnp.where(sub8 == x, target, 0.0), axis=0, keepdims=True)
                wanted = jnp.broadcast_to(row, (128, 128)).T
                misfit = pred - wanted
                loss = loss + jnp.sum(misfit * misfit, axis=0, keepdims=True)
                dwo = dwo + jnp.sum(hid * misfit, axis=0, keepdims=True)
                d_hid = (misfit * wo_row).astype(bf16)
                dh[i, slot, x] = d_hid
                g = (d_hid.astype(f32) * slope).astype(bf16).astype(f32)
                up, down = z_shifted(g, z_ids)
                for k, v in enumerate((up, g, down)):
                    gp[i, x + 1, slot, 1:5, :, k * 128 : (k + 1) * 128] = v.astype(bf16).reshape(4, 32, 128)
            lhs = jnp.concatenate(
                [jnp.concatenate([nt[slot, q + x] for x in range(8)], axis=1) for q in range(3)], axis=0
            )
            for r in range(3):
                rhs = gp[i, 1:9, slot, 2 - r : 6 - r].reshape(1024, 384)
                d = jnp.dot(lhs, rhs, preferred_element_type=f32)
                for q in range(3):
                    for p in range(3):
                        rows = pl.ds(((p * 3 + q) * 3 + r) * 128, 128)
                        piece = d[q * 128 : (q + 1) * 128, p * 128 : (p + 1) * 128]
                        conv[rows, :] += piece.astype(bf16).astype(f32)
            small[28:29, :] += dwo.astype(bf16).astype(f32)
            small[32:33, :] += 0.5 * loss

    def one_pair(i, carry):
        first_part(i)
        return carry

    lax.fori_loop(0, CAP // PAIR, one_pair, 0)

    subs = row_cuts(rows)
    far_side = n_gy // 2
    signs = (1, -1)
    keys = [(0, 0), (1, 2), (0, 1), (1, 3), (0, 2), (1, 0), (0, 3), (1, 1)]
    depth = {(side, part): far_side if part // 2 == side else n_gy - 1 - far_side for side, part in keys}
    share = n_gy * n_ga
    per = 32 // n_gx

    def wrap(index):
        return (index + 2 * n_gy) % n_gy

    def rows_of(index, part):
        low, size = subs[part]
        return pl.ds(pl.multiple_of(wrap(index) * rows + low, 8), size)

    def next_to(side):
        return {"gy": wrap(gy + signs[side])}

    def ring_copy(step, side, part):
        low, size = subs[part]
        if step == 0:
            return remote(
                leaf_out.at[side, pl.ds(low, size)], leaf_in.at[side, pl.ds(low, size)],
                ring_send.at[0, side, part], ring_recv.at[0, side, part], next_to(side),
            )
        return remote(
            ring.at[step - 1, side, pl.ds(low, size)], ring.at[step, side, pl.ds(low, size)],
            ring_send.at[step, side, part], ring_recv.at[step, side, part], next_to(side),
        )

    for side, part in keys:
        low, size = subs[part]
        leaf = rows_of(gy + signs[side] * depth[side, part], part)
        leaf_out[side, pl.ds(low, size), :] = conv[leaf, :].astype(bf16)
    started = []

    def begin(copy):
        copy.start()
        started.append(copy)
        return copy

    line_copies = []

    def backward_steps():
        dgain = jnp.zeros((1, 128), f32)
        for pair in range(CAP // PAIR):
            dwl = [jnp.zeros((32, 128), f32)] * PAIR
            for x in range(8):
                both = conv_rows(gp.at[pair], wb, x, -1)
                for slot in range(PAIR):
                    dn = both[slot].astype(bf16).astype(f32)
                    wide = lifted[pair, slot, x].astype(f32)
                    inv = lax.rsqrt(jnp.mean(wide * wide, axis=1, keepdims=True) + 1e-06)
                    dgain = dgain + jnp.sum(dn * (wide * inv), axis=0, keepdims=True)
                    dt = dn * gain_row
                    mean = jnp.sum(dt * wide, axis=1, keepdims=True) * (1.0 / 128.0)
                    d_low = dh[pair, slot, x].astype(f32) + dt * inv - (inv * inv * inv * mean) * wide
                    d_pre = d_low.astype(bf16).astype(f32) * slope1[pair, slot, x]
                    dwl[slot] = dwl[slot] + jnp.dot(
                        nu[pair, slot, x].astype(bf16), d_pre.astype(bf16), preferred_element_type=f32
                    )
                yield
            for part in dwl:
                small[0:32, :] += part.astype(bf16).astype(f32)
        small[27:28, :] += dgain
        for k in range(n_gx):
            pieces[k] = jnp.concatenate(
                [small[per * k : per * k + per, :], jnp.zeros((8 - per, 128), f32)], axis=0
            )
        from_line_sums[gx] = pieces[gx]

        line_copies.extend(
            begin(remote(
                pieces.at[device["gx"]], from_line_sums.at[gx], a_send.at[far], a_recv.at[far], device
            ))
            for far, device in line_partners(n_gx)
        )
        yield

    flying = {key: begin(ring_copy(0, *key)) for key in keys}
    backward = backward_steps()
    for _ in range(BEFORE):
        next(backward)

    pairs = {}
    for step in range(far_side):
        for key in keys:
            side, part = key
            low, size = subs[part]
            if step >= depth[key]:
                continue
            flying[key].wait_recv()
            if step + 1 < depth[key]:
                there = rows_of(gy + signs[side] * (depth[key] - 1 - step), part)
                here = pl.ds(low, size)
                came = leaf_in[side, here, :].astype(f32) if step == 0 else ring[step, side, here, :]
                ring[step, side, here, :] = came + conv[there, :]
                flying[key] = begin(ring_copy(step + 1, *key))
            elif step == far_side - 1:
                here = pl.ds(low, size)
                near = depth[1 - side, part] - 1
                own[here, :] = (
                    ring[step, side, here, :] + ring[near, 1 - side, here, :]
                ) + conv[rows_of(gy, part), :]
                pairs[part] = begin(remote(
                    own.at[here], other.at[here], pair_send.at[part], pair_recv.at[part],
                    {"ga": 1 - ga},
                ))
            next(backward, None)

    for copy in line_copies:
        copy.wait_recv()
    piece = lax.fori_loop(0, n_gx, lambda k, acc: acc + from_line_sums[k], jnp.zeros((8, 128), f32))

    def gather_copy(step, side, part):
        low, size = subs[part]
        where = gathered.at[wrap(gy - signs[side] * step), pl.ds(low, size)]
        return remote(
            where, where,
            gather_send.at[step, side, part], gather_recv.at[step, side, part], next_to(side),
        )

    squares = jnp.zeros((1, 128), f32)
    for part in (0, 2, 1, 3):
        low, size = subs[part]
        here = pl.ds(low, size)
        pairs[part].wait_recv()
        total = own[here, :] + other[here, :]
        gathered[gy, here, :] = total.astype(bf16)
        for side in (part // 2, 1 - part // 2):
            flying[side, part] = begin(gather_copy(0, side, part))
        squares = squares + jnp.sum(total * total, axis=0, keepdims=True)
    squares = jnp.where(ga == 0, squares, 0.0)
    tile_b[...] = jnp.where(sub8 < per, piece, jnp.where(sub8 == per, squares, 0.0))
    from_group[line_id] = tile_b[...]
    group_copies = [
        begin(remote(tile_b, from_group.at[line_id], b_send.at[far], b_recv.at[far], device))
        for far, device in group_partners(n_gy, n_ga)
    ]

    for copy in more:
        copy.wait_recv()

    def emit(z, value):
        prev[z] = value

    advance(1, later, emit, False)
    leave = [pltpu.make_async_copy(prev, new_field, load_sem.at[0])]
    leave[0].start()
    for step in range(far_side):
        for key in keys:
            if step >= depth[key]:
                continue
            flying[key].wait_recv()
            if step + 1 < depth[key]:
                flying[key] = begin(gather_copy(step + 1, *key))
        if step == 1:
            for copy in group_copies:
                copy.wait_recv()
            summed = lax.fori_loop(
                0, share, lambda k, acc: acc + from_group[k], jnp.zeros((8, 128), f32)
            )
            tile_c[...] = summed
            from_all[gx] = summed
            last_copies = [
                begin(remote(tile_c, from_all.at[gx], c_send.at[far], c_recv.at[far], device))
                for far, device in line_partners(n_gx)
            ]

    leave.append(pltpu.make_async_copy(gathered, total_out, load_sem.at[1]))
    leave[1].start()
    for copy in last_copies:
        copy.wait_recv()
    shared = jnp.concatenate([from_all[k, 0:per, :] for k in range(n_gx)], axis=0)
    conv_squares = lax.fori_loop(
        0, n_gx, lambda k, acc: acc + from_all[k], jnp.zeros((8, 128), f32)
    )[per : per + 1]
    all_squares = jnp.sum(
        conv_squares + jnp.sum(shared * shared, axis=0, keepdims=True), axis=1, keepdims=True
    )
    scale = lax.rsqrt(all_squares / entries + 1e-06)
    tail_out[0:32, :] = shared * scale
    loss = small[32:33, :] / (PVOX * jnp.maximum(rank[0:1], 1.0))
    tail_out[32:40, :] = jnp.where(sub8 == 0, jnp.broadcast_to(scale, (8, 128)), loss)
    for copy in leave:
        copy.wait()
    for copy in started + first + halos + more:
        copy.wait_send()


def whole_call(
    count, dest, start_x, start_y, field, prev_field, diffusivity, velocity,
    w_lift, gain, w_conv, w_out, entries,
):
    n_gx, n_gy, n_ga = (lax.axis_size(name) for name in ("gx", "gy", "ga"))
    size_z, size_x, size_y = field.shape
    share = n_gy * n_ga
    rows = w_conv.shape[0] // n_gy
    far_side = n_gy // 2
    vmem = pl.BlockSpec(memory_space=pltpu.VMEM)
    hbm = pl.BlockSpec(memory_space=pl.ANY)
    dma = pltpu.SemaphoreType.DMA
    held = pltpu.VMEM
    return pl.pallas_call(
        functools.partial(whole_kernel, n_gx, n_gy, n_ga, rows, entries),
        out_shape=(
            jax.ShapeDtypeStruct(field.shape, f32),
            jax.ShapeDtypeStruct((n_gy, rows, 128), bf16),
            jax.ShapeDtypeStruct((40, 128), f32),
        ),
        in_specs=[hbm] * 8 + [vmem, vmem, hbm, vmem],
        out_specs=(hbm, hbm, vmem),
        scratch_shapes=[
            held((size_z + 2, size_x, size_y), f32),
            held((size_z + 2, size_x, size_y), f32),
            held((size_z, size_x, size_y), f32),
            held((size_z, size_x, size_y), f32),
            held((3, size_z, size_x, size_y), f32),
            held(w_conv.shape, bf16),
            held((48, 128), bf16),
            held((n_gx, 48, 128), bf16),
            held((STEPS, size_x, 128), f32),
            held((STEPS, 2, size_z, 128), f32),
            held((STEPS, 2, size_z, 128), f32),
            held((STEPS, 2, size_x, 128), f32),
            held((STEPS, 2, size_x, 128), f32),
            held((16 * CAP, 128), f32),
            held((3, 384, 384), bf16),
            held((3, 384, 384), bf16),
            held((32, 128), f32),
            held((10, PAIR, 6, 32, 384), bf16),
            held((CAP // PAIR, 10, PAIR, 6, 32, 384), bf16),
            held((PAIR, 10, 128, 128), bf16),
            held((CAP // PAIR, PAIR, 8, 32, 128), f32),
            held((CAP // PAIR, PAIR, 8, 128, 128), bf16),
            held((CAP // PAIR, PAIR, 8, 128, 128), f32),
            held((8, PAIR, 128, 128), f32),
            held((CAP // PAIR, PAIR, 8, 128, 128), bf16),
            held(w_conv.shape, f32),
            held((40, 128), f32),
            held((2, rows, 128), bf16),
            held((2, rows, 128), bf16),
            held((far_side, 2, rows, 128), f32),
            held((rows, 128), f32),
            held((rows, 128), f32),
            held((n_gy, rows, 128), bf16),
            held((n_gx, 8, 128), f32),
            held((n_gx, 8, 128), f32),
            held((8, 128), f32),
            held((share, 8, 128), f32),
            held((8, 128), f32),
            held((n_gx, 8, 128), f32),
            dma((9,)),
            dma((n_gx,)), dma((n_gx,)),
            dma((STEPS * 5,)), dma((STEPS * 5,)),
            dma((far_side, 2, 4)), dma((far_side, 2, 4)),
            dma((4,)), dma((4,)),
            dma((far_side, 2, 4)), dma((far_side, 2, 4)),
            dma((n_gx,)), dma((n_gx,)),
            dma((share,)), dma((share,)),
            dma((n_gx,)), dma((n_gx,)),
            pltpu.SMEM((1,), jnp.int32),
            pltpu.SMEM((2,), jnp.int32),
            pltpu.SMEM((2,), jnp.int32),
            pltpu.SMEM((2,), jnp.int32),
        ],
        compiler_params=pltpu.CompilerParams(
            collective_id=0, has_side_effects=True, vmem_limit_bytes=56 * 1024 * 1024
        ),
    )(
        count, dest, start_x, start_y, field, prev_field, diffusivity, velocity,
        w_lift, gain, w_conv, w_out,
    )


def finish_kernel(total, tail, cells, conv_out, lift_out, gain_out, out_out, loss_out, cells_out):
    cells_out[...] = cells[...]
    scale = tail[32:33, :]
    for chunk in range(total.shape[0]):
        size = total.shape[1]
        conv_out[pl.ds(chunk * size, size), :] = total[chunk].astype(f32) * scale
    lift_out[...] = tail[0:27, :]
    gain_out[...] = tail[27:28, :]
    out_out[...] = tail[28:29, :]
    loss_out[...] = tail[33:34, :]


def finish_call(total, tail, cells):
    vmem = pl.BlockSpec(memory_space=pltpu.VMEM)
    tile = functools.partial(jax.ShapeDtypeStruct, dtype=f32)
    return pl.pallas_call(
        finish_kernel,
        out_shape=(
            tile((total.shape[0] * total.shape[1], 128)),
            tile((27, 128)), tile((1, 128)), tile((1, 128)), tile((1, 128)),
            tile(cells.shape),
        ),
        in_specs=[vmem] * 3,
        out_specs=(vmem,) * 6,
        compiler_params=pltpu.CompilerParams(vmem_limit_bytes=56 * 1024 * 1024),
    )(total, tail, cells)


def body(
    field, prev_field, diffusivity, velocity, w_lift, norm_gain, w_conv, w_out,
    tile_count, patch_dest, anchor_x, anchor_y,
):
    entries = w_lift.size + norm_gain.size + w_out.size + lax.axis_size("gx") * w_conv[0].size
    stepped, total, tail = whole_call(
        tile_count.reshape(1), patch_dest.reshape(2), anchor_x.reshape(2), anchor_y.reshape(2),
        field, prev_field, diffusivity, velocity,
        w_lift, norm_gain[None], w_conv[0], w_out[None], entries,
    )
    dir_conv, lift, gain, out, loss, new_field = finish_call(total, tail, stepped)
    return (
        new_field, loss[:, :1].reshape(1, 1, 1), lift, gain.reshape(-1),
        dir_conv.reshape(w_conv.shape), out.reshape(-1),
    )


def solution(mesh):
    tiles = P("ga", "gx", "gy")
    slots = P("ga", "gx", "gy", None)
    in_specs = (
        tiles, tiles, tiles, P(None, "ga", "gx", "gy"), P(), P(), P("gx", None, None), P(),
        tiles, slots, slots, slots,
    )
    out_specs = (tiles, tiles, P(), P(), P("gx", None, None), P())
    return jax.shard_map(body, mesh=mesh, in_specs=in_specs, out_specs=out_specs, check_vma=False)
```

```python
import functools

import jax
import jax.numpy as jnp
from jax import lax
from jax.experimental import pallas as pl
from jax.experimental.pallas import tpu as pltpu
from jax.sharding import PartitionSpec as P

STEPS = 2
PVOX = 1024
CAP = 4
PAIR = 2
BEFORE = 5
ROOT = 0.7978845608028654
CUBE = 0.044715
MESH = pl.DeviceIdType.MESH
f32, bf16 = jnp.float32, jnp.bfloat16


def gelu_both(v):
    v2 = v * v
    t = jnp.tanh(ROOT * (v + CUBE * (v * v2)))
    half = 0.5 * (1.0 + t)
    slope = half + 0.5 * v * (1.0 - t * t) * (ROOT * (1.0 + 3.0 * CUBE * v2))
    return v * half, slope


def z_shifted(block, z_ids):
    up = jnp.where(z_ids == 31, 0.0, pltpu.roll(block, 127, 0))
    down = jnp.where(z_ids == 0, 0.0, pltpu.roll(block, 1, 0))
    return up, down


def move_y(block, by):
    if by == 0:
        return block
    gap = jnp.zeros_like(block[:, :1])
    parts = [block[:, 1:], gap] if by > 0 else [gap, block[:, :-1]]
    return jnp.concatenate(parts, axis=1)


def conv_rows(source, weights, x, sign):
    acc = None
    number = PAIR
    for q in range(3):
        x_in = x + sign * (q - 1)
        if x_in < 0 or x_in > 7:
            continue
        lhs = source[x_in + 1, :, 1:5].reshape(number * 128, 384)
        d = jnp.dot(lhs, weights[q], preferred_element_type=f32).reshape(number, 4, 32, 384)
        for r in range(3):
            piece = move_y(d[:, :, :, r * 128 : (r + 1) * 128], sign * (r - 1))
            acc = piece if acc is None else acc + piece
    return acc.reshape(number, 128, 128)


def lanes_of(shape):
    return lax.broadcasted_iota(jnp.int32, shape, len(shape) - 1)


def group_partners(n_gy, n_ga):
    gy, ga = lax.axis_index("gy"), lax.axis_index("ga")
    for far in range(1, n_gy * n_ga):
        there = (gy + far % n_gy) % n_gy
        across = (ga + far // n_gy) % n_ga
        yield far, {"gy": there, "ga": across}


def line_partners(n_gx):
    gx = lax.axis_index("gx")
    for far in range(1, n_gx):
        yield far, {"gx": (gx + far) % n_gx}


def meet(devices):
    barrier = pltpu.get_barrier_semaphore()
    for device in devices:
        pl.semaphore_signal(barrier, inc=1, device_id=device, device_id_type=MESH)
    return barrier, len(devices)


def several(count, step, carry, at_once=4):
    def run(block, carry):
        for i in range(at_once):
            carry = step(block * at_once + i, carry)
        return carry

    return lax.fori_loop(0, count // at_once, run, carry)


def remote(src, dst, send_sem, recv_sem, device):
    return pltpu.make_async_remote_copy(
        src_ref=src, dst_ref=dst, send_sem=send_sem, recv_sem=recv_sem,
        device_id=device, device_id_type=MESH,
    )


def row_cuts(rows):
    tiles = rows // 16
    ends = [16 * (tiles * i // 4 + (1 if 0 < i < 4 and tiles * i % 4 else 0)) for i in range(5)]
    return [(low, high - low) for low, high in zip(ends, ends[1:])]


def whole_kernel(
    n_gx, n_gy, n_ga, rows, entries,
    count_in, dest_in, start_x_in, start_y_in, field, prev_field, diffusivity, velocity,
    w_lift, gain, w_conv, w_out,
    new_field, total_out, tail_out, *scratch,
):
    (
        state, later, prev, diff, speed, weights,
        mine, line, z_in, x_out, x_in, y_out, y_in, records,
        wf, wb, lift_rows, vp, gp, nt, nu, lifted, slope1, pre2, dh,
        conv, small, leaf_out, leaf_in, ring, own, other, gathered,
        pieces, from_line_sums, tile_b, from_group, tile_c, from_all,
        load_sem, line_send, line_recv, halo_send, halo_recv,
        ring_send, ring_recv, pair_send, pair_recv, gather_send, gather_recv,
        a_send, a_recv, b_send, b_recv, c_send, c_recv,
        count, dest, start_x, start_y,
    ) = scratch
    gx, gy, ga = lax.axis_index("gx"), lax.axis_index("gy"), lax.axis_index("ga")
    line_id = ga * n_gy + gy
    size_z, size_x, size_y = prev.shape
    loads = [
        pltpu.make_async_copy(field, state.at[pl.ds(1, size_z)], load_sem.at[0]),
        pltpu.make_async_copy(prev_field, prev, load_sem.at[1]),
        pltpu.make_async_copy(diffusivity, diff, load_sem.at[2]),
        pltpu.make_async_copy(velocity, speed, load_sem.at[3]),
        pltpu.make_async_copy(w_conv, weights, load_sem.at[4]),
    ]
    loads += [
        pltpu.make_async_copy(source, held, load_sem.at[5 + i])
        for i, (source, held) in enumerate(
            ((count_in, count), (dest_in, dest), (start_x_in, start_x), (start_y_in, start_y))
        )
    ]
    for load in loads:
        load.start()
    barrier, expected = meet(
        [device for _, device in line_partners(n_gx)]
        + [device for _, device in group_partners(n_gy, n_ga)]
    )
    sub8 = lax.broadcasted_iota(jnp.int32, (8, 128), 0)
    lane8 = lanes_of((8, 128))
    xi = lax.broadcasted_iota(jnp.int32, (size_x, 128), 0)
    li = lanes_of((size_x, 128))
    row_y = lax.broadcasted_iota(jnp.int32, (128, 128), 0)
    col = lanes_of((128, 128))
    z_mask = (
        lax.broadcasted_iota(jnp.int32, (size_z, 8, 128), 0) == lanes_of((size_z, 8, 128)) % size_z
    )
    zero_tile = jnp.zeros((size_x, 128), f32)

    def pack_faces(step, cells, high, low):
        x_out[step, 0] = cells[1 : size_z + 1, 0, :]
        x_out[step, 1] = cells[1 : size_z + 1, size_x - 1, :]
        y_out[step, 0] = low
        y_out[step, 1] = high

    def halo_copies(step, cells):
        base = step * 5
        z_src = cells.at[size_z - (size_z - 1) * ga]
        there = {"ga": 1 - ga}
        z_out_copy = remote(
            z_src, z_in.at[step], halo_send.at[base], halo_recv.at[base], there
        )
        copies = [z_out_copy]
        for side in range(2):
            near = (gx + (n_gx - 1 if side == 0 else 1)) % n_gx
            copies.append(remote(
                x_out.at[step, side], x_in.at[step, 1 - side],
                halo_send.at[base + 1 + side], halo_recv.at[base + 1 + side], {"gx": near},
            ))
        for side in range(2):
            near = (gy + (n_gy - 1 if side == 0 else 1)) % n_gy
            copies.append(remote(
                y_out.at[step, side], y_in.at[step, 1 - side],
                halo_send.at[base + 3 + side], halo_recv.at[base + 3 + side], {"gy": near},
            ))
        return copies

    def place(z, cells, high, low):
        high = jnp.where(li == z, pltpu.roll(cells, z + 1, 1), high)
        low = jnp.where(li == z, pltpu.roll(cells, z, 1), low)
        return high, low

    def advance(step, cells, store, pack):
        z_face = z_in[step]
        cells[0] = jnp.where(ga == 1, z_face, 0.0)
        cells[size_z + 1] = jnp.where(ga == 0, z_face, 0.0)

        def layer(z, faces):
            centre = cells[z + 1]
            below = cells[z]
            above = cells[z + 2]
            behind = jnp.where(xi == 0, x_in[step, 0, pl.ds(z, 1), :], pltpu.roll(centre, 1, 0))
            ahead = jnp.where(
                xi == size_x - 1, x_in[step, 1, pl.ds(z, 1), :], pltpu.roll(centre, size_x - 1, 0)
            )
            left = jnp.where(
                li == 0, pltpu.roll(y_in[step, 0], 128 - z, 1), pltpu.roll(centre, 1, 1)
            )
            right = jnp.where(
                li == 127, pltpu.roll(y_in[step, 1], 127 - z, 1), pltpu.roll(centre, 127, 1)
            )
            laplace = above + below + (ahead + behind) + (right + left) - 6.0 * centre
            moved = jnp.zeros_like(centre)
            for d, (low, high) in enumerate(((below, above), (behind, ahead), (left, right))):
                v = speed[d, z]
                moved = moved + (
                    jnp.maximum(v, 0.0) * (centre - low) + jnp.minimum(v, 0.0) * (high - centre)
                )
            result = centre + diff[z] * laplace - moved
            store(z, result)
            return place(z, result, *faces) if pack else faces

        if not pack:
            return layer
        return several(size_z, layer, (zero_tile, zero_tile))

    loads[0].wait()
    loads[1].wait()
    for load in loads[5:]:
        load.wait()
    for k in range(2):
        chosen = (row_y == start_y[k] + col // size_z).astype(bf16)
        parts = []
        for source in (0, 1):
            if source == 0:
                window = prev[:, pl.ds(start_x[k], 8), :]
            else:
                window = state[1 : size_z + 1, pl.ds(start_x[k], 8), :]
            spread = jnp.dot(
                window.reshape(size_z * 8, 128).astype(bf16), chosen, preferred_element_type=f32
            ).reshape(size_z, 8, 128)
            parts.append(jnp.sum(jnp.where(z_mask, spread, 0.0), axis=0))
        mine[pl.ds(16 * k, 16), :] = jnp.concatenate(parts, axis=0).astype(bf16)
    goals = [jnp.where(k < count[0], dest[k], -1).astype(f32) for k in range(2)]
    mine[32:48, :] = jnp.concatenate(
        [jnp.full((8, 128), goals[0]), jnp.full((8, 128), goals[1])], axis=0
    ).astype(bf16)
    line[gx] = mine[...]

    pl.semaphore_wait(barrier, expected)
    first = []
    for far, device in line_partners(n_gx):
        copy = remote(mine, line.at[gx], line_send.at[far], line_recv.at[far], device)
        copy.start()
        first.append(copy)
    high, low = several(
        size_z, lambda z, faces: place(z, state[z + 1], *faces), (zero_tile, zero_tile)
    )
    pack_faces(0, state, high, low)
    halos = halo_copies(0, state)
    for copy in halos:
        copy.start()

    for held in (nu, conv, small, lift_rows):
        held[...] = jnp.zeros_like(held)
    for edge in (0, 5):
        gp[:, :, :, edge] = jnp.zeros_like(gp[:, :, :, edge])
    for edge in (0, 9):
        nt[:, edge] = jnp.zeros_like(nt[:, edge])
    lift_rows[0:27, :] = w_lift[...].astype(f32)
    lift_weights = lift_rows[...].astype(bf16)
    gain_row = gain[...]
    wo_row = w_out[...].astype(f32)

    loads[4].wait()
    for q in range(3):
        for r in range(3):
            for p in range(3):
                blk = weights[pl.ds(((p * 3 + q) * 3 + r) * 128, 128), :]
                wf[q, pl.ds(p * 128, 128), pl.ds(r * 128, 128)] = blk
                wb[q, pl.ds(p * 128, 128), pl.ds(r * 128, 128)] = blk.astype(f32).T.astype(bf16)

    loads[2].wait()
    loads[3].wait()
    for copy in halos:
        copy.wait_recv()

    def keep(z, value):
        later[z + 1] = value

    high, low = advance(0, state, keep, True)
    pack_faces(1, later, high, low)
    more = halo_copies(1, later)
    for copy in more:
        copy.start()

    for copy in first:
        copy.wait_recv()
    empty = jnp.zeros((16, 128), f32)
    myself = gx.astype(f32)

    def from_line(source, carry):
        rank, picked = carry
        for k in range(2):
            goal = line[source, 32:48, :].astype(f32)[8 * k : 8 * k + 8]
            record = line[source, pl.ds(16 * k, 16), :].astype(f32)
            hit = goal == myself
            picked = tuple(
                jnp.where(jnp.concatenate([hit & (rank == c)] * 2, axis=0), record, old)
                for c, old in enumerate(picked)
            )
            rank = rank + hit.astype(f32)
        return rank, picked

    rank, picked = lax.fori_loop(
        0, n_gx, from_line, (jnp.zeros((8, 128), f32), (empty,) * CAP)
    )
    for c in range(CAP):
        records[pl.ds(16 * c, 16), :] = picked[c]

    z_ids = lax.broadcasted_iota(jnp.int32, (128, 128), 0) % 32

    def first_part(i):
        for slot in range(PAIR):
            u = records[pl.ds(16 * (PAIR * i + slot), 8), :]
            for p in range(3):
                dz = p - 1
                uz = u if dz == 0 else pltpu.roll(u, (-dz) % 128, 1)
                okz = (lane8 % 32 + dz >= 0) & (lane8 % 32 + dz < 32)
                for q in range(3):
                    dx = q - 1
                    ux = uz if dx == 0 else pltpu.roll(uz, (-dx) % 8, 0)
                    okx = (sub8 + dx >= 0) & (sub8 + dx < 8)
                    for r in range(3):
                        dy = r - 1
                        uy = ux if dy == 0 else pltpu.roll(ux, (-32 * dy) % 128, 1)
                        oky = (lane8 // 32 + dy >= 0) & (lane8 // 32 + dy < 4)
                        nu[i, slot, :, p * 9 + q * 3 + r, :] = jnp.where(okz & okx & oky, uy, 0.0)
            for x in range(8):
                pre = lax.dot_general(
                    nu[i, slot, x].astype(bf16), lift_weights, (((0,), (0,)), ((), ())), preferred_element_type=f32
                )
                val, slope = gelu_both(pre)
                slope1[i, slot, x] = slope
                low = val.astype(bf16)
                lifted[i, slot, x] = low
                wide = low.astype(f32)
                inv = lax.rsqrt(jnp.mean(wide * wide, axis=1, keepdims=True) + 1e-06)
                normed = (wide * inv * gain_row).astype(bf16).astype(f32)
                up, down = z_shifted(normed, z_ids)
                for k, v in enumerate((down, normed, up)):
                    vp[x + 1, slot, 1:5, :, k * 128 : (k + 1) * 128] = v.astype(bf16).reshape(4, 32, 128)
                nt[slot, x + 1] = normed.T.astype(bf16)
        for x in range(8):
            pre2[x] = conv_rows(vp, wf, x, 1)
        for slot in range(PAIR):
            target = records[pl.ds(16 * (PAIR * i + slot) + 8, 8), :]
            loss = dwo = jnp.zeros((1, 128), f32)
            for x in range(8):
                mixed, slope = gelu_both(pre2[x, slot])
                hid = (lifted[i, slot, x].astype(f32) + mixed).astype(bf16).astype(f32)
                pred = jnp.sum(hid * wo_row, axis=1, keepdims=True)
                row = jnp.sum(jnp.where(sub8 == x, target, 0.0), axis=0, keepdims=True)
                wanted = jnp.broadcast_to(row, (128, 128)).T
                misfit = pred - wanted
                loss = loss + jnp.sum(misfit * misfit, axis=0, keepdims=True)
                dwo = dwo + jnp.sum(hid * misfit, axis=0, keepdims=True)
                d_hid = (misfit * wo_row).astype(bf16)
                dh[i, slot, x] = d_hid
                g = (d_hid.astype(f32) * slope).astype(bf16).astype(f32)
                up, down = z_shifted(g, z_ids)
                for k, v in enumerate((up, g, down)):
                    gp[i, x + 1, slot, 1:5, :, k * 128 : (k + 1) * 128] = v.astype(bf16).reshape(4, 32, 128)
            lhs = jnp.concatenate(
                [jnp.concatenate([nt[slot, q + x] for x in range(8)], axis=1) for q in range(3)], axis=0
            )
            for r in range(3):
                rhs = gp[i, 1:9, slot, 2 - r : 6 - r].reshape(1024, 384)
                d = jnp.dot(lhs, rhs, preferred_element_type=f32)
                for q in range(3):
                    for p in range(3):
                        rows = pl.ds(((p * 3 + q) * 3 + r) * 128, 128)
                        piece = d[q * 128 : (q + 1) * 128, p * 128 : (p + 1) * 128]
                        conv[rows, :] += piece.astype(bf16).astype(f32)
            small[28:29, :] += dwo.astype(bf16).astype(f32)
            small[32:33, :] += 0.5 * loss

    def one_pair(i, carry):
        first_part(i)
        return carry

    lax.fori_loop(0, CAP // PAIR, one_pair, 0)

    subs = row_cuts(rows)
    far_side = n_gy // 2
    signs = (1, -1)
    keys = [(0, 0), (1, 2), (0, 1), (1, 3), (0, 2), (1, 0), (0, 3), (1, 1)]
    depth = {(side, part): far_side if part // 2 == side else n_gy - 1 - far_side for side, part in keys}
    share = n_gy * n_ga
    per = 32 // n_gx

    def wrap(index):
        return (index + 2 * n_gy) % n_gy

    def rows_of(index, part):
        low, size = subs[part]
        return pl.ds(pl.multiple_of(wrap(index) * rows + low, 8), size)

    def next_to(side):
        return {"gy": wrap(gy + signs[side])}

    def ring_copy(step, side, part):
        low, size = subs[part]
        if step == 0:
            return remote(
                leaf_out.at[side, pl.ds(low, size)], leaf_in.at[side, pl.ds(low, size)],
                ring_send.at[0, side, part], ring_recv.at[0, side, part], next_to(side),
            )
        return remote(
            ring.at[step - 1, side, pl.ds(low, size)], ring.at[step, side, pl.ds(low, size)],
            ring_send.at[step, side, part], ring_recv.at[step, side, part], next_to(side),
        )

    for side, part in keys:
        low, size = subs[part]
        leaf = rows_of(gy + signs[side] * depth[side, part], part)
        leaf_out[side, pl.ds(low, size), :] = conv[leaf, :].astype(bf16)
    started = []

    def begin(copy):
        copy.start()
        started.append(copy)
        return copy

    line_copies = []
    leave = [pltpu.make_async_copy(prev, new_field, load_sem.at[0])]

    def emit(z, value):
        prev[z] = value

    def backward_steps():
        dgain = jnp.zeros((1, 128), f32)
        for pair in range(CAP // PAIR):
            dwl = [jnp.zeros((32, 128), f32)] * PAIR
            for x in range(8):
                both = conv_rows(gp.at[pair], wb, x, -1)
                for slot in range(PAIR):
                    dn = both[slot].astype(bf16).astype(f32)
                    wide = lifted[pair, slot, x].astype(f32)
                    inv = lax.rsqrt(jnp.mean(wide * wide, axis=1, keepdims=True) + 1e-06)
                    dgain = dgain + jnp.sum(dn * (wide * inv), axis=0, keepdims=True)
                    dt = dn * gain_row
                    mean = jnp.sum(dt * wide, axis=1, keepdims=True) * (1.0 / 128.0)
                    d_low = dh[pair, slot, x].astype(f32) + dt * inv - (inv * inv * inv * mean) * wide
                    d_pre = d_low.astype(bf16).astype(f32) * slope1[pair, slot, x]
                    dwl[slot] = dwl[slot] + jnp.dot(
                        nu[pair, slot, x].astype(bf16), d_pre.astype(bf16), preferred_element_type=f32
                    )
                yield
            for part in dwl:
                small[0:32, :] += part.astype(bf16).astype(f32)
        small[27:28, :] += dgain
        for k in range(n_gx):
            pieces[k] = jnp.concatenate(
                [small[per * k : per * k + per, :], jnp.zeros((8 - per, 128), f32)], axis=0
            )
        from_line_sums[gx] = pieces[gx]

        line_copies.extend(
            begin(remote(
                pieces.at[device["gx"]], from_line_sums.at[gx], a_send.at[far], a_recv.at[far], device
            ))
            for far, device in line_partners(n_gx)
        )
        yield
        for copy in more:
            copy.wait_recv()
        layer = advance(1, later, emit, False)
        for z in range(size_z):
            layer(z, None)
            if z % 4 == 3:
                yield
        leave[0].start()

    flying = {key: begin(ring_copy(0, *key)) for key in keys}
    backward = backward_steps()
    for _ in range(BEFORE):
        next(backward)

    pairs = {}
    for step in range(far_side):
        for key in keys:
            side, part = key
            low, size = subs[part]
            if step >= depth[key]:
                continue
            flying[key].wait_recv()
            if step + 1 < depth[key]:
                there = rows_of(gy + signs[side] * (depth[key] - 1 - step), part)
                here = pl.ds(low, size)
                came = leaf_in[side, here, :].astype(f32) if step == 0 else ring[step, side, here, :]
                ring[step, side, here, :] = came + conv[there, :]
                flying[key] = begin(ring_copy(step + 1, *key))
            elif step == far_side - 1:
                here = pl.ds(low, size)
                near = depth[1 - side, part] - 1
                own[here, :] = (
                    ring[step, side, here, :] + ring[near, 1 - side, here, :]
                ) + conv[rows_of(gy, part), :]
                pairs[part] = begin(remote(
                    own.at[here], other.at[here], pair_send.at[part], pair_recv.at[part],
                    {"ga": 1 - ga},
                ))
            next(backward, None)
    for _ in backward:
        pass

    for copy in line_copies:
        copy.wait_recv()
    piece = lax.fori_loop(0, n_gx, lambda k, acc: acc + from_line_sums[k], jnp.zeros((8, 128), f32))

    def gather_copy(step, side, part):
        low, size = subs[part]
        where = gathered.at[wrap(gy - signs[side] * step), pl.ds(low, size)]
        return remote(
            where, where,
            gather_send.at[step, side, part], gather_recv.at[step, side, part], next_to(side),
        )

    squares = jnp.zeros((1, 128), f32)
    for part in (0, 2, 1, 3):
        low, size = subs[part]
        here = pl.ds(low, size)
        pairs[part].wait_recv()
        total = own[here, :] + other[here, :]
        gathered[gy, here, :] = total.astype(bf16)
        for side in (part // 2, 1 - part // 2):
            flying[side, part] = begin(gather_copy(0, side, part))
        squares = squares + jnp.sum(total * total, axis=0, keepdims=True)
    squares = jnp.where(ga == 0, squares, 0.0)
    tile_b[...] = jnp.where(sub8 < per, piece, jnp.where(sub8 == per, squares, 0.0))
    from_group[line_id] = tile_b[...]
    group_copies = [
        begin(remote(tile_b, from_group.at[line_id], b_send.at[far], b_recv.at[far], device))
        for far, device in group_partners(n_gy, n_ga)
    ]

    for step in range(far_side):
        for key in keys:
            if step >= depth[key]:
                continue
            flying[key].wait_recv()
            if step + 1 < depth[key]:
                flying[key] = begin(gather_copy(step + 1, *key))
        if step == 1:
            for copy in group_copies:
                copy.wait_recv()
            summed = lax.fori_loop(
                0, share, lambda k, acc: acc + from_group[k], jnp.zeros((8, 128), f32)
            )
            tile_c[...] = summed
            from_all[gx] = summed
            last_copies = [
                begin(remote(tile_c, from_all.at[gx], c_send.at[far], c_recv.at[far], device))
                for far, device in line_partners(n_gx)
            ]

    leave.append(pltpu.make_async_copy(gathered, total_out, load_sem.at[1]))
    leave[1].start()
    for copy in last_copies:
        copy.wait_recv()
    shared = jnp.concatenate([from_all[k, 0:per, :] for k in range(n_gx)], axis=0)
    conv_squares = lax.fori_loop(
        0, n_gx, lambda k, acc: acc + from_all[k], jnp.zeros((8, 128), f32)
    )[per : per + 1]
    all_squares = jnp.sum(
        conv_squares + jnp.sum(shared * shared, axis=0, keepdims=True), axis=1, keepdims=True
    )
    scale = lax.rsqrt(all_squares / entries + 1e-06)
    tail_out[0:32, :] = shared * scale
    loss = small[32:33, :] / (PVOX * jnp.maximum(rank[0:1], 1.0))
    tail_out[32:40, :] = jnp.where(sub8 == 0, jnp.broadcast_to(scale, (8, 128)), loss)
    for copy in leave:
        copy.wait()
    for copy in started + first + halos + more:
        copy.wait_send()


def whole_call(
    count, dest, start_x, start_y, field, prev_field, diffusivity, velocity,
    w_lift, gain, w_conv, w_out, entries,
):
    n_gx, n_gy, n_ga = (lax.axis_size(name) for name in ("gx", "gy", "ga"))
    size_z, size_x, size_y = field.shape
    share = n_gy * n_ga
    rows = w_conv.shape[0] // n_gy
    far_side = n_gy // 2
    vmem = pl.BlockSpec(memory_space=pltpu.VMEM)
    hbm = pl.BlockSpec(memory_space=pl.ANY)
    dma = pltpu.SemaphoreType.DMA
    held = pltpu.VMEM
    return pl.pallas_call(
        functools.partial(whole_kernel, n_gx, n_gy, n_ga, rows, entries),
        out_shape=(
            jax.ShapeDtypeStruct(field.shape, f32),
            jax.ShapeDtypeStruct((n_gy, rows, 128), bf16),
            jax.ShapeDtypeStruct((40, 128), f32),
        ),
        in_specs=[hbm] * 8 + [vmem, vmem, hbm, vmem],
        out_specs=(hbm, hbm, vmem),
        scratch_shapes=[
            held((size_z + 2, size_x, size_y), f32),
            held((size_z + 2, size_x, size_y), f32),
            held((size_z, size_x, size_y), f32),
            held((size_z, size_x, size_y), f32),
            held((3, size_z, size_x, size_y), f32),
            held(w_conv.shape, bf16),
            held((48, 128), bf16),
            held((n_gx, 48, 128), bf16),
            held((STEPS, size_x, 128), f32),
            held((STEPS, 2, size_z, 128), f32),
            held((STEPS, 2, size_z, 128), f32),
            held((STEPS, 2, size_x, 128), f32),
            held((STEPS, 2, size_x, 128), f32),
            held((16 * CAP, 128), f32),
            held((3, 384, 384), bf16),
            held((3, 384, 384), bf16),
            held((32, 128), f32),
            held((10, PAIR, 6, 32, 384), bf16),
            held((CAP // PAIR, 10, PAIR, 6, 32, 384), bf16),
            held((PAIR, 10, 128, 128), bf16),
            held((CAP // PAIR, PAIR, 8, 32, 128), f32),
            held((CAP // PAIR, PAIR, 8, 128, 128), bf16),
            held((CAP // PAIR, PAIR, 8, 128, 128), f32),
            held((8, PAIR, 128, 128), f32),
            held((CAP // PAIR, PAIR, 8, 128, 128), bf16),
            held(w_conv.shape, f32),
            held((40, 128), f32),
            held((2, rows, 128), bf16),
            held((2, rows, 128), bf16),
            held((far_side, 2, rows, 128), f32),
            held((rows, 128), f32),
            held((rows, 128), f32),
            held((n_gy, rows, 128), bf16),
            held((n_gx, 8, 128), f32),
            held((n_gx, 8, 128), f32),
            held((8, 128), f32),
            held((share, 8, 128), f32),
            held((8, 128), f32),
            held((n_gx, 8, 128), f32),
            dma((9,)),
            dma((n_gx,)), dma((n_gx,)),
            dma((STEPS * 5,)), dma((STEPS * 5,)),
            dma((far_side, 2, 4)), dma((far_side, 2, 4)),
            dma((4,)), dma((4,)),
            dma((far_side, 2, 4)), dma((far_side, 2, 4)),
            dma((n_gx,)), dma((n_gx,)),
            dma((share,)), dma((share,)),
            dma((n_gx,)), dma((n_gx,)),
            pltpu.SMEM((1,), jnp.int32),
            pltpu.SMEM((2,), jnp.int32),
            pltpu.SMEM((2,), jnp.int32),
            pltpu.SMEM((2,), jnp.int32),
        ],
        compiler_params=pltpu.CompilerParams(
            collective_id=0, has_side_effects=True, vmem_limit_bytes=56 * 1024 * 1024
        ),
    )(
        count, dest, start_x, start_y, field, prev_field, diffusivity, velocity,
        w_lift, gain, w_conv, w_out,
    )


def finish_kernel(total, tail, cells, conv_out, lift_out, gain_out, out_out, loss_out, cells_out):
    cells_out[...] = cells[...]
    scale = tail[32:33, :]
    for chunk in range(total.shape[0]):
        size = total.shape[1]
        conv_out[pl.ds(chunk * size, size), :] = total[chunk].astype(f32) * scale
    lift_out[...] = tail[0:27, :]
    gain_out[...] = tail[27:28, :]
    out_out[...] = tail[28:29, :]
    loss_out[...] = tail[33:34, :]


def finish_call(total, tail, cells):
    vmem = pl.BlockSpec(memory_space=pltpu.VMEM)
    tile = functools.partial(jax.ShapeDtypeStruct, dtype=f32)
    return pl.pallas_call(
        finish_kernel,
        out_shape=(
            tile((total.shape[0] * total.shape[1], 128)),
            tile((27, 128)), tile((1, 128)), tile((1, 128)), tile((1, 128)),
            tile(cells.shape),
        ),
        in_specs=[vmem] * 3,
        out_specs=(vmem,) * 6,
        compiler_params=pltpu.CompilerParams(vmem_limit_bytes=56 * 1024 * 1024),
    )(total, tail, cells)


def body(
    field, prev_field, diffusivity, velocity, w_lift, norm_gain, w_conv, w_out,
    tile_count, patch_dest, anchor_x, anchor_y,
):
    entries = w_lift.size + norm_gain.size + w_out.size + lax.axis_size("gx") * w_conv[0].size
    stepped, total, tail = whole_call(
        tile_count.reshape(1), patch_dest.reshape(2), anchor_x.reshape(2), anchor_y.reshape(2),
        field, prev_field, diffusivity, velocity,
        w_lift, norm_gain[None], w_conv[0], w_out[None], entries,
    )
    dir_conv, lift, gain, out, loss, new_field = finish_call(total, tail, stepped)
    return (
        new_field, loss[:, :1].reshape(1, 1, 1), lift, gain.reshape(-1),
        dir_conv.reshape(w_conv.shape), out.reshape(-1),
    )


def solution(mesh):
    tiles = P("ga", "gx", "gy")
    slots = P("ga", "gx", "gy", None)
    in_specs = (
        tiles, tiles, tiles, P(None, "ga", "gx", "gy"), P(), P(), P("gx", None, None), P(),
        tiles, slots, slots, slots,
    )
    out_specs = (tiles, tiles, P(), P(), P("gx", None, None), P())
    return jax.shard_map(body, mesh=mesh, in_specs=in_specs, out_specs=out_specs, check_vma=False)
```
